256 devices in a mesh: tm: 32 (over y, z), chan: 8 (over x, core).
Axes of the slice: x: 4, y: 4, z: 8, core: 2. Of those that a mesh axis runs over, the one named last changes fastest.
Arguments:
- observations: bfloat16 [8192, 8192], P('tm', 'chan'), may hold values from -6 to 6
- emission: bfloat16 [8192, 256], P('chan'), may hold values from -0.0625 to 0.0625
- noise_precision: float32 [8192], P('chan'), may hold values from 0.3 to 3
- transition: float32 [256, 256], replicated, may hold values from -1 to 1
- info_gain: float32 [256, 256], replicated, may hold values from -2 to 2
- smoother_gain: float32 [256, 256], replicated, may hold values from -1 to 1
- smoother_input: float32 [256, 256], replicated, may hold values from -0.1 to 0.1
Outputs:
- smoothed: float32 [8192, 256], P('tm')
- cross_stat: float32 [8192, 256], P('chan')
- noise_var: float32 [8192], P('chan')
- state_moment: float32 [256, 256], replicated
The draws below stay inside these ranges and needn't reach their ends.
All inputs are finite; a program needn't handle non-finite values.
Results may differ from the reference program's by a relative error of at most 0.0039.
Values sent between devices are 32-bit elements; how exact they have to be, the bound alone decides.
No kernel may reach another device: no remote copies, remote signals or barrier semaphores. Data moves between devices by JAX's collectives and lax.ppermute only.
A program may use at most 256 MiB of HBM per device.

```python
import math
import jax
import jax.numpy as jnp
from jax import lax

S = 256
P_SIZE = 8192
BIN_DEV = 256
TIME = 8192
N_TM = 32


FULL_PRECISION = lax.Precision.HIGHEST


def decay_times(key, slow_share):
    pair_count = S // 2
    pick_key, fast_key, slow_key = jax.random.split(key, 3)
    is_slow = jax.random.randint(pick_key, (pair_count,), 0, 100) < slow_share
    fast_times = jnp.exp(jax.random.uniform(fast_key, (pair_count,), jnp.float32, math.log(30.0), math.log(50.0)))
    lengthy = jnp.exp(jax.random.uniform(slow_key, (pair_count,), jnp.float32, math.log(0.5 * TIME), math.log(4.0 * TIME)))
    return jnp.where(is_slow, lengthy, fast_times)


def orthogonal(key, salt):
    base_key = jax.random.fold_in(key, salt)
    perm_key, sign_key, vector_key = jax.random.split(base_key, 3)
    row_index = jnp.arange(S, dtype=jnp.float32)[:, None]
    col_index = jnp.arange(S, dtype=jnp.float32)[None, :]
    cosine_table = jnp.cos(math.pi * (col_index + 0.5) * row_index / S) * math.sqrt(2.0 / S)
    row_scale = jnp.where(jnp.arange(S) == 0, math.sqrt(0.5), 1.0).astype(jnp.float32)
    cosine_table = cosine_table * row_scale[:, None]
    order = jax.random.permutation(perm_key, S)
    shuffled = cosine_table[order]
    signs = (2 * jax.random.randint(sign_key, (S,), 0, 2) - 1).astype(jnp.float32)
    shuffled = shuffled * signs[None, :]
    vector = jax.random.normal(vector_key, (S,), jnp.float32)
    length_sq = jnp.sum(vector * vector)
    image = jnp.sum(shuffled * vector[None, :], axis=1)
    reflected = shuffled - 2.0 / length_sq * image[:, None] * vector[None, :]
    return reflected.astype(jnp.float32)


def conjugate(left, middle, right):
    inner = jnp.dot(left, middle, precision=FULL_PRECISION, preferred_element_type=jnp.float32)
    return jnp.dot(inner, right.T, precision=FULL_PRECISION, preferred_element_type=jnp.float32)


def rotations(key, times):
    angles = jax.random.uniform(key, (S // 2,), jnp.float32, 0.25, 0.8)
    radius = jnp.exp(-1.0 / times)
    row_index = jnp.arange(S)[:, None]
    col_index = jnp.arange(S)[None, :]
    cosine = jnp.repeat(radius * jnp.cos(angles), 2)[:, None]
    sine_part = jnp.repeat(radius * jnp.sin(angles), 2)[:, None]
    same_pair = row_index // 2 == col_index // 2
    entries = jnp.where(row_index == col_index, cosine, jnp.where(row_index % 2 == 0, -sine_part, sine_part))
    return jnp.where(same_pair, entries, 0.0).astype(jnp.float32)


def mixing(key, row_scale, spread):
    off_diag = jnp.clip(jax.random.normal(key, (S, S), jnp.float32), -4.0, 4.0) * (0.3 / math.sqrt(S))
    off_flat = jax.random.uniform(jax.random.fold_in(key, 1), (S, S), jnp.float32, -1.0, 1.0) * (0.52 / math.sqrt(S))
    off_part = spread * off_flat + (1.0 - spread) * off_diag
    matrix = jnp.eye(S, dtype=jnp.float32) + off_part * (1.0 - jnp.eye(S, dtype=jnp.float32))
    return (jnp.repeat(row_scale, 2)[:, None] * matrix).astype(jnp.float32)


def draw_transition(key, part):
    basis = orthogonal(key, 31)
    times = decay_times(key, 50)
    key = jax.random.fold_in(key, 11)
    return conjugate(basis, rotations(key, times), basis).astype(jnp.float32)


def draw_info_gain(key, part):
    basis = orthogonal(key, 31)
    times = decay_times(key, 50)
    spread = 0.0
    key = jax.random.fold_in(key, 12)
    radius = jnp.exp(-1.0 / times)
    mixed = mixing(key, jnp.sqrt(1.0 - radius * radius), spread)
    gained = jnp.dot(basis, mixed, precision=FULL_PRECISION, preferred_element_type=jnp.float32)
    return jnp.clip(gained, -2.0, 2.0).astype(jnp.float32)


def draw_smoother_gain(key, part):
    second_basis = orthogonal(key, 32)
    times = decay_times(jax.random.fold_in(key, 21), 50)
    key = jax.random.fold_in(key, 13)
    return conjugate(second_basis, rotations(key, times), second_basis).astype(jnp.float32)


def draw_smoother_input(key, part):
    basis = orthogonal(key, 31)
    second_basis = orthogonal(key, 32)
    times = decay_times(jax.random.fold_in(key, 21), 50)
    spread = 0.0
    key = jax.random.fold_in(key, 14)
    radius = jnp.exp(-1.0 / times)
    mixed = mixing(key, 1.0 - radius, spread)
    return jnp.clip(conjugate(second_basis, mixed, basis), -0.1, 0.1).astype(jnp.float32)


def level_of(rng, extent, shards, least, top_value):
    factor_of, own = 1.0, jax.random.fold_in(rng, 6)
    for dim, shards_of in shards:
        steps = jnp.exp(jax.random.uniform(jax.random.fold_in(own, dim), (shards_of,), jnp.float32, least / len(shards), top_value / len(shards)))
        factor_of = factor_of * jnp.repeat(steps, extent[dim] // shards_of).reshape([-1 if axis == dim else 1 for axis in range(len(extent))])
    return factor_of


def centred(own_key, extent, scale, most, cuts=(), kind=jnp.bfloat16):
    factor_of = level_of(own_key, extent, cuts, -0.22, 0.18) if cuts else 1.0
    values = jax.random.normal(own_key, extent, jnp.float32) * scale * factor_of
    return jnp.minimum(jnp.maximum(values, -most), most).astype(kind)


def setup_inputs(seed: int = 0) -> dict:
    arg_keys = jax.random.split(jax.random.key(seed), 8)
    return {
        "observations": centred(arg_keys[0], (TIME, P_SIZE), 1.0, 6.0, ((0, 32), (1, 8))),
        "emission": centred(arg_keys[1], (P_SIZE, S), P_SIZE ** -0.5, 0.0625, ((0, 8),)),
        "noise_precision": jnp.clip(jnp.exp(math.log(3.0) - 2.3025851 * jax.random.uniform(arg_keys[2], (P_SIZE,), jnp.float32) ** level_of(arg_keys[2], (P_SIZE,), ((0, 8),), -0.2, 0.2)), 0.3, 3.0),
        "transition": draw_transition(jax.random.fold_in(arg_keys[7], 71), 0),
        "info_gain": draw_info_gain(jax.random.fold_in(arg_keys[7], 71), 0),
        "smoother_gain": draw_smoother_gain(jax.random.fold_in(arg_keys[7], 71), 0),
        "smoother_input": draw_smoother_input(jax.random.fold_in(arg_keys[7], 71), 0),
    }


FULL_PRECISION = lax.Precision.HIGHEST

def reference(observations, emission, noise_precision, transition, info_gain, smoother_gain, smoother_input):
    weighted = (emission.astype(jnp.float32) * noise_precision[:, None]).astype(jnp.bfloat16)
    information = jnp.dot(observations, weighted, preferred_element_type=jnp.float32)
    drive_rows = jnp.dot(information, info_gain.T, precision=FULL_PRECISION, preferred_element_type=jnp.float32)

    def forward_step(state_now, drive_row):
        state_next = jnp.dot(transition, state_now, precision=FULL_PRECISION) + drive_row
        return (state_next, state_next)
    _, filtered = lax.scan(forward_step, jnp.zeros((S,), jnp.float32), drive_rows)
    inputs = jnp.dot(filtered, smoother_input.T, precision=FULL_PRECISION, preferred_element_type=jnp.float32)
    inputs = inputs.at[TIME - 1].set(filtered[TIME - 1])

    def backward_step(state_now, input_row):
        state_next = jnp.dot(smoother_gain, state_now, precision=FULL_PRECISION) + input_row
        return (state_next, state_next)
    _, smoothed = lax.scan(backward_step, jnp.zeros((S,), jnp.float32), inputs, reverse=True)
    states_bf = smoothed.astype(jnp.bfloat16)
    cross_stat = jnp.dot(observations.T, states_bf, preferred_element_type=jnp.float32) / math.sqrt(TIME)

    def block_error(pieces):
        block_obs, block_states = pieces
        predicted = jnp.dot(block_states, emission.T, preferred_element_type=jnp.float32)
        error_rows = block_obs.astype(jnp.float32) - predicted
        return lax.optimization_barrier(jnp.sum(error_rows * error_rows, axis=0))
    error_blocks = lax.map(block_error, (observations.reshape(N_TM, BIN_DEV, P_SIZE), states_bf.reshape(N_TM, BIN_DEV, S)))
    noise_var = lax.optimization_barrier(jnp.sum(error_blocks, axis=0)) / TIME
    state_moment = jnp.dot(smoothed.T, smoothed, precision=FULL_PRECISION, preferred_element_type=jnp.float32) / TIME
    return (smoothed, cross_stat, noise_var, state_moment)
```

```python
import math

import jax
import jax.numpy as jnp
from jax import lax
from jax.sharding import Mesh, PartitionSpec as P

FULL_PRECISION = lax.Precision.HIGHEST
N_Y, N_Z, N_X, N_CORE = 4, 8, 4, 2


def product(left, right):
    return jnp.dot(left, right, precision=FULL_PRECISION, preferred_element_type=jnp.float32)


def shift(value, axis, count, by):
    return lax.ppermute(value, axis, [(i, (i + by) % count) for i in range(count)])


def chan_sum(rows):
    half = rows.shape[0] // 2
    core = lax.axis_index("core")
    mine = lax.dynamic_slice_in_dim(rows, core * half, half, 0)
    other = lax.dynamic_slice_in_dim(rows, (1 - core) * half, half, 0)
    mine = mine + shift(other, "core", N_CORE, 1)
    moved = [shift(mine, "x", N_X, by) for by in (2, 1, 3)]
    total = mine + moved[0] + moved[1] + moved[2]
    theirs = shift(total, "core", N_CORE, 1)
    first = jnp.where(core == 0, total, theirs)
    second = jnp.where(core == 0, theirs, total)
    return jnp.concatenate([first, second], axis=0)


def tm_gather(rows):
    spread = jnp.broadcast_to(rows[None], (N_Y * N_Z,) + rows.shape)
    return lax.all_to_all(spread, ("y", "z"), 0, 0)


def y_scatter_sum(chunks):
    place = lax.axis_index("y")
    total = lax.dynamic_index_in_dim(chunks, place, 0, False)
    for by in (2, 1, 3):
        piece = lax.dynamic_index_in_dim(chunks, (place + by) % N_Y, 0, False)
        total = total + shift(piece, "y", N_Y, by)
    return total


def y_gather(piece):
    place = lax.axis_index("y")
    out = jnp.zeros((N_Y,) + piece.shape, piece.dtype)
    out = lax.dynamic_update_index_in_dim(out, piece, place, 0)
    for by in (2, 1, 3):
        out = lax.dynamic_update_index_in_dim(
            out, shift(piece, "y", N_Y, by), (place - by) % N_Y, 0
        )
    return out


def tm_sum(cross, error, moment):
    state_width = cross.shape[1]
    chunks = jnp.concatenate(
        [
            cross.reshape(N_Y, -1, state_width),
            moment.reshape(N_Y, -1, state_width),
            jnp.pad(error.reshape(N_Y, 1, state_width), ((0, 0), (0, 7), (0, 0))),
        ],
        axis=1,
    )
    c_rows, m_rows = cross.shape[0] // N_Y, moment.shape[0] // N_Y
    part = y_scatter_sum(chunks)
    width = error.shape[0] // (N_Y * N_Z)
    z_error = jnp.pad(
        part[c_rows + m_rows].reshape(N_Z, 1, width), ((0, 0), (0, 7), (0, state_width - width))
    )
    z_chunks = jnp.concatenate(
        [
            part[:c_rows].reshape(N_Z, -1, state_width),
            part[c_rows : c_rows + m_rows].reshape(N_Z, -1, state_width),
            z_error,
        ],
        axis=1,
    )
    piece = jnp.sum(lax.all_to_all(z_chunks, "z", 0, 0), axis=0)
    spread = jnp.broadcast_to(piece[None], (N_Z,) + piece.shape)
    whole = lax.all_to_all(spread, "z", 0, 0)
    c_z, m_z = c_rows // N_Z, m_rows // N_Z
    part = jnp.concatenate(
        [
            whole[:, :c_z].reshape(c_rows, state_width),
            whole[:, c_z : c_z + m_z].reshape(m_rows, state_width),
            jnp.pad(whole[:, c_z + m_z, :width].reshape(1, state_width), ((0, 7), (0, 0))),
        ],
        axis=0,
    )
    out = y_gather(part)
    return (
        out[:, :c_rows].reshape(cross.shape),
        out[:, c_rows + m_rows].reshape(error.shape),
        out[:, c_rows : c_rows + m_rows].reshape(moment.shape),
    )


def powers_of(matrix, count):
    found = [matrix]
    for _ in range(count - 1):
        found.append(product(found[-1], found[-1]))
    return found


def forward_prefix(rows_in, powers):
    current = rows_in
    length = current.shape[0]
    for level, powered in enumerate(powers):
        offset = 2**level
        moved = product(current[: length - offset], powered.T)
        current = current + jnp.concatenate(
            [jnp.zeros((offset, current.shape[1]), jnp.float32), moved], axis=0
        )
    return current


def backward_prefix(rows_in, powers):
    current = rows_in
    for level, powered in enumerate(powers):
        offset = 2**level
        moved = product(current[offset:], powered.T)
        current = current + jnp.concatenate(
            [moved, jnp.zeros((offset, current.shape[1]), jnp.float32)], axis=0
        )
    return current


def local(
    observations, emission, noise_precision, transition, info_gain, smoother_gain, smoother_input
):
    bin_rows = observations.shape[0]
    blocks = N_Y * N_Z
    levels = int(math.log2(bin_rows))
    block_levels = int(math.log2(blocks))
    weighted = (emission.astype(jnp.float32) * noise_precision[:, None]).astype(jnp.bfloat16)
    information = chan_sum(jnp.dot(observations, weighted, preferred_element_type=jnp.float32))

    a_powers = powers_of(transition, levels + block_levels)
    b_powers = powers_of(smoother_gain, levels + block_levels)
    lifted = product(smoother_gain, product(smoother_input, transition))
    for level in range(levels):
        lifted = lifted + product(b_powers[level], product(lifted, a_powers[level]))

    drive_rows = product(information, info_gain.T)
    filtered = forward_prefix(drive_rows, a_powers[:levels])
    inputs = product(filtered, smoother_input.T)
    smoothed = backward_prefix(inputs, b_powers[:levels])
    ends = jnp.concatenate([filtered[-1:], product(smoothed[:1], smoother_gain.T)], axis=0)
    gathered = tm_gather(ends)

    after = forward_prefix(gathered[:, 0], a_powers[levels:])
    zero = jnp.zeros((1, after.shape[1]), jnp.float32)
    enter = jnp.concatenate([zero, after[:-1]], axis=0)
    last = after[-1:]
    following = gathered[:, 1] + product(enter, lifted.T)
    final = last - product(last, smoother_input.T)
    follow = backward_prefix(
        jnp.concatenate([following[1:], final], axis=0), b_powers[levels:]
    )
    block = lax.axis_index(("y", "z"))
    carry = lax.dynamic_index_in_dim(enter, block, 0, True)
    carry_back = lax.dynamic_index_in_dim(follow, block, 0, True)

    drive_rows = drive_rows.at[:1].add(product(carry, transition.T))
    filtered = forward_prefix(drive_rows, a_powers[:levels])
    inputs = product(filtered, smoother_input.T).at[-1:].add(carry_back)
    smoothed = backward_prefix(inputs, b_powers[:levels])

    states_bf = smoothed.astype(jnp.bfloat16)
    cross_local = lax.dot_general(
        observations, states_bf, (((0,), (0,)), ((), ())), preferred_element_type=jnp.float32
    )
    predicted = lax.dot_general(
        states_bf, emission, (((1,), (1,)), ((), ())), preferred_element_type=jnp.float32
    )
    error_rows = observations.astype(jnp.float32) - predicted
    error_local = jnp.sum(error_rows * error_rows, axis=0)
    moment_local = lax.dot_general(
        smoothed,
        smoothed,
        (((0,), (0,)), ((), ())),
        precision=FULL_PRECISION,
        preferred_element_type=jnp.float32,
    )
    cross_sum, error_sum, moment_sum = tm_sum(cross_local, error_local, moment_local)
    total_bins = bin_rows * blocks
    return (
        smoothed,
        cross_sum / math.sqrt(total_bins),
        error_sum / total_bins,
        moment_sum / total_bins,
    )


def solution(mesh):
    tm, chan = ("y", "z"), ("x", "core")
    split = Mesh(mesh.devices.reshape(N_Y, N_Z, N_X, N_CORE), tm + chan)
    placed = (P(tm, chan), P(chan, None), P(chan), P(), P(), P(), P())
    return jax.shard_map(
        local,
        mesh=split,
        in_specs=placed,
        out_specs=(P(tm, None), P(chan, None), P(chan), P()),
        check_vma=False,
    )
```

```python
import functools
import math

import jax
import jax.numpy as jnp
import numpy as np
from jax import lax
from jax.experimental import pallas as pl
from jax.experimental.pallas import tpu as pltpu
from jax.sharding import Mesh, PartitionSpec as P

N_Y, N_Z, N_X, N_CORE = 4, 8, 4, 2
BLOCKS = N_Y * N_Z
SUB = 8
F32, BF16 = jnp.float32, jnp.bfloat16
KERNELS = True


def call(body, outs, *args):
    if not KERNELS:
        return body(*args)

    def kernel(*refs):
        values = body(*[ref[...] for ref in refs[: len(args)]])
        for ref, value in zip(refs[len(args) :], values):
            ref[...] = value

    return pl.pallas_call(
        kernel,
        out_shape=[jax.ShapeDtypeStruct(shape, dtype) for shape, dtype in outs],
        compiler_params=pltpu.CompilerParams(vmem_limit_bytes=56 * 2**20),
        name=body.__name__,
    )(*args)


def roll(rows, by):
    if KERNELS:
        return pltpu.roll(rows, by % rows.shape[0], 0)
    return jnp.roll(rows, by, 0)


def row_index(rows):
    return lax.broadcasted_iota(jnp.int32, rows.shape, 0)


def dot(left, right, dims=((1,), (0,))):
    return lax.dot_general(left, right, (dims, ((), ())), preferred_element_type=F32)


def dot_full(left, right):
    return jnp.dot(left, right, precision=lax.Precision.HIGHEST, preferred_element_type=F32)


def cut(value):
    high = value.astype(BF16)
    return high, (value - high.astype(F32)).astype(BF16)


def mul(rows, high, low):
    rows_high, rows_low = cut(rows)
    return dot(rows_high, high) + (dot(rows_low, high) + dot(rows_high, low))


def stack_cut(values):
    pairs = [cut(value) for value in values]
    return jnp.stack([p[0] for p in pairs]), jnp.stack([p[1] for p in pairs])


def small_powers(transition, info_gain, smoother_gain, smoother_input):
    a, b, g, k = transition.T, smoother_gain.T, smoother_input.T, info_gain.T
    kg = dot_full(k, g)
    ag = dot_full(a, g)
    lead = stack_cut([k, kg, dot_full(kg, b), ag, g])
    m = dot_full(ag, b)
    a_list, b_list, m_list, n_list = [], [], [], []
    for _ in range(8):
        a_list.append(a)
        b_list.append(b)
        m_list.append(m)
        n = mul(a, *cut(m))
        n_list.append(n)
        m = m + mul(n, *cut(b))
        a, b = dot_full(a, a), dot_full(b, b)
    return (
        *lead,
        *stack_cut(a_list),
        *stack_cut(b_list),
        *stack_cut(m_list),
        *stack_cut(n_list),
        a,
        b,
        m,
    )


def big_powers(a, b, m):
    a_list, b_list = [a], [b]
    for _ in range(4):
        a_list.append(dot_full(a_list[-1], a_list[-1]))
        b_list.append(dot_full(b_list[-1], b_list[-1]))
    return (*stack_cut(a_list), *stack_cut(b_list), *cut(m))


def information_part(core, order, observations, emission, noise_precision):
    rows = dot(order, observations).astype(BF16)
    scale = jnp.broadcast_to(noise_precision, (128, noise_precision.shape[1])).T
    scale = jnp.concatenate([scale] * (emission.shape[1] // 128), axis=1)
    weighted = (emission.astype(F32) * scale).astype(BF16)
    information = dot(rows, weighted)
    half = rows.shape[0] // 2
    first = jnp.broadcast_to(core, (half, information.shape[1])) == 0
    mine = jnp.where(first, information[:half], information[half:])
    other = jnp.where(first, information[half:], information[:half])
    return mine, other


def channel_slices(order, observations):
    rows = dot(order, observations)
    width = rows.shape[1] // N_Y
    return tuple(rows[:, i * width : (i + 1) * width] for i in range(N_Y))


def up_sweep(lead, a_cut, b_cut, m_cut, information):
    lead_high, lead_low = lead
    drive = mul(information, lead_high[0], lead_low[0])
    shown = mul(information, lead_high[1], lead_low[1])
    end = drive
    start = mul(information, lead_high[2], lead_low[2])
    ends, follows = [], []
    for level in range(5):
        half = end.shape[0] // 2
        first, second = end[:half], end[half:]
        follow = start[half:] + mul(first, m_cut[0][level], m_cut[1][level])
        ends.append(first)
        follows.append(follow)
        start = start[:half] + mul(follow, b_cut[0][level], b_cut[1][level])
        end = second + mul(first, a_cut[0][level], a_cut[1][level])
    return shown, end, start, ends, follows


def sub_sweep(a_cut, b_cut, m_cut, end, start):
    ends, follows = [], []
    for level in range(5, 8):
        by = 2 ** (level - 5)
        follow = roll(start, -by) + mul(end, m_cut[0][level], m_cut[1][level])
        ends.append(end)
        follows.append(follow)
        start = start + mul(follow, b_cut[0][level], b_cut[1][level])
        end = mul(end, a_cut[0][level], a_cut[1][level]) + roll(end, -by)
    return end, start, ends, follows


def block_ends(core, total, theirs, lead_h, lead_l, a_h, a_l, b_h, b_l, m_h, m_l):
    first = jnp.broadcast_to(core, total.shape) == 0
    information = jnp.concatenate(
        [jnp.where(first, total, theirs), jnp.where(first, theirs, total)], axis=0
    )
    a_cut, b_cut, m_cut = (a_h, a_l), (b_h, b_l), (m_h, m_l)
    _, end, start, _, _ = up_sweep((lead_h, lead_l), a_cut, b_cut, m_cut, information)
    end, start, _, _ = sub_sweep(a_cut, b_cut, m_cut, end, start)
    pair = jnp.concatenate([end[None, :1], start[None, :1]], axis=1)
    return information, jnp.broadcast_to(pair, (BLOCKS, 2, end.shape[1]))


def spread_first(rows, by):
    rows = jnp.where(row_index(rows) % (2 * by) == 0, rows, 0.0)
    step = 1
    while step < 2 * by:
        rows = rows + roll(rows, step)
        step *= 2
    return rows


def joined(pieces):
    width = pieces[0].shape[1]
    return jnp.concatenate(
        [piece.reshape(-1, 1, SUB, width) for piece in pieces], axis=1
    ).reshape(-1, width)


def block_trees(
    o0, o1, o2, o3, i0, i1, i2, i3, lead_h, lead_l, a_h, a_l, b_h, b_l, m_h, m_l
):
    a_cut, b_cut, m_cut = (a_h, a_l), (b_h, b_l), (m_h, m_l)
    information = joined([i0, i1, i2, i3])
    shown, end, start, ends, follows = up_sweep(
        (lead_h, lead_l), a_cut, b_cut, m_cut, information
    )
    _, _, sub_ends, sub_follows = sub_sweep(a_cut, b_cut, m_cut, end, start)
    sub_ends = [spread_first(rows, 2**i) for i, rows in enumerate(sub_ends)]
    sub_follows = [spread_first(rows, 2**i) for i, rows in enumerate(sub_follows)]
    observed = joined([o0, o1, o2, o3]).astype(BF16)
    return (
        shown,
        jnp.concatenate(ends, axis=0),
        jnp.concatenate(follows, axis=0),
        jnp.concatenate(sub_ends, axis=0),
        jnp.concatenate(sub_follows, axis=0),
        observed,
    )


def states_and_sums(
    block,
    natural,
    gathered,
    shown,
    ends,
    follows,
    sub_ends,
    sub_follows,
    observed,
    emission,
    lead_h,
    lead_l,
    a_h,
    a_l,
    b_h,
    b_l,
    n_h,
    n_l,
    a_big_h,
    a_big_l,
    b_big_h,
    b_big_l,
    m_h,
    m_l,
):
    width = shown.shape[1]
    after = gathered[:, 0]
    index = row_index(after)
    for level in range(5):
        by = 2**level
        before = jnp.where(index >= by, roll(after, by), 0.0)
        after = after + mul(before, a_big_h[level], a_big_l[level])
    enter = jnp.where(index >= 1, roll(after, 1), 0.0)
    follow = gathered[:, 1] + mul(enter, m_h, m_l)
    final = after - mul(after, lead_h[4], lead_l[4])
    follow = jnp.where(index < BLOCKS - 1, roll(follow, -1), final)
    for level in range(5):
        by = 2**level
        later = jnp.where(index < BLOCKS - by, roll(follow, -by), 0.0)
        follow = follow + mul(later, b_big_h[level], b_big_l[level])

    place = lax.broadcasted_iota(jnp.int32, (N_Y * SUB, BLOCKS), 0)
    source = lax.broadcasted_iota(jnp.int32, (N_Y * SUB, BLOCKS), 1)
    wanted = jnp.broadcast_to(block, place.shape) - N_Z * (place // SUB)
    pick = (source == jnp.where(wanted < 0, wanted + BLOCKS, wanted)).astype(BF16)

    def picked(rows):
        high, low = cut(rows)
        return dot(pick, high) + dot(pick, low)

    enter, follow = picked(enter), picked(follow)
    count = N_Y * SUB
    index = row_index(enter)
    for level in (7, 6, 5):
        by = 2 ** (level - 5)
        part = (level - 5) * count
        second = sub_ends[part : part + count] + mul(enter, a_h[level], a_l[level])
        first = (
            sub_follows[part : part + count]
            + mul(enter, n_h[level], n_l[level])
            + mul(follow, b_h[level], b_l[level])
        )
        is_second = (index // by) % 2 == 1
        enter = jnp.where(is_second, second, enter)
        follow = jnp.where(is_second, follow, first)

    bottom = ends.shape[0]
    for level in (4, 3, 2, 1, 0):
        rows = enter.shape[0]
        top, bottom = bottom, bottom - rows
        second = ends[bottom:top] + mul(enter, a_h[level], a_l[level])
        first = (
            follows[bottom:top]
            + mul(enter, n_h[level], n_l[level])
            + mul(follow, b_h[level], b_l[level])
        )
        enter = jnp.concatenate([enter, second], axis=0)
        follow = jnp.concatenate([first, follow], axis=0)
    smoothed = shown + mul(enter, lead_h[3], lead_l[3]) + follow

    high, low = cut(smoothed)
    cross = dot(observed, high, ((0,), (0,)))
    predicted = dot(high, emission, ((1,), (1,)))
    error = observed.astype(F32) - predicted
    error = jnp.broadcast_to(jnp.sum(error * error, axis=0, keepdims=True), (8, error.shape[1]))
    crossed = dot(high, jnp.concatenate([high, low], axis=1), ((0,), (0,)))
    moment = crossed[:, :width] + (crossed[:, width:] + crossed[:, width:].T)

    own = smoothed.reshape(-1, N_Y, SUB, width)[:, 0].reshape(-1, width)
    high, rest = own.astype(BF16), own
    out = dot(natural, high)
    for _ in range(2):
        rest = rest - high.astype(F32)
        high = rest.astype(BF16)
        out = out + dot(natural, high)

    channels = cross.shape[0]
    share = moment.shape[0] // N_Y
    y = jnp.broadcast_to(block, (share, width)) // N_Z
    mine = moment[:share]
    for i in range(1, N_Y):
        mine = jnp.where(y == i, moment[i * share : (i + 1) * share], mine)
    payload = jnp.concatenate(
        [
            cross.reshape(N_Z, channels // N_Z, width),
            mine.reshape(N_Z, share // N_Z, width),
            jnp.broadcast_to(error[None], (N_Z,) + error.shape),
        ],
        axis=1,
    )
    return out, payload


def add_pieces(pieces):
    total = pieces[0]
    for i in range(1, N_Z):
        total = total + pieces[i]
    kept = total.shape[0] - 8
    return jnp.broadcast_to(total[None, :kept], (N_Z, kept, total.shape[1])), total[kept:]


def assemble(bins, channel_rows, place, sums, errors):
    width = sums[0].shape[2]
    cross, moment, error = [], [], []
    for i in range(N_Y):
        want = jnp.broadcast_to(place, sums[0].shape) - i
        want = jnp.where(want < 0, want + N_Y, want)
        whole = sums[0]
        for by in range(1, N_Y):
            whole = jnp.where(want == by, sums[by], whole)
        cross.append(whole[:, :channel_rows].reshape(-1, width) * (1.0 / math.sqrt(bins)))
        moment.append(whole[:, channel_rows:].reshape(-1, width) * (1.0 / bins))
        want = want[0, :8]
        line = errors[0]
        for by in range(1, N_Y):
            line = jnp.where(want == by, errors[by], line)
        error.append(line[:1] * (1.0 / bins))
    return (
        jnp.concatenate(cross, axis=0),
        jnp.concatenate(moment, axis=0),
        jnp.concatenate(error, axis=1),
    )


def shift(value, axis, count, by):
    return lax.ppermute(value, axis, [(i, (i + by) % count) for i in range(count)])


def bit_reversed(count):
    bits = count.bit_length() - 1
    return [int(format(i, "0%db" % bits)[::-1], 2) for i in range(count)]


def row_order(bins):
    length = bins // SUB
    times = np.array([[j * length + t for j in range(SUB)] for t in bit_reversed(length)])
    return np.eye(bins, dtype=np.float32)[times.reshape(-1)]


def local(
    observations, emission, noise_precision, transition, info_gain, smoother_gain, smoother_input
):
    bins, channels = observations.shape
    width = transition.shape[0]
    y, core = lax.axis_index("y"), lax.axis_index("core")
    order = jnp.asarray(row_order(bins), BF16)
    natural = jnp.asarray(row_order(bins).T, BF16)
    one = lambda number: number.astype(jnp.int32).reshape(1, 1)

    mine, other = call(
        information_part,
        [((bins // 2, width), F32)] * 2,
        one(core),
        order,
        observations,
        emission,
        noise_precision.reshape(1, channels),
    )
    mine = mine + shift(other, "core", N_CORE, 1)
    moved = [shift(mine, "x", N_X, by) for by in (2, 1, 3)]

    slices = call(channel_slices, [((bins, channels // N_Y), F32)] * N_Y, order, observations)
    slices = jnp.stack(slices)
    piece = lambda by: lax.dynamic_index_in_dim(slices, (y + by) % N_Y, 0, False)
    observed = [piece(0)] + [shift(piece(by), "y", N_Y, by) for by in (1, 2, 3)]
    emission_part = lax.dynamic_slice_in_dim(
        emission, y * (channels // N_Y), channels // N_Y, 0
    )

    square = (width, width)
    stack = lambda n: [((n,) + square, BF16)] * 2
    small = call(
        small_powers,
        stack(5) + stack(8) * 4 + [(square, F32)] * 3,
        transition,
        info_gain,
        smoother_gain,
        smoother_input,
    )
    lead, a_cut, b_cut, m_cut, n_cut = (small[i : i + 2] for i in range(0, 10, 2))

    total = mine + moved[0] + moved[1] + moved[2]
    theirs = shift(total, "core", N_CORE, 1)
    information, ends = call(
        block_ends,
        [((bins, width), F32), ((BLOCKS, 2, width), F32)],
        one(core),
        total,
        theirs,
        *lead,
        *a_cut,
        *b_cut,
        *m_cut,
    )
    gathered = lax.all_to_all(ends, ("y", "z"), 0, 0)
    informations = [information] + [shift(information, "y", N_Y, by) for by in (1, 2, 3)]
    big = call(big_powers, stack(5) * 2 + [(square, BF16)] * 2, *small[10:])
    tree_rows = N_Y * SUB * 31
    shown, tree_ends, follows, sub_ends, sub_follows, seen = call(
        block_trees,
        [
            ((N_Y * bins, width), F32),
            ((tree_rows, width), F32),
            ((tree_rows, width), F32),
            ((3 * N_Y * SUB, width), F32),
            ((3 * N_Y * SUB, width), F32),
            ((N_Y * bins, channels // N_Y), BF16),
        ],
        *observed,
        *informations,
        *lead,
        *a_cut,
        *b_cut,
        *m_cut,
    )
    channel_rows, moment_rows = channels // (N_Y * N_Z), width // (N_Y * N_Z)
    smoothed, payload = call(
        states_and_sums,
        [((bins, width), F32), ((N_Z, channel_rows + moment_rows + 8, width), F32)],
        one(lax.axis_index(("y", "z"))),
        natural,
        gathered,
        shown,
        tree_ends,
        follows,
        sub_ends,
        sub_follows,
        seen,
        emission_part,
        *lead,
        *a_cut,
        *b_cut,
        *n_cut,
        *big,
    )
    payload = lax.all_to_all(payload, "z", 0, 0)
    spread, error = call(
        add_pieces,
        [((N_Z, channel_rows + moment_rows, width), F32), ((8, width), F32)],
        payload,
    )
    whole = lax.all_to_all(spread, "z", 0, 0)
    errors = [error] + [shift(error, "y", N_Y, by) for by in (1, 2, 3)]
    sums = [whole] + [shift(whole, "y", N_Y, by) for by in (2, 1, 3)]
    sums = [sums[0], sums[2], sums[1], sums[3]]

    def finish(place, s0, s1, s2, s3, e0, e1, e2, e3):
        return assemble(bins * BLOCKS, channel_rows, place, [s0, s1, s2, s3], [e0, e1, e2, e3])

    cross, moment, error = call(
        finish,
        [((channels, width), F32), (square, F32), ((1, channels), F32)],
        one(y),
        *sums,
        *errors,
    )
    return smoothed, cross, error.reshape(channels), moment


def solution(mesh):
    tm, chan = ("y", "z"), ("x", "core")
    split = Mesh(mesh.devices.reshape(N_Y, N_Z, N_X, N_CORE), tm + chan)
    placed = (P(tm, chan), P(chan, None), P(chan), P(), P(), P(), P())
    return jax.shard_map(
        local,
        mesh=split,
        in_specs=placed,
        out_specs=(P(tm, None), P(chan, None), P(chan), P()),
        check_vma=False,
    )
```

```python
import functools
import math

import jax
import jax.numpy as jnp
import numpy as np
from jax import lax
from jax.experimental import pallas as pl
from jax.experimental.pallas import tpu as pltpu
from jax.sharding import Mesh, PartitionSpec as P

N_Y, N_Z, N_X, N_CORE = 4, 8, 4, 2
BLOCKS = N_Y * N_Z
SUB = 8
F32, BF16 = jnp.float32, jnp.bfloat16
KERNELS = True


def call(body, outs, *args, limit=16, scalars=(), hbm=()):
    if not KERNELS:
        return body(*[arg[0, 0] if i in scalars else arg for i, arg in enumerate(args)])

    def kernel(*refs):
        values = body(
            *[ref[0, 0] if i in scalars else ref[...] for i, ref in enumerate(refs[: len(args)])]
        )
        for ref, value in zip(refs[len(args) :], values):
            ref[...] = value

    args = [
        arg if i in scalars else pltpu.with_memory_space_constraint(arg, pltpu.VMEM)
        for i, arg in enumerate(args)
    ]
    return pl.pallas_call(
        kernel,
        out_shape=[
            jax.ShapeDtypeStruct(shape, dtype) if i in hbm else pltpu.VMEM(shape, dtype)
            for i, (shape, dtype) in enumerate(outs)
        ],
        in_specs=[
            pl.BlockSpec(memory_space=pltpu.SMEM if i in scalars else pltpu.VMEM)
            for i in range(len(args))
        ],
        out_specs=[pl.BlockSpec(memory_space=pltpu.VMEM)] * len(outs),
        compiler_params=pltpu.CompilerParams(vmem_limit_bytes=limit * 2**20),
        name=body.__name__,
    )(*args)


def roll(rows, by):
    if KERNELS:
        return pltpu.roll(rows, by % rows.shape[0], 0)
    return jnp.roll(rows, by, 0)


def roll_lanes(rows, by):
    if KERNELS:
        return pltpu.roll(rows, by, 1)
    return jnp.roll(rows, by, 1)


def row_index(rows):
    return lax.broadcasted_iota(jnp.int32, rows.shape, 0)


def dot(left, right, dims=((1,), (0,))):
    return lax.dot_general(left, right, (dims, ((), ())), preferred_element_type=F32)


def dot_full(left, right):
    return jnp.dot(left, right, precision=lax.Precision.HIGHEST, preferred_element_type=F32)


def cut(value):
    high = value.astype(BF16)
    return high, (value - high.astype(F32)).astype(BF16)


def mul(rows, high, low):
    rows_high, rows_low = cut(rows)
    return dot(rows_high, high) + (dot(rows_low, high) + dot(rows_high, low))


def stack_cut(values):
    pairs = [cut(value) for value in values]
    return jnp.stack([p[0] for p in pairs]), jnp.stack([p[1] for p in pairs])


def small_powers(transition, info_gain, smoother_gain, smoother_input):
    a, b, g, k = transition.T, smoother_gain.T, smoother_input.T, info_gain.T
    kg = dot_full(k, g)
    ag = dot_full(a, g)
    lead = stack_cut([k, kg, dot_full(kg, b), ag, g])
    m = dot_full(ag, b)
    a_list, b_list, m_list, n_list = [], [], [], []
    for _ in range(8):
        a_list.append(a)
        b_list.append(b)
        m_list.append(m)
        n = mul(a, *cut(m))
        n_list.append(n)
        m = m + mul(n, *cut(b))
        a, b = dot_full(a, a), dot_full(b, b)
    return (
        *lead,
        *stack_cut(a_list),
        *stack_cut(b_list),
        *stack_cut(m_list),
        *stack_cut(n_list),
        a,
        b,
        m,
    )


def big_powers(a, b, m):
    a_list, b_list = [a], [b]
    for _ in range(4):
        a_list.append(dot_full(a_list[-1], a_list[-1]))
        b_list.append(dot_full(b_list[-1], b_list[-1]))
    return (*stack_cut(a_list), *stack_cut(b_list), *cut(m))


def information_part(core, order, observations, emission, noise_precision):
    rows = dot(order, observations).astype(BF16)
    scale = jnp.broadcast_to(noise_precision, (128, noise_precision.shape[1])).T
    scale = jnp.concatenate([scale] * (emission.shape[1] // 128), axis=1)
    weighted = (emission.astype(F32) * scale).astype(BF16)
    information = dot(rows, weighted)
    half = rows.shape[0] // 2
    first = core == 0
    mine = jnp.where(first, information[:half], information[half:])
    other = jnp.where(first, information[half:], information[:half])
    return mine, other


def chosen(number, values):
    out = values[0]
    for i in range(1, len(values)):
        out = jnp.where(number == i, values[i], out)
    return out


def channel_slices(y, order, observations, emission):
    rows = dot(order, observations)
    width = rows.shape[1] // N_Y
    parts = [rows[:, i * width : (i + 1) * width] for i in range(N_Y)]
    emission = emission.astype(F32)
    emission = chosen(y, [emission[i * width : (i + 1) * width] for i in range(N_Y)])
    turned = [chosen(y, [parts[(i + by) % N_Y] for i in range(N_Y)]) for by in range(N_Y)]
    return (*turned, emission.astype(BF16))


def up_sweep(lead, a_cut, b_cut, m_cut, information):
    lead_high, lead_low = lead
    drive = mul(information, lead_high[0], lead_low[0])
    shown = mul(information, lead_high[1], lead_low[1])
    end = drive
    start = mul(information, lead_high[2], lead_low[2])
    ends, follows = [], []
    for level in range(5):
        half = end.shape[0] // 2
        first, second = end[:half], end[half:]
        follow = start[half:] + mul(first, m_cut[0][level], m_cut[1][level])
        ends.append(first)
        follows.append(follow)
        start = start[:half] + mul(follow, b_cut[0][level], b_cut[1][level])
        end = second + mul(first, a_cut[0][level], a_cut[1][level])
    return shown, end, start, ends, follows


def sub_sweep(a_cut, b_cut, m_cut, end, start):
    ends, follows = [], []
    for level in range(5, 8):
        by = 2 ** (level - 5)
        follow = roll(start, -by) + mul(end, m_cut[0][level], m_cut[1][level])
        ends.append(end)
        follows.append(follow)
        start = start + mul(follow, b_cut[0][level], b_cut[1][level])
        end = mul(end, a_cut[0][level], a_cut[1][level]) + roll(end, -by)
    return end, start, ends, follows


def block_ends(core, total, theirs, lead_h, lead_l, a_h, a_l, b_h, b_l, m_h, m_l):
    first = core == 0
    information = jnp.concatenate(
        [jnp.where(first, total, theirs), jnp.where(first, theirs, total)], axis=0
    )
    a_cut, b_cut, m_cut = (a_h, a_l), (b_h, b_l), (m_h, m_l)
    _, end, start, _, _ = up_sweep((lead_h, lead_l), a_cut, b_cut, m_cut, information)
    end, start, _, _ = sub_sweep(a_cut, b_cut, m_cut, end, start)
    pair = jnp.concatenate([end[None, :1], start[None, :1]], axis=1)
    return information, jnp.broadcast_to(pair, (BLOCKS, 2, end.shape[1]))


def spread_first(rows, by):
    rows = jnp.where(row_index(rows) % (2 * by) == 0, rows, 0.0)
    step = 1
    while step < 2 * by:
        rows = rows + roll(rows, step)
        step *= 2
    return rows


def joined(pieces):
    width = pieces[0].shape[1]
    return jnp.concatenate(
        [piece.reshape(-1, 1, SUB, width) for piece in pieces], axis=1
    ).reshape(-1, width)


def block_trees(
    o0, o1, o2, o3, i0, i1, i2, i3, lead_h, lead_l, a_h, a_l, b_h, b_l, m_h, m_l
):
    a_cut, b_cut, m_cut = (a_h, a_l), (b_h, b_l), (m_h, m_l)
    information = joined([i0, i1, i2, i3])
    shown, end, start, ends, follows = up_sweep(
        (lead_h, lead_l), a_cut, b_cut, m_cut, information
    )
    _, _, sub_ends, sub_follows = sub_sweep(a_cut, b_cut, m_cut, end, start)
    sub_ends = [spread_first(rows, 2**i) for i, rows in enumerate(sub_ends)]
    sub_follows = [spread_first(rows, 2**i) for i, rows in enumerate(sub_follows)]
    observed = joined([o0, o1, o2, o3]).astype(BF16)
    return (
        shown,
        jnp.concatenate(ends, axis=0),
        jnp.concatenate(follows, axis=0),
        jnp.concatenate(sub_ends, axis=0),
        jnp.concatenate(sub_follows, axis=0),
        observed,
    )


def states_and_sums(
    block,
    natural,
    gathered,
    shown,
    ends,
    follows,
    sub_ends,
    sub_follows,
    observed,
    emission,
    lead_h,
    lead_l,
    a_h,
    a_l,
    b_h,
    b_l,
    n_h,
    n_l,
    a_big_h,
    a_big_l,
    b_big_h,
    b_big_l,
    m_h,
    m_l,
):
    width = shown.shape[1]
    after = gathered[:, 0]
    index = row_index(after)
    for level in range(5):
        by = 2**level
        before = jnp.where(index >= by, roll(after, by), 0.0)
        after = after + mul(before, a_big_h[level], a_big_l[level])
    enter = jnp.where(index >= 1, roll(after, 1), 0.0)
    follow = gathered[:, 1] + mul(enter, m_h, m_l)
    final = after - mul(after, lead_h[4], lead_l[4])
    follow = jnp.where(index < BLOCKS - 1, roll(follow, -1), final)
    for level in range(5):
        by = 2**level
        later = jnp.where(index < BLOCKS - by, roll(follow, -by), 0.0)
        follow = follow + mul(later, b_big_h[level], b_big_l[level])

    place = lax.broadcasted_iota(jnp.int32, (N_Y * SUB, BLOCKS), 0)
    source = lax.broadcasted_iota(jnp.int32, (N_Y * SUB, BLOCKS), 1)
    wanted = block - N_Z * (place // SUB)
    pick = (source == jnp.where(wanted < 0, wanted + BLOCKS, wanted)).astype(BF16)

    def picked(rows):
        high, low = cut(rows)
        return dot(pick, high) + dot(pick, low)

    enter, follow = picked(enter), picked(follow)
    count = N_Y * SUB
    index = row_index(enter)
    for level in (7, 6, 5):
        by = 2 ** (level - 5)
        part = (level - 5) * count
        second = sub_ends[part : part + count] + mul(enter, a_h[level], a_l[level])
        first = (
            sub_follows[part : part + count]
            + mul(enter, n_h[level], n_l[level])
            + mul(follow, b_h[level], b_l[level])
        )
        is_second = (index // by) % 2 == 1
        enter = jnp.where(is_second, second, enter)
        follow = jnp.where(is_second, follow, first)

    bottom = ends.shape[0]
    for level in (4, 3, 2, 1, 0):
        rows = enter.shape[0]
        top, bottom = bottom, bottom - rows
        second = ends[bottom:top] + mul(enter, a_h[level], a_l[level])
        first = (
            follows[bottom:top]
            + mul(enter, n_h[level], n_l[level])
            + mul(follow, b_h[level], b_l[level])
        )
        enter = jnp.concatenate([enter, second], axis=0)
        follow = jnp.concatenate([first, follow], axis=0)
    smoothed = shown + mul(enter, lead_h[3], lead_l[3]) + follow

    high, low = cut(smoothed)
    cross = dot(observed, high, ((0,), (0,)))
    predicted = dot(high, emission, ((1,), (1,)))
    error = observed.astype(F32) - predicted
    error = jnp.broadcast_to(jnp.sum(error * error, axis=0, keepdims=True), (8, error.shape[1]))
    crossed = dot(high, jnp.concatenate([high, low], axis=1), ((0,), (0,)))
    moment = crossed[:, :width] + (crossed[:, width:] + crossed[:, width:].T)

    own = smoothed.reshape(-1, N_Y, SUB, width)[:, 0].reshape(-1, width)
    high, rest = own.astype(BF16), own
    out = dot(natural, high)
    for _ in range(2):
        rest = rest - high.astype(F32)
        high = rest.astype(BF16)
        out = out + dot(natural, high)

    channels = cross.shape[0]
    share, line = width // N_Y, channels // N_Z
    y = block // N_Z
    mine = chosen(y, [moment[i * share : (i + 1) * share] for i in range(N_Y)])
    free = share * jnp.where(y == N_Y - 1, 0, y + 1)
    lane = lax.broadcasted_iota(jnp.int32, (8, width), 1)
    row = lax.broadcasted_iota(jnp.int32, (8, width), 0)
    is_free = (lane >= free) & (lane < free + share)
    is_error = (lane >= free) & (lane < free + line) & (row == 0)
    chunks = []
    for z in range(N_Z):
        turned = roll_lanes(error, free + (width - line * z))
        tile = jnp.where(is_free, 0.0, mine[8 * z : 8 * z + 8])
        chunks.append(jnp.where(is_error, turned, tile))
    payload = jnp.concatenate(
        [cross.reshape(N_Z, line, width), jnp.stack(chunks)], axis=1
    )
    return out, payload


def add_pieces(pieces):
    total = pieces[0]
    for i in range(1, N_Z):
        total = total + pieces[i]
    return (jnp.broadcast_to(total[None], (N_Z,) + total.shape),)


def assemble(bins, place, *sums):
    width = sums[0].shape[2]
    share = width // N_Y
    line = sums[0].shape[1] - 8
    lane = lax.broadcasted_iota(jnp.int32, (8, width), 1)
    cross, moment, errors = [], [], []
    for y in range(N_Y):
        whole = chosen(place, [sums[(i - y) % N_Y] for i in range(N_Y)])
        cross.append(whole[:, :line].reshape(-1, width) * (1.0 / math.sqrt(bins)))
        moment.append(whole[:, line:].reshape(-1, width))
        error = jnp.zeros((8, width), F32)
        for z in range(N_Z):
            turned = roll_lanes(whole[z, line:], (line * z - share * ((y + 1) % N_Y)) % width)
            error = jnp.where((lane >= line * z) & (lane < line * z + line), turned, error)
        errors.append(error[:1] * (1.0 / bins))
    moment = jnp.concatenate(moment, axis=0)
    row = lax.broadcasted_iota(jnp.int32, moment.shape, 0) // share
    column = lax.broadcasted_iota(jnp.int32, moment.shape, 1) // share
    free = column == jnp.where(row == N_Y - 1, 0, row + 1)
    moment = jnp.where(free, moment.T, moment) * (1.0 / bins)
    return jnp.concatenate(cross, axis=0), moment, jnp.concatenate(errors, axis=1)


def shift(value, axis, count, by):
    return lax.ppermute(value, axis, [(i, (i + by) % count) for i in range(count)])


def bit_reversed(count):
    bits = count.bit_length() - 1
    return [int(format(i, "0%db" % bits)[::-1], 2) for i in range(count)]


def row_order(bins):
    length = bins // SUB
    times = np.array([[j * length + t for j in range(SUB)] for t in bit_reversed(length)])
    return np.eye(bins, dtype=np.float32)[times.reshape(-1)]


def local(
    observations, emission, noise_precision, transition, info_gain, smoother_gain, smoother_input
):
    bins, channels = observations.shape
    width = transition.shape[0]
    y, core = lax.axis_index("y"), lax.axis_index("core")
    order = jnp.asarray(row_order(bins), BF16)
    natural = jnp.asarray(row_order(bins).T, BF16)
    one = lambda number: number.astype(jnp.int32).reshape(1, 1)

    mine, other = call(
        information_part,
        [((bins // 2, width), F32)] * 2,
        one(core),
        order,
        observations,
        emission,
        noise_precision.reshape(1, channels),
        scalars=(0,),
    )
    mine = mine + shift(other, "core", N_CORE, 1)
    mine, later = lax.optimization_barrier((mine, observations))
    moved = [shift(mine, "x", N_X, by) for by in (2, 1, 3)]

    part = channels // N_Y
    *slices, emission_part = call(
        channel_slices,
        [((bins, part), F32)] * N_Y + [((part, width), BF16)],
        one(y),
        order,
        later,
        emission,
        scalars=(0,),
    )
    observed = slices[:1] + [shift(slices[by], "y", N_Y, by) for by in (1, 2, 3)]

    square = (width, width)
    stack = lambda n: [((n,) + square, BF16)] * 2
    small = call(
        small_powers,
        stack(5) + stack(8) * 4 + [(square, F32)] * 3,
        transition,
        info_gain,
        smoother_gain,
        smoother_input,
    )
    lead, a_cut, b_cut, m_cut, n_cut = (small[i : i + 2] for i in range(0, 10, 2))

    total = mine + moved[0] + moved[1] + moved[2]
    theirs = shift(total, "core", N_CORE, 1)
    information, ends = call(
        block_ends,
        [((bins, width), F32), ((BLOCKS, 2, width), F32)],
        one(core),
        total,
        theirs,
        *lead,
        *a_cut,
        *b_cut,
        *m_cut,
        scalars=(0,),
    )
    gathered = lax.all_to_all(ends, ("y", "z"), 0, 0)
    informations = [information] + [shift(information, "y", N_Y, by) for by in (1, 2, 3)]
    big = call(big_powers, stack(5) * 2 + [(square, BF16)] * 2, *small[10:])
    tree_rows = N_Y * SUB * 31
    shown, tree_ends, follows, sub_ends, sub_follows, seen = call(
        block_trees,
        [
            ((N_Y * bins, width), F32),
            ((tree_rows, width), F32),
            ((tree_rows, width), F32),
            ((3 * N_Y * SUB, width), F32),
            ((3 * N_Y * SUB, width), F32),
            ((N_Y * bins, channels // N_Y), BF16),
        ],
        *observed,
        *informations,
        *lead,
        *a_cut,
        *b_cut,
        *m_cut,
    )
    rows = channels // (N_Y * N_Z) + 8
    smoothed, payload = call(
        states_and_sums,
        [((bins, width), F32), ((N_Z, rows, width), F32)],
        one(lax.axis_index(("y", "z"))),
        natural,
        gathered,
        shown,
        tree_ends,
        follows,
        sub_ends,
        sub_follows,
        seen,
        emission_part,
        *lead,
        *a_cut,
        *b_cut,
        *n_cut,
        *big,
        scalars=(0,),
    )
    payload = lax.all_to_all(payload, "z", 0, 0)
    (spread,) = call(add_pieces, [((N_Z, rows, width), F32)], payload)
    whole = lax.all_to_all(spread, "z", 0, 0)
    far, near, back = (shift(whole, "y", N_Y, by) for by in (2, 1, 3))

    def finish(*args):
        return assemble(bins * BLOCKS, *args)

    cross, moment, error = call(
        finish,
        [((channels, width), F32), (square, F32), ((1, channels), F32)],
        one(y),
        whole,
        near,
        far,
        back,
        scalars=(0,),
        hbm=(0, 1, 2),
    )
    return smoothed, cross, error.reshape(channels), moment


def solution(mesh):
    tm, chan = ("y", "z"), ("x", "core")
    split = Mesh(mesh.devices.reshape(N_Y, N_Z, N_X, N_CORE), tm + chan)
    placed = (P(tm, chan), P(chan, None), P(chan), P(), P(), P(), P())
    return jax.shard_map(
        local,
        mesh=split,
        in_specs=placed,
        out_specs=(P(tm, None), P(chan, None), P(chan), P()),
        check_vma=False,
    )
```

```python
import functools
import math

import jax
import jax.numpy as jnp
import numpy as np
from jax import lax
from jax.experimental import pallas as pl
from jax.experimental.pallas import tpu as pltpu
from jax.sharding import Mesh, PartitionSpec as P

N_Y, N_Z, N_X, N_CORE = 4, 8, 4, 2
BLOCKS = N_Y * N_Z
SUB = 8
F32, BF16 = jnp.float32, jnp.bfloat16
KERNELS = True


class Late:
    def __init__(self, buffer, copies):
        self.buffer, self.copies, self.shape = buffer, copies, buffer.shape

    def wait(self, slots):
        for slot in slots:
            if self.copies[slot] is not None:
                self.copies[slot].wait()
                self.copies[slot] = None

    def __getitem__(self, key):
        if isinstance(key, int) and len(self.copies) > 1:
            self.wait([key])
        else:
            self.wait(range(len(self.copies)))
        return self.buffer[key]


def levels_of(shape):
    return shape[0] if len(shape) == 3 and shape[1] == shape[2] else 1


def start_order(shapes, falling):
    order, i = [], 0
    while i < len(shapes):
        count, j = levels_of(shapes[i]), i + 1
        while count > 1 and j < len(shapes) and levels_of(shapes[j]) == count:
            j += 1
        for level in reversed(range(count)) if i in falling else range(count):
            order += [(k, level) for k in range(i, j)]
        i = j
    return order


def call(body, outs, *args, fast=(), keep=(), falling=(), limit=40):
    if not KERNELS:
        results = [jnp.zeros(shape, dtype) for shape, dtype in outs]
        for i, place, value in body(*args):
            if place is None:
                results[i] = value
            elif isinstance(place, int):
                results[i] = results[i].at[place].set(value)
            else:
                results[i] = results[i].at[place[0] : place[0] + place[1]].set(value)
        return results

    late = [i for i in range(len(args)) if i not in fast]
    shapes = [args[i].shape for i in late]
    sent = [i for i in range(len(outs)) if i not in keep]

    def kernel(*refs):
        in_refs = refs[: len(args)]
        out_refs = refs[len(args) : len(args) + len(outs)]
        rest = refs[len(args) + len(outs) :]
        in_buffers = rest[: len(late)]
        out_buffers = dict(zip(sent, rest[len(late) : -2]))
        in_sems, out_sems = rest[-2:]
        copies = [[None] * levels_of(shape) for shape in shapes]
        for number, (i, level) in enumerate(start_order(shapes, [late.index(f) for f in falling])):
            source, buffer = in_refs[late[i]], in_buffers[i]
            if len(copies[i]) > 1:
                source, buffer = source.at[level], buffer.at[level]
            copies[i][level] = pltpu.make_async_copy(source, buffer, in_sems.at[number])
            copies[i][level].start()
        values = list(in_refs)
        for i, buffer, made in zip(late, in_buffers, copies):
            values[i] = Late(buffer, made)
        leaving = []
        for i, place, value in body(*values):
            index = Ellipsis if place is None else place
            if isinstance(place, tuple):
                index = pl.ds(place[0], place[1])
            if i in keep:
                out_refs[i][index] = value
                continue
            out_buffers[i][index] = value
            source, target = out_buffers[i], out_refs[i]
            if place is not None:
                source, target = source.at[index], target.at[index]
            leaving.append(pltpu.make_async_copy(source, target, out_sems.at[len(leaving)]))
            leaving[-1].start()
        for i in late:
            values[i].wait(range(len(values[i].copies)))
        for copy in leaving:
            copy.wait()

    args = [
        pltpu.with_memory_space_constraint(arg, pltpu.VMEM) if i in fast else arg
        for i, arg in enumerate(args)
    ]
    vmem, plain = pl.BlockSpec(memory_space=pltpu.VMEM), pl.BlockSpec(memory_space=pl.ANY)
    return pl.pallas_call(
        kernel,
        out_shape=[
            pltpu.VMEM(shape, dtype) if i in keep else jax.ShapeDtypeStruct(shape, dtype)
            for i, (shape, dtype) in enumerate(outs)
        ],
        in_specs=[vmem if i in fast else plain for i in range(len(args))],
        out_specs=[vmem if i in keep else plain for i in range(len(outs))],
        scratch_shapes=[pltpu.VMEM(args[i].shape, args[i].dtype) for i in late]
        + [pltpu.VMEM(*outs[i]) for i in sent]
        + [
            pltpu.SemaphoreType.DMA((max(1, sum(map(levels_of, shapes))),)),
            pltpu.SemaphoreType.DMA((100,)),
        ],
        compiler_params=pltpu.CompilerParams(vmem_limit_bytes=limit * 2**20),
        name=body.__name__,
    )(*args)


def roll(rows, by):
    if KERNELS:
        return pltpu.roll(rows, by % rows.shape[0], 0)
    return jnp.roll(rows, by, 0)


def roll_lanes(rows, by):
    if KERNELS:
        return pltpu.roll(rows, by, 1)
    return jnp.roll(rows, by, 1)


def row_index(rows):
    return lax.broadcasted_iota(jnp.int32, rows.shape, 0)


def dot(left, right, dims=((1,), (0,))):
    return lax.dot_general(left, right, (dims, ((), ())), preferred_element_type=F32)


def dot_full(left, right):
    return jnp.dot(left, right, precision=lax.Precision.HIGHEST, preferred_element_type=F32)


def cut(value):
    high = value.astype(BF16)
    return high, (value - high.astype(F32)).astype(BF16)


def mul(rows, high, low):
    rows_high, rows_low = cut(rows)
    return dot(rows_high, high) + (dot(rows_low, high) + dot(rows_high, low))


def put(first, place, value):
    high, low = cut(value)
    yield first, place, high
    yield first + 1, place, low


def small_powers(transition, info_gain, smoother_gain, smoother_input):
    a, g = transition[...].T, smoother_input[...].T
    b, k = smoother_gain[...].T, info_gain[...].T
    ag = dot_full(a, g)
    m = dot_full(ag, b)
    for level in range(8):
        yield from put(2, level, a)
        yield from put(4, level, b)
        yield from put(6, level, m)
        n = mul(a, *cut(m))
        m = m + mul(n, *cut(b))
        a, b = dot_full(a, a), dot_full(b, b)
        yield from put(8, level, n)
        if level == 0:
            kg = dot_full(k, g)
            for i, value in enumerate([k, kg, dot_full(kg, smoother_gain[...].T), ag, g]):
                yield from put(0, i, value)
    yield 10, None, a
    yield 11, None, b
    yield 12, None, m


def big_powers(a, b, m):
    yield from put(4, None, m[...])
    a, b = a[...], b[...]
    for level in range(5):
        if level:
            a, b = dot_full(a, a), dot_full(b, b)
        yield from put(0, level, a)
        yield from put(2, level, b)


def information_part(order, noise_precision, emission, observations):
    scale = jnp.broadcast_to(noise_precision[...], (128, noise_precision.shape[1])).T
    scale = jnp.concatenate([scale] * (emission.shape[1] // 128), axis=1)
    weighted = (emission[...].astype(F32) * scale).astype(BF16)
    rows = dot(order[...], observations[...]).astype(BF16)
    information = dot(rows, weighted)
    half = rows.shape[0] // 2
    first = lax.axis_index("core") == 0
    yield 1, None, jnp.where(first, information[half:], information[:half])
    yield 0, None, jnp.where(first, information[:half], information[half:])


def chosen(number, values):
    out = values[0]
    for i in range(1, len(values)):
        out = jnp.where(number == i, values[i], out)
    return out


def channel_slices(order, observations, emission):
    y = lax.axis_index("y")
    rows = dot(order[...], observations[...])
    width = rows.shape[1] // N_Y
    parts = [rows[:, i * width : (i + 1) * width] for i in range(N_Y)]
    for by in (1, 2, 3, 0):
        yield by, None, chosen(y, [parts[(i + by) % N_Y] for i in range(N_Y)])
    emission = emission[...].astype(F32)
    emission = chosen(y, [emission[i * width : (i + 1) * width] for i in range(N_Y)])
    yield 4, None, emission.astype(BF16)


def up_sweep(lead, a_cut, b_cut, m_cut, information):
    lead_high, lead_low = lead
    drive = mul(information, lead_high[0], lead_low[0])
    shown = mul(information, lead_high[1], lead_low[1])
    end = drive
    start = mul(information, lead_high[2], lead_low[2])
    ends, follows = [], []
    for level in range(5):
        half = end.shape[0] // 2
        first, second = end[:half], end[half:]
        follow = start[half:] + mul(first, m_cut[0][level], m_cut[1][level])
        ends.append(first)
        follows.append(follow)
        start = start[:half] + mul(follow, b_cut[0][level], b_cut[1][level])
        end = second + mul(first, a_cut[0][level], a_cut[1][level])
    return shown, end, start, ends, follows


def sub_sweep(a_cut, b_cut, m_cut, end, start):
    ends, follows = [], []
    for level in range(5, 8):
        by = 2 ** (level - 5)
        follow = roll(start, -by) + mul(end, m_cut[0][level], m_cut[1][level])
        ends.append(end)
        follows.append(follow)
        start = start + mul(follow, b_cut[0][level], b_cut[1][level])
        end = mul(end, a_cut[0][level], a_cut[1][level]) + roll(end, -by)
    return end, start, ends, follows


def block_ends(total, theirs, lead_h, lead_l, m_h, m_l, b_h, b_l, a_h, a_l):
    first = lax.axis_index("core") == 0
    total, theirs = total[...], theirs[...]
    information = jnp.concatenate(
        [jnp.where(first, total, theirs), jnp.where(first, theirs, total)], axis=0
    )
    yield 0, None, information
    a_cut, b_cut, m_cut = (a_h, a_l), (b_h, b_l), (m_h, m_l)
    _, end, start, _, _ = up_sweep((lead_h, lead_l), a_cut, b_cut, m_cut, information)
    end, start, _, _ = sub_sweep(a_cut, b_cut, m_cut, end, start)
    pair = jnp.concatenate([end[None, :1], start[None, :1]], axis=1)
    yield 1, None, jnp.broadcast_to(pair, (BLOCKS, 2, end.shape[1]))


def spread_first(rows, by):
    rows = jnp.where(row_index(rows) % (2 * by) == 0, rows, 0.0)
    step = 1
    while step < 2 * by:
        rows = rows + roll(rows, step)
        step *= 2
    return rows


def joined(pieces):
    width = pieces[0].shape[1]
    return jnp.concatenate(
        [piece[...].reshape(-1, 1, SUB, width) for piece in pieces], axis=1
    ).reshape(-1, width)


def block_trees(
    i0, i1, i2, i3, lead_h, lead_l, m_h, m_l, b_h, b_l, a_h, a_l, o0, o1, o2, o3
):
    a_cut, b_cut, m_cut = (a_h, a_l), (b_h, b_l), (m_h, m_l)
    information = joined([i0, i1, i2, i3])
    shown, end, start, ends, follows = up_sweep(
        (lead_h, lead_l), a_cut, b_cut, m_cut, information
    )
    yield 0, None, shown
    at = 0
    for i in range(5):
        yield 1, (at, ends[i].shape[0]), ends[i]
        yield 2, (at, ends[i].shape[0]), follows[i]
        at += ends[i].shape[0]
    _, _, sub_ends, sub_follows = sub_sweep(a_cut, b_cut, m_cut, end, start)
    count = end.shape[0]
    for i in range(3):
        yield 3, (i * count, count), spread_first(sub_ends[i], 2**i)
        yield 4, (i * count, count), spread_first(sub_follows[i], 2**i)
    yield 5, None, joined([o0, o1, o2, o3]).astype(BF16)


def states_and_sums(
    gathered,
    a_big_h,
    a_big_l,
    lead_h,
    lead_l,
    m_h,
    m_l,
    b_big_h,
    b_big_l,
    sub_ends,
    sub_follows,
    a_h,
    a_l,
    n_h,
    n_l,
    b_h,
    b_l,
    ends,
    follows,
    shown,
    emission,
    observed,
    natural,
):
    block = lax.axis_index("y") * N_Z + lax.axis_index("z")
    width = shown.shape[1]
    gathered = gathered[...]
    after = gathered[:, 0]
    index = row_index(after)
    for level in range(5):
        by = 2**level
        before = jnp.where(index >= by, roll(after, by), 0.0)
        after = after + mul(before, a_big_h[level], a_big_l[level])
    enter = jnp.where(index >= 1, roll(after, 1), 0.0)
    follow = gathered[:, 1] + mul(enter, m_h[...], m_l[...])
    final = after - mul(after, lead_h[4], lead_l[4])
    follow = jnp.where(index < BLOCKS - 1, roll(follow, -1), final)
    for level in range(5):
        by = 2**level
        later = jnp.where(index < BLOCKS - by, roll(follow, -by), 0.0)
        follow = follow + mul(later, b_big_h[level], b_big_l[level])

    place = lax.broadcasted_iota(jnp.int32, (N_Y * SUB, BLOCKS), 0)
    source = lax.broadcasted_iota(jnp.int32, (N_Y * SUB, BLOCKS), 1)
    wanted = block - N_Z * (place // SUB)
    pick = (source == jnp.where(wanted < 0, wanted + BLOCKS, wanted)).astype(BF16)

    def picked(rows):
        high, low = cut(rows)
        return dot(pick, high) + dot(pick, low)

    enter, follow = picked(enter), picked(follow)
    count = N_Y * SUB
    index = row_index(enter)
    for level in (7, 6, 5):
        by = 2 ** (level - 5)
        part = (level - 5) * count
        second = sub_ends[part : part + count] + mul(enter, a_h[level], a_l[level])
        first = (
            sub_follows[part : part + count]
            + mul(enter, n_h[level], n_l[level])
            + mul(follow, b_h[level], b_l[level])
        )
        is_second = (index // by) % 2 == 1
        enter = jnp.where(is_second, second, enter)
        follow = jnp.where(is_second, follow, first)

    bottom = ends.shape[0]
    for level in (4, 3, 2, 1, 0):
        rows = enter.shape[0]
        top, bottom = bottom, bottom - rows
        second = ends[bottom:top] + mul(enter, a_h[level], a_l[level])
        first = (
            follows[bottom:top]
            + mul(enter, n_h[level], n_l[level])
            + mul(follow, b_h[level], b_l[level])
        )
        enter = jnp.concatenate([enter, second], axis=0)
        follow = jnp.concatenate([first, follow], axis=0)
    smoothed = shown[...] + mul(enter, lead_h[3], lead_l[3]) + follow
    observed, emission, natural = observed[...], emission[...], natural[...]

    high, low = cut(smoothed)
    cross = dot(observed, high, ((0,), (0,)))
    predicted = dot(high, emission, ((1,), (1,)))
    error = observed.astype(F32) - predicted
    error = jnp.broadcast_to(jnp.sum(error * error, axis=0, keepdims=True), (8, error.shape[1]))
    crossed = dot(high, jnp.concatenate([high, low], axis=1), ((0,), (0,)))
    moment = crossed[:, :width] + (crossed[:, width:] + crossed[:, width:].T)

    channels = cross.shape[0]
    share, line = width // N_Y, channels // N_Z
    y = block // N_Z
    mine = chosen(y, [moment[i * share : (i + 1) * share] for i in range(N_Y)])
    free = share * jnp.where(y == N_Y - 1, 0, y + 1)
    lane = lax.broadcasted_iota(jnp.int32, (8, width), 1)
    row = lax.broadcasted_iota(jnp.int32, (8, width), 0)
    is_free = (lane >= free) & (lane < free + share)
    is_error = (lane >= free) & (lane < free + line) & (row == 0)
    chunks = []
    for z in range(N_Z):
        turned = roll_lanes(error, free + (width - line * z))
        tile = jnp.where(is_free, 0.0, mine[8 * z : 8 * z + 8])
        chunks.append(jnp.where(is_error, turned, tile))
    yield 1, None, jnp.concatenate([cross.reshape(N_Z, line, width), jnp.stack(chunks)], axis=1)

    own = smoothed.reshape(-1, N_Y, SUB, width)[:, 0].reshape(-1, width)
    high, rest = own.astype(BF16), own
    out = dot(natural, high)
    for _ in range(2):
        rest = rest - high.astype(F32)
        high = rest.astype(BF16)
        out = out + dot(natural, high)
    yield 0, None, out


def add_pieces(pieces):
    total = pieces[0]
    for i in range(1, N_Z):
        total = total + pieces[i]
    yield 0, None, jnp.broadcast_to(total[None], (N_Z,) + total.shape)


def assemble(bins, *sums):
    place = lax.axis_index("y")
    sums = [part[...] for part in sums]
    width = sums[0].shape[2]
    share = width // N_Y
    line = sums[0].shape[1] - 8
    lane = lax.broadcasted_iota(jnp.int32, (8, width), 1)
    cross, moment, errors = [], [], []
    for y in range(N_Y):
        whole = chosen(place, [sums[(i - y) % N_Y] for i in range(N_Y)])
        cross.append(whole[:, :line].reshape(-1, width) * (1.0 / math.sqrt(bins)))
        moment.append(whole[:, line:].reshape(-1, width))
        error = jnp.zeros((8, width), F32)
        for z in range(N_Z):
            turned = roll_lanes(whole[z, line:], (line * z - share * ((y + 1) % N_Y)) % width)
            error = jnp.where((lane >= line * z) & (lane < line * z + line), turned, error)
        errors.append(error[:1] * (1.0 / bins))
    moment = jnp.concatenate(moment, axis=0)
    row = lax.broadcasted_iota(jnp.int32, moment.shape, 0) // share
    column = lax.broadcasted_iota(jnp.int32, moment.shape, 1) // share
    free = column == jnp.where(row == N_Y - 1, 0, row + 1)
    moment = jnp.where(free, moment.T, moment) * (1.0 / bins)
    yield 0, None, jnp.concatenate(cross, axis=0)
    yield 1, None, moment
    yield 2, None, jnp.concatenate(errors, axis=1)


def shift(value, axis, count, by):
    return lax.ppermute(value, axis, [(i, (i + by) % count) for i in range(count)])


def bit_reversed(count):
    bits = count.bit_length() - 1
    return [int(format(i, "0%db" % bits)[::-1], 2) for i in range(count)]


def row_order(bins):
    length = bins // SUB
    times = np.array([[j * length + t for j in range(SUB)] for t in bit_reversed(length)])
    return np.eye(bins, dtype=np.float32)[times.reshape(-1)]


def local(
    observations, emission, noise_precision, transition, info_gain, smoother_gain, smoother_input
):
    bins, channels = observations.shape
    width = transition.shape[0]
    order = jnp.asarray(row_order(bins), BF16)
    natural = jnp.asarray(row_order(bins).T, BF16)

    mine, other = call(
        information_part,
        [((bins // 2, width), F32)] * 2,
        order,
        noise_precision.reshape(1, channels),
        emission,
        observations,
        keep=(0, 1),
    )
    mine = mine + shift(other, "core", N_CORE, 1)
    mine, later = lax.optimization_barrier((mine, observations))
    moved = [shift(mine, "x", N_X, by) for by in (2, 1, 3)]

    part = channels // N_Y
    *slices, emission_part = call(
        channel_slices,
        [((bins, part), F32)] * N_Y + [((part, width), BF16)],
        order,
        later,
        emission,
        keep=(1, 2, 3),
    )
    observed = slices[:1] + [shift(slices[by], "y", N_Y, by) for by in (1, 2, 3)]

    square = (width, width)
    stack = lambda n: [((n,) + square, BF16)] * 2
    small = call(
        small_powers,
        stack(5) + stack(8) * 4 + [(square, F32)] * 3,
        transition,
        info_gain,
        smoother_gain,
        smoother_input,
    )
    lead, a_cut, b_cut, m_cut, n_cut = (small[i : i + 2] for i in range(0, 10, 2))

    total = mine + moved[0] + moved[1] + moved[2]
    theirs = shift(total, "core", N_CORE, 1)
    information, ends = call(
        block_ends,
        [((bins, width), F32), ((BLOCKS, 2, width), F32)],
        total,
        theirs,
        *lead,
        *m_cut,
        *b_cut,
        *a_cut,
        fast=(0, 1),
    )
    gathered = lax.all_to_all(ends, ("y", "z"), 0, 0)
    informations = [information] + [shift(information, "y", N_Y, by) for by in (1, 2, 3)]
    big = call(big_powers, stack(5) * 2 + [(square, BF16)] * 2, *small[10:])
    tree_rows = N_Y * SUB * 31
    shown, tree_ends, follows, sub_ends, sub_follows, seen = call(
        block_trees,
        [
            ((N_Y * bins, width), F32),
            ((tree_rows, width), F32),
            ((tree_rows, width), F32),
            ((3 * N_Y * SUB, width), F32),
            ((3 * N_Y * SUB, width), F32),
            ((N_Y * bins, part), BF16),
        ],
        *informations,
        *lead,
        *m_cut,
        *b_cut,
        *a_cut,
        *observed,
    )
    rows = channels // (N_Y * N_Z) + 8
    smoothed, payload = call(
        states_and_sums,
        [((bins, width), F32), ((N_Z, rows, width), F32)],
        gathered,
        *big[:2],
        *lead,
        *big[4:],
        *big[2:4],
        sub_ends,
        sub_follows,
        *a_cut,
        *n_cut,
        *b_cut,
        tree_ends,
        follows,
        shown,
        emission_part,
        seen,
        natural,
        falling=(11,),
        fast=(0,),
    )
    payload = lax.all_to_all(payload, "z", 0, 0)
    (spread,) = call(add_pieces, [((N_Z, rows, width), F32)], payload, fast=(0,))
    whole = lax.all_to_all(spread, "z", 0, 0)
    far, near, back = (shift(whole, "y", N_Y, by) for by in (2, 1, 3))
    cross, moment, error = call(
        functools.wraps(assemble)(functools.partial(assemble, bins * BLOCKS)),
        [((channels, width), F32), (square, F32), ((1, channels), F32)],
        whole,
        near,
        far,
        back,
        fast=(0, 1, 2, 3),
    )
    return smoothed, cross, error.reshape(channels), moment


def solution(mesh):
    tm, chan = ("y", "z"), ("x", "core")
    split = Mesh(mesh.devices.reshape(N_Y, N_Z, N_X, N_CORE), tm + chan)
    placed = (P(tm, chan), P(chan, None), P(chan), P(), P(), P(), P())
    return jax.shard_map(
        local,
        mesh=split,
        in_specs=placed,
        out_specs=(P(tm, None), P(chan, None), P(chan), P()),
        check_vma=False,
    )
```

```python
import functools
import math

import jax
import jax.numpy as jnp
import numpy as np
from jax import lax
from jax.experimental import pallas as pl
from jax.experimental.pallas import tpu as pltpu
from jax.sharding import Mesh, PartitionSpec as P

N_Y, N_Z, N_X, N_CORE = 4, 8, 4, 2
BLOCKS = N_Y * N_Z
SUB = 8
F32, BF16 = jnp.float32, jnp.bfloat16
KERNELS = True


class Late:
    def __init__(self, buffer, copies):
        self.buffer, self.copies, self.shape = buffer, copies, buffer.shape

    def __getitem__(self, key):
        while self.copies:
            self.copies.pop().wait()
        return self.buffer[key]


def pieces_of(shape):
    count = 4 if shape[0] >= 256 else 1
    return [(i * (shape[0] // count), shape[0] // count) for i in range(count)]


def call(body, outs, *args, large=(), sent=(), limit=16):
    if not KERNELS:
        results = [jnp.zeros(shape, dtype) for shape, dtype in outs]
        for i, place, value in body(*args):
            if place is None:
                results[i] = value
            elif isinstance(place, int):
                results[i] = results[i].at[place].set(value)
            else:
                results[i] = results[i].at[place[0] : place[0] + place[1]].set(value)
        return results

    n_in, n_out = len(args), len(outs)

    def kernel(*refs):
        values, out_refs, rest = list(refs[:n_in]), refs[n_in : n_in + n_out], refs[n_in + n_out :]
        targets = dict(zip(sent, rest[len(large) : -2]))
        in_sems, out_sems = rest[-2:]
        number = 0
        for i, buffer in zip(large, rest[: len(large)]):
            copies = []
            for start, size in pieces_of(buffer.shape):
                rows = pl.ds(start, size)
                copies.append(
                    pltpu.make_async_copy(refs[i].at[rows], buffer.at[rows], in_sems.at[number])
                )
                copies[-1].start()
                number += 1
            values[i] = Late(buffer, copies)
        leaving = []
        for i, place, value in body(*values):
            index = Ellipsis if place is None else place
            if isinstance(place, tuple):
                index = pl.ds(place[0], place[1])
            if i not in sent:
                out_refs[i][index] = value
                continue
            buffer = targets[i]
            buffer[index] = value
            spans = pieces_of(value.shape) if place is None else [place]
            for start, size in spans:
                rows = pl.ds(start, size)
                leaving.append(
                    pltpu.make_async_copy(
                        buffer.at[rows], out_refs[i].at[rows], out_sems.at[len(leaving)]
                    )
                )
                leaving[-1].start()
        for copy in leaving:
            copy.wait()

    args = [
        pltpu.with_memory_space_constraint(arg, pltpu.HBM if i in large else pltpu.VMEM)
        for i, arg in enumerate(args)
    ]
    vmem, far = pl.BlockSpec(memory_space=pltpu.VMEM), pl.BlockSpec(memory_space=pltpu.HBM)
    return pl.pallas_call(
        kernel,
        out_shape=[(pltpu.HBM if i in sent else pltpu.VMEM)(*kind) for i, kind in enumerate(outs)],
        in_specs=[far if i in large else vmem for i in range(n_in)],
        out_specs=[far if i in sent else vmem for i in range(n_out)],
        scratch_shapes=[pltpu.VMEM(args[i].shape, args[i].dtype) for i in large]
        + [pltpu.VMEM(*outs[i]) for i in sent]
        + [pltpu.SemaphoreType.DMA((32,)), pltpu.SemaphoreType.DMA((32,))],
        compiler_params=pltpu.CompilerParams(vmem_limit_bytes=limit * 2**20),
        name=body.__name__,
    )(*args)


def roll(rows, by):
    if KERNELS:
        return pltpu.roll(rows, by % rows.shape[0], 0)
    return jnp.roll(rows, by, 0)


def roll_lanes(rows, by):
    if KERNELS:
        return pltpu.roll(rows, by, 1)
    return jnp.roll(rows, by, 1)


def row_index(rows):
    return lax.broadcasted_iota(jnp.int32, rows.shape, 0)


def dot(left, right, dims=((1,), (0,))):
    return lax.dot_general(left, right, (dims, ((), ())), preferred_element_type=F32)


def dot_full(left, right):
    return jnp.dot(left, right, precision=lax.Precision.HIGHEST, preferred_element_type=F32)


def cut(value):
    high = value.astype(BF16)
    return high, (value - high.astype(F32)).astype(BF16)


def mul(rows, high, low):
    rows_high, rows_low = cut(rows)
    return dot(rows_high, high) + (dot(rows_low, high) + dot(rows_high, low))


def put(first, place, value):
    high, low = cut(value)
    yield first, place, high
    yield first + 1, place, low


def small_powers(transition, info_gain, smoother_gain, smoother_input):
    a, g = transition[...].T, smoother_input[...].T
    b, k = smoother_gain[...].T, info_gain[...].T
    ag = dot_full(a, g)
    m = dot_full(ag, b)
    for level in range(8):
        yield from put(2, level, a)
        yield from put(4, level, b)
        yield from put(6, level, m)
        n = mul(a, *cut(m))
        m = m + mul(n, *cut(b))
        a, b = dot_full(a, a), dot_full(b, b)
        yield from put(8, level, n)
        if level == 0:
            kg = dot_full(k, g)
            for i, value in enumerate([k, kg, dot_full(kg, smoother_gain[...].T), ag, g]):
                yield from put(0, i, value)
    yield 10, None, a
    yield 11, None, b
    yield 12, None, m


def big_powers(a, b, m):
    yield from put(4, None, m[...])
    a, b = a[...], b[...]
    for level in range(5):
        if level:
            a, b = dot_full(a, a), dot_full(b, b)
        yield from put(0, level, a)
        yield from put(2, level, b)


def information_part(order, noise_precision, emission, observations):
    scale = jnp.broadcast_to(noise_precision[...], (128, noise_precision.shape[1])).T
    scale = jnp.concatenate([scale] * (emission.shape[1] // 128), axis=1)
    weighted = (emission[...].astype(F32) * scale).astype(BF16)
    rows = dot(order[...], observations[...]).astype(BF16)
    information = dot(rows, weighted)
    half = rows.shape[0] // 2
    first = lax.axis_index("core") == 0
    yield 1, None, jnp.where(first, information[half:], information[:half])
    yield 0, None, jnp.where(first, information[:half], information[half:])


def chosen(number, values):
    out = values[0]
    for i in range(1, len(values)):
        out = jnp.where(number == i, values[i], out)
    return out


def channel_slices(order, observations, emission):
    y = lax.axis_index("y")
    rows = dot(order[...], observations[...])
    width = rows.shape[1] // N_Y
    parts = [rows[:, i * width : (i + 1) * width] for i in range(N_Y)]
    for by in (1, 2, 3, 0):
        yield by, None, chosen(y, [parts[(i + by) % N_Y] for i in range(N_Y)])
    emission = emission[...].astype(F32)
    emission = chosen(y, [emission[i * width : (i + 1) * width] for i in range(N_Y)])
    yield 4, None, emission.astype(BF16)


def up_sweep(lead, a_cut, b_cut, m_cut, information):
    lead_high, lead_low = lead
    drive = mul(information, lead_high[0], lead_low[0])
    shown = mul(information, lead_high[1], lead_low[1])
    end = drive
    start = mul(information, lead_high[2], lead_low[2])
    ends, follows = [], []
    for level in range(5):
        half = end.shape[0] // 2
        first, second = end[:half], end[half:]
        follow = start[half:] + mul(first, m_cut[0][level], m_cut[1][level])
        ends.append(first)
        follows.append(follow)
        start = start[:half] + mul(follow, b_cut[0][level], b_cut[1][level])
        end = second + mul(first, a_cut[0][level], a_cut[1][level])
    return shown, end, start, ends, follows


def sub_sweep(a_cut, b_cut, m_cut, end, start):
    ends, follows = [], []
    for level in range(5, 8):
        by = 2 ** (level - 5)
        follow = roll(start, -by) + mul(end, m_cut[0][level], m_cut[1][level])
        ends.append(end)
        follows.append(follow)
        start = start + mul(follow, b_cut[0][level], b_cut[1][level])
        end = mul(end, a_cut[0][level], a_cut[1][level]) + roll(end, -by)
    return end, start, ends, follows


def block_ends(total, theirs, lead_h, lead_l, m_h, m_l, b_h, b_l, a_h, a_l):
    first = lax.axis_index("core") == 0
    total, theirs = total[...], theirs[...]
    information = jnp.concatenate(
        [jnp.where(first, total, theirs), jnp.where(first, theirs, total)], axis=0
    )
    yield 0, None, information
    a_cut, b_cut, m_cut = (a_h, a_l), (b_h, b_l), (m_h, m_l)
    _, end, start, _, _ = up_sweep((lead_h, lead_l), a_cut, b_cut, m_cut, information)
    end, start, _, _ = sub_sweep(a_cut, b_cut, m_cut, end, start)
    pair = jnp.concatenate([end[None, :1], start[None, :1]], axis=1)
    yield 1, None, jnp.broadcast_to(pair, (BLOCKS, 2, end.shape[1]))


def spread_first(rows, by):
    rows = jnp.where(row_index(rows) % (2 * by) == 0, rows, 0.0)
    step = 1
    while step < 2 * by:
        rows = rows + roll(rows, step)
        step *= 2
    return rows


def joined(pieces):
    width = pieces[0].shape[1]
    return jnp.concatenate(
        [piece[...].reshape(-1, 1, SUB, width) for piece in pieces], axis=1
    ).reshape(-1, width)


def block_trees(
    i0, i1, i2, i3, lead_h, lead_l, m_h, m_l, b_h, b_l, a_h, a_l, o0, o1, o2, o3
):
    a_cut, b_cut, m_cut = (a_h, a_l), (b_h, b_l), (m_h, m_l)
    information = joined([i0, i1, i2, i3])
    shown, end, start, ends, follows = up_sweep(
        (lead_h, lead_l), a_cut, b_cut, m_cut, information
    )
    yield 0, None, shown
    at = 0
    for i in range(5):
        yield 1, (at, ends[i].shape[0]), ends[i]
        yield 2, (at, ends[i].shape[0]), follows[i]
        at += ends[i].shape[0]
    _, _, sub_ends, sub_follows = sub_sweep(a_cut, b_cut, m_cut, end, start)
    count = end.shape[0]
    for i in range(3):
        yield 3, (i * count, count), spread_first(sub_ends[i], 2**i)
        yield 4, (i * count, count), spread_first(sub_follows[i], 2**i)
    yield 5, None, joined([o0, o1, o2, o3]).astype(BF16)


def states_and_sums(
    gathered,
    a_big_h,
    a_big_l,
    lead_h,
    lead_l,
    m_h,
    m_l,
    b_big_h,
    b_big_l,
    sub_ends,
    sub_follows,
    a_h,
    a_l,
    n_h,
    n_l,
    b_h,
    b_l,
    ends,
    follows,
    shown,
    emission,
    observed,
    natural,
):
    block = lax.axis_index("y") * N_Z + lax.axis_index("z")
    width = shown.shape[1]
    gathered = gathered[...]
    after = gathered[:, 0]
    index = row_index(after)
    for level in range(5):
        by = 2**level
        before = jnp.where(index >= by, roll(after, by), 0.0)
        after = after + mul(before, a_big_h[level], a_big_l[level])
    enter = jnp.where(index >= 1, roll(after, 1), 0.0)
    follow = gathered[:, 1] + mul(enter, m_h[...], m_l[...])
    final = after - mul(after, lead_h[4], lead_l[4])
    follow = jnp.where(index < BLOCKS - 1, roll(follow, -1), final)
    for level in range(5):
        by = 2**level
        later = jnp.where(index < BLOCKS - by, roll(follow, -by), 0.0)
        follow = follow + mul(later, b_big_h[level], b_big_l[level])

    place = lax.broadcasted_iota(jnp.int32, (N_Y * SUB, BLOCKS), 0)
    source = lax.broadcasted_iota(jnp.int32, (N_Y * SUB, BLOCKS), 1)
    wanted = block - N_Z * (place // SUB)
    pick = (source == jnp.where(wanted < 0, wanted + BLOCKS, wanted)).astype(BF16)

    def picked(rows):
        high, low = cut(rows)
        return dot(pick, high) + dot(pick, low)

    enter, follow = picked(enter), picked(follow)
    count = N_Y * SUB
    index = row_index(enter)
    for level in (7, 6, 5):
        by = 2 ** (level - 5)
        part = (level - 5) * count
        second = sub_ends[part : part + count] + mul(enter, a_h[level], a_l[level])
        first = (
            sub_follows[part : part + count]
            + mul(enter, n_h[level], n_l[level])
            + mul(follow, b_h[level], b_l[level])
        )
        is_second = (index // by) % 2 == 1
        enter = jnp.where(is_second, second, enter)
        follow = jnp.where(is_second, follow, first)

    bottom = ends.shape[0]
    for level in (4, 3, 2, 1, 0):
        rows = enter.shape[0]
        top, bottom = bottom, bottom - rows
        second = ends[bottom:top] + mul(enter, a_h[level], a_l[level])
        first = (
            follows[bottom:top]
            + mul(enter, n_h[level], n_l[level])
            + mul(follow, b_h[level], b_l[level])
        )
        enter = jnp.concatenate([enter, second], axis=0)
        follow = jnp.concatenate([first, follow], axis=0)
    smoothed = shown[...] + mul(enter, lead_h[3], lead_l[3]) + follow
    observed, emission, natural = observed[...], emission[...], natural[...]

    high, low = cut(smoothed)
    cross = dot(observed, high, ((0,), (0,)))
    predicted = dot(high, emission, ((1,), (1,)))
    error = observed.astype(F32) - predicted
    error = jnp.broadcast_to(jnp.sum(error * error, axis=0, keepdims=True), (8, error.shape[1]))
    crossed = dot(high, jnp.concatenate([high, low], axis=1), ((0,), (0,)))
    moment = crossed[:, :width] + (crossed[:, width:] + crossed[:, width:].T)

    channels = cross.shape[0]
    share, line = width // N_Y, channels // N_Z
    y = block // N_Z
    mine = chosen(y, [moment[i * share : (i + 1) * share] for i in range(N_Y)])
    free = share * jnp.where(y == N_Y - 1, 0, y + 1)
    lane = lax.broadcasted_iota(jnp.int32, (8, width), 1)
    row = lax.broadcasted_iota(jnp.int32, (8, width), 0)
    is_free = (lane >= free) & (lane < free + share)
    is_error = (lane >= free) & (lane < free + line) & (row == 0)
    chunks = []
    for z in range(N_Z):
        turned = roll_lanes(error, free + (width - line * z))
        tile = jnp.where(is_free, 0.0, mine[8 * z : 8 * z + 8])
        chunks.append(jnp.where(is_error, turned, tile))
    yield 1, None, jnp.concatenate([cross.reshape(N_Z, line, width), jnp.stack(chunks)], axis=1)

    own = smoothed.reshape(-1, N_Y, SUB, width)[:, 0].reshape(-1, width)
    high, rest = own.astype(BF16), own
    out = dot(natural, high)
    for _ in range(2):
        rest = rest - high.astype(F32)
        high = rest.astype(BF16)
        out = out + dot(natural, high)
    yield 0, None, out


def add_pieces(pieces):
    total = pieces[0]
    for i in range(1, N_Z):
        total = total + pieces[i]
    yield 0, None, jnp.broadcast_to(total[None], (N_Z,) + total.shape)


def assemble(bins, *sums):
    place = lax.axis_index("y")
    sums = [part[...] for part in sums]
    width = sums[0].shape[2]
    share = width // N_Y
    line = sums[0].shape[1] - 8
    lane = lax.broadcasted_iota(jnp.int32, (8, width), 1)
    cross, moment, errors = [], [], []
    for y in range(N_Y):
        whole = chosen(place, [sums[(i - y) % N_Y] for i in range(N_Y)])
        cross.append(whole[:, :line].reshape(-1, width) * (1.0 / math.sqrt(bins)))
        moment.append(whole[:, line:].reshape(-1, width))
        error = jnp.zeros((8, width), F32)
        for z in range(N_Z):
            turned = roll_lanes(whole[z, line:], (line * z - share * ((y + 1) % N_Y)) % width)
            error = jnp.where((lane >= line * z) & (lane < line * z + line), turned, error)
        errors.append(error[:1] * (1.0 / bins))
    moment = jnp.concatenate(moment, axis=0)
    row = lax.broadcasted_iota(jnp.int32, moment.shape, 0) // share
    column = lax.broadcasted_iota(jnp.int32, moment.shape, 1) // share
    free = column == jnp.where(row == N_Y - 1, 0, row + 1)
    moment = jnp.where(free, moment.T, moment) * (1.0 / bins)
    yield 0, None, jnp.concatenate(cross, axis=0)
    yield 1, None, moment
    yield 2, None, jnp.concatenate(errors, axis=1)


def shift(value, axis, count, by):
    return lax.ppermute(value, axis, [(i, (i + by) % count) for i in range(count)])


def bit_reversed(count):
    bits = count.bit_length() - 1
    return [int(format(i, "0%db" % bits)[::-1], 2) for i in range(count)]


def row_order(bins):
    length = bins // SUB
    times = np.array([[j * length + t for j in range(SUB)] for t in bit_reversed(length)])
    return np.eye(bins, dtype=np.float32)[times.reshape(-1)]


def local(
    observations, emission, noise_precision, transition, info_gain, smoother_gain, smoother_input
):
    bins, channels = observations.shape
    width = transition.shape[0]
    order = jnp.asarray(row_order(bins), BF16)
    natural = jnp.asarray(row_order(bins).T, BF16)

    mine, other = call(
        information_part,
        [((bins // 2, width), F32)] * 2,
        order,
        noise_precision.reshape(1, channels),
        emission,
        observations,
        large=(0, 1, 2, 3),
    )
    mine = mine + shift(other, "core", N_CORE, 1)
    mine, later = lax.optimization_barrier((mine, observations))
    moved = [shift(mine, "x", N_X, by) for by in (2, 1, 3)]

    part = channels // N_Y
    *slices, emission_part = call(
        channel_slices,
        [((bins, part), F32)] * N_Y + [((part, width), BF16)],
        order,
        later,
        emission,
    )
    observed = slices[:1] + [shift(slices[by], "y", N_Y, by) for by in (1, 2, 3)]

    square = (width, width)
    stack = lambda n: [((n,) + square, BF16)] * 2
    small = call(
        small_powers,
        stack(5) + stack(8) * 4 + [(square, F32)] * 3,
        transition,
        info_gain,
        smoother_gain,
        smoother_input,
    )
    lead, a_cut, b_cut, m_cut, n_cut = (small[i : i + 2] for i in range(0, 10, 2))

    total = mine + moved[0] + moved[1] + moved[2]
    theirs = shift(total, "core", N_CORE, 1)
    information, ends = call(
        block_ends,
        [((bins, width), F32), ((BLOCKS, 2, width), F32)],
        total,
        theirs,
        *lead,
        *m_cut,
        *b_cut,
        *a_cut,
    )
    ends, observed = lax.optimization_barrier((ends, observed))
    gathered = lax.all_to_all(ends, ("y", "z"), 0, 0)
    gathered, information = lax.optimization_barrier((gathered, information))
    informations = [information] + [shift(information, "y", N_Y, by) for by in (1, 2, 3)]
    big = call(big_powers, stack(5) * 2 + [(square, BF16)] * 2, *small[10:])
    tree_rows = N_Y * SUB * 31
    shown, tree_ends, follows, sub_ends, sub_follows, seen = call(
        block_trees,
        [
            ((N_Y * bins, width), F32),
            ((tree_rows, width), F32),
            ((tree_rows, width), F32),
            ((3 * N_Y * SUB, width), F32),
            ((3 * N_Y * SUB, width), F32),
            ((N_Y * bins, part), BF16),
        ],
        *informations,
        *lead,
        *m_cut,
        *b_cut,
        *a_cut,
        *observed,
    )
    rows = channels // (N_Y * N_Z) + 8
    smoothed, payload = call(
        states_and_sums,
        [((bins, width), F32), ((N_Z, rows, width), F32)],
        gathered,
        *big[:2],
        *lead,
        *big[4:],
        *big[2:4],
        sub_ends,
        sub_follows,
        *a_cut,
        *n_cut,
        *b_cut,
        tree_ends,
        follows,
        shown,
        emission_part,
        seen,
        natural,
    )
    payload = lax.all_to_all(payload, "z", 0, 0)
    (spread,) = call(add_pieces, [((N_Z, rows, width), F32)], payload)
    whole = lax.all_to_all(spread, "z", 0, 0)
    far, near, back = (shift(whole, "y", N_Y, by) for by in (2, 1, 3))
    cross, moment, error = call(
        functools.wraps(assemble)(functools.partial(assemble, bins * BLOCKS)),
        [((channels, width), F32), (square, F32), ((1, channels), F32)],
        whole,
        near,
        far,
        back,
        sent=(0, 1, 2),
    )
    return smoothed, cross, error.reshape(channels), moment


def solution(mesh):
    tm, chan = ("y", "z"), ("x", "core")
    split = Mesh(mesh.devices.reshape(N_Y, N_Z, N_X, N_CORE), tm + chan)
    placed = (P(tm, chan), P(chan, None), P(chan), P(), P(), P(), P())
    return jax.shard_map(
        local,
        mesh=split,
        in_specs=placed,
        out_specs=(P(tm, None), P(chan, None), P(chan), P()),
        check_vma=False,
    )
```

```python
import functools
import math

import jax
import jax.numpy as jnp
import numpy as np
from jax import lax
from jax.experimental import pallas as pl
from jax.experimental.pallas import tpu as pltpu
from jax.sharding import Mesh, PartitionSpec as P

N_Y, N_Z, N_X, N_CORE = 4, 8, 4, 2
BLOCKS = N_Y * N_Z
SUB = 8
F32, BF16 = jnp.float32, jnp.bfloat16
KERNELS = True


class Late:
    def __init__(self, buffer, copies):
        self.buffer, self.copies, self.shape = buffer, copies, buffer.shape

    def __getitem__(self, key):
        while self.copies:
            self.copies.pop().wait()
        return self.buffer[key]


def pieces_of(shape):
    count = 4 if shape[0] >= 256 else 1
    return [(i * (shape[0] // count), shape[0] // count) for i in range(count)]


def call(body, outs, *args, large=(), sent=(), limit=16):
    if not KERNELS:
        results = [jnp.zeros(shape, dtype) for shape, dtype in outs]
        for i, place, value in body(*args):
            if place is None:
                results[i] = value
            elif isinstance(place, int):
                results[i] = results[i].at[place].set(value)
            else:
                results[i] = results[i].at[place[0] : place[0] + place[1]].set(value)
        return results

    n_in, n_out = len(args), len(outs)

    def kernel(*refs):
        values, out_refs, rest = list(refs[:n_in]), refs[n_in : n_in + n_out], refs[n_in + n_out :]
        targets = dict(zip(sent, rest[len(large) : -2]))
        in_sems, out_sems = rest[-2:]
        number = 0
        for i, buffer in zip(large, rest[: len(large)]):
            copies = []
            for start, size in pieces_of(buffer.shape):
                rows = pl.ds(start, size)
                copies.append(
                    pltpu.make_async_copy(refs[i].at[rows], buffer.at[rows], in_sems.at[number])
                )
                copies[-1].start()
                number += 1
            values[i] = Late(buffer, copies)
        leaving = []
        for i, place, value in body(*values):
            index = Ellipsis if place is None else place
            if isinstance(place, tuple):
                index = pl.ds(place[0], place[1])
            if i not in sent:
                out_refs[i][index] = value
                continue
            buffer = targets[i]
            buffer[index] = value
            spans = pieces_of(value.shape) if place is None else [place]
            for start, size in spans:
                rows = pl.ds(start, size)
                leaving.append(
                    pltpu.make_async_copy(
                        buffer.at[rows], out_refs[i].at[rows], out_sems.at[len(leaving)]
                    )
                )
                leaving[-1].start()
        for copy in leaving:
            copy.wait()

    args = [
        pltpu.with_memory_space_constraint(arg, pltpu.HBM if i in large else pltpu.VMEM)
        for i, arg in enumerate(args)
    ]
    vmem, far = pl.BlockSpec(memory_space=pltpu.VMEM), pl.BlockSpec(memory_space=pltpu.HBM)
    return pl.pallas_call(
        kernel,
        out_shape=[(pltpu.HBM if i in sent else pltpu.VMEM)(*kind) for i, kind in enumerate(outs)],
        in_specs=[far if i in large else vmem for i in range(n_in)],
        out_specs=[far if i in sent else vmem for i in range(n_out)],
        scratch_shapes=[pltpu.VMEM(args[i].shape, args[i].dtype) for i in large]
        + [pltpu.VMEM(*outs[i]) for i in sent]
        + [pltpu.SemaphoreType.DMA((32,)), pltpu.SemaphoreType.DMA((32,))],
        compiler_params=pltpu.CompilerParams(vmem_limit_bytes=limit * 2**20),
        name=body.__name__,
    )(*args)


def roll(rows, by):
    if KERNELS:
        return pltpu.roll(rows, by % rows.shape[0], 0)
    return jnp.roll(rows, by, 0)


def roll_lanes(rows, by):
    if KERNELS:
        return pltpu.roll(rows, by, 1)
    return jnp.roll(rows, by, 1)


def row_index(rows):
    return lax.broadcasted_iota(jnp.int32, rows.shape, 0)


def dot(left, right, dims=((1,), (0,))):
    return lax.dot_general(left, right, (dims, ((), ())), preferred_element_type=F32)


def cut(value):
    count = value.shape[0]
    if count < 16:
        value = jnp.concatenate([value, value], axis=0)
    high = value.astype(BF16)
    return high, (value - high.astype(F32)).astype(BF16), count


def cut_full(value):
    high = value.astype(BF16)
    rest = value - high.astype(F32)
    middle = rest.astype(BF16)
    return high, middle, (rest - middle.astype(F32)).astype(BF16)


def dot_pairs(pairs):
    left = jnp.concatenate([pair[0] for pair in pairs], axis=1)
    right = jnp.concatenate([pair[1] for pair in pairs], axis=0)
    return dot(left, right)


def dot_full(left, right):
    a, b = left, right
    return dot_pairs(
        [(a[0], b[0]), (a[0], b[1]), (a[1], b[0]), (a[1], b[1]), (a[0], b[2]), (a[2], b[0])]
    )


def mul(rows, matrix):
    return dot_pairs(pairs_of(rows, matrix))[: rows[2]]


def pairs_of(rows, matrix):
    return [(rows[0], matrix[0]), (rows[1], matrix[0]), (rows[0], matrix[1])]


def at(matrices, level):
    return matrices[0][level], matrices[1][level]


def put(first, place, value):
    yield first, place, value[0]
    yield first + 1, place, value[1]


def small_powers(transition, info_gain, smoother_gain, smoother_input):
    a, g = cut_full(transition[...].T), cut_full(smoother_input[...].T)
    b, k = cut_full(smoother_gain[...].T), cut_full(info_gain[...].T)
    ag = dot_full(a, g)
    kg = dot_full(k, g)
    m = dot_full(cut_full(ag), b)
    for i, value in enumerate([k, cut(kg), cut(dot_full(cut_full(kg), b)), cut(ag), g]):
        yield from put(0, i, value)
    for level in range(8):
        m_cut = cut(m)
        yield from put(2, level, a)
        yield from put(4, level, b)
        yield from put(6, level, m_cut)
        n_cut = cut(mul((a[0], a[1], a[0].shape[0]), m_cut))
        m = m + mul(n_cut, b)
        a, b = dot_full(a, a), dot_full(b, b)
        if level < 7:
            a, b = cut_full(a), cut_full(b)
        yield from put(8, level, n_cut)
    yield 10, None, a
    yield 11, None, b
    yield 12, None, m


def big_powers(a, b, m):
    yield from put(4, None, cut(m[...]))
    a, b = a[...], b[...]
    for level in range(5):
        a, b = cut_full(a), cut_full(b)
        yield from put(0, level, a)
        yield from put(2, level, b)
        if level < 4:
            a, b = dot_full(a, a), dot_full(b, b)


def information_part(order, noise_precision, emission, observations):
    scale = jnp.broadcast_to(noise_precision[...], (128, noise_precision.shape[1])).T
    scale = jnp.concatenate([scale] * (emission.shape[1] // 128), axis=1)
    weighted = (emission[...].astype(F32) * scale).astype(BF16)
    rows = dot(order[...], observations[...]).astype(BF16)
    information = dot(rows, weighted)
    half = rows.shape[0] // 2
    first = lax.axis_index("core") == 0
    yield 1, None, jnp.where(first, information[half:], information[:half])
    yield 0, None, jnp.where(first, information[:half], information[half:])
    yield 2, None, rows


def chosen(number, values):
    out = values[0]
    for i in range(1, len(values)):
        out = jnp.where(number == i, values[i], out)
    return out


def up_sweep(lead, a_cut, b_cut, m_cut, information):
    information = cut(information)
    end, shown, start = (mul(information, at(lead, i)) for i in range(3))
    ends, follows = [], []
    for level in range(5):
        half = end.shape[0] // 2
        first, second = end[:half], end[half:]
        first_cut = cut(first)
        follow = start[half:] + mul(first_cut, at(m_cut, level))
        ends.append(first)
        follows.append(follow)
        start = start[:half] + mul(cut(follow), at(b_cut, level))
        end = second + mul(first_cut, at(a_cut, level))
    return shown, end, start, ends, follows


def sub_sweep(a_cut, b_cut, m_cut, end, start):
    ends, follows = [], []
    for level in range(5, 8):
        by = 2 ** (level - 5)
        end_cut = cut(end)
        follow = roll(start, -by) + mul(end_cut, at(m_cut, level))
        ends.append(end)
        follows.append(follow)
        start = start + mul(cut(follow), at(b_cut, level))
        end = mul(end_cut, at(a_cut, level)) + roll(end, -by)
    return end, start, ends, follows


def both_halves(total, theirs):
    first = lax.axis_index("core") == 0
    total, theirs = total[...], theirs[...]
    return jnp.concatenate(
        [jnp.where(first, total, theirs), jnp.where(first, theirs, total)], axis=0
    )


def block_tree(total, theirs, lead_h, lead_l, m_h, m_l, b_h, b_l, a_h, a_l):
    information = both_halves(total, theirs)
    a_cut, b_cut, m_cut = (a_h, a_l), (b_h, b_l), (m_h, m_l)
    shown, end, start, ends, follows = up_sweep(
        (lead_h, lead_l), a_cut, b_cut, m_cut, information
    )
    end, start, sub_ends, sub_follows = sub_sweep(a_cut, b_cut, m_cut, end, start)
    pair = jnp.concatenate([end[None, :1], start[None, :1]], axis=1)
    yield 0, None, jnp.broadcast_to(pair, (BLOCKS, 2, end.shape[1]))
    yield 1, None, shown
    place = 0
    for i in range(5):
        yield 2, (place, ends[i].shape[0]), ends[i]
        yield 3, (place, ends[i].shape[0]), follows[i]
        place += ends[i].shape[0]
    for i in range(3):
        yield 4, (i * SUB, SUB), spread_first(sub_ends[i], 2**i)
        yield 5, (i * SUB, SUB), spread_first(sub_follows[i], 2**i)


def spread_first(rows, by):
    rows = jnp.where(row_index(rows) % (2 * by) == 0, rows, 0.0)
    step = 1
    while step < 2 * by:
        rows = rows + roll(rows, step)
        step *= 2
    return rows


def states_and_sums(
    gathered,
    a_big_h,
    a_big_l,
    lead_h,
    lead_l,
    m_h,
    m_l,
    b_big_h,
    b_big_l,
    sub_ends,
    sub_follows,
    a_h,
    a_l,
    n_h,
    n_l,
    b_h,
    b_l,
    ends,
    follows,
    shown,
    emission,
    observed,
):
    block = lax.axis_index("y") * N_Z + lax.axis_index("z")
    width = shown.shape[1]
    gathered = gathered[...]
    after = gathered[:, 0]
    index = row_index(after)
    for level in range(5):
        by = 2**level
        before = jnp.where(index >= by, roll(after, by), 0.0)
        after = after + mul(cut(before), at((a_big_h, a_big_l), level))
    enter = jnp.where(index >= 1, roll(after, 1), 0.0)
    follow = gathered[:, 1] + mul(cut(enter), (m_h[...], m_l[...]))
    final = after - mul(cut(after), at((lead_h, lead_l), 4))
    follow = jnp.where(index < BLOCKS - 1, roll(follow, -1), final)
    for level in range(5):
        by = 2**level
        later = jnp.where(index < BLOCKS - by, roll(follow, -by), 0.0)
        follow = follow + mul(cut(later), at((b_big_h, b_big_l), level))

    source = lax.broadcasted_iota(jnp.int32, (16, BLOCKS), 1)
    pick = (source == block).astype(BF16)

    def picked(rows):
        high, low, _ = cut(rows)
        return (dot(pick, high) + dot(pick, low))[:SUB]

    def children(enter, follow, level):
        enter = cut(enter)
        first = pairs_of(enter, at((n_h, n_l), level)) + pairs_of(
            cut(follow), at((b_h, b_l), level)
        )
        return mul(enter, at((a_h, a_l), level)), dot_pairs(first)[: enter[2]]

    enter, follow = picked(enter), picked(follow)
    count = SUB
    index = row_index(enter)
    for level in (7, 6, 5):
        by = 2 ** (level - 5)
        part = (level - 5) * count
        second, first = children(enter, follow, level)
        second = sub_ends[part : part + count] + second
        first = sub_follows[part : part + count] + first
        is_second = (index // by) % 2 == 1
        enter = jnp.where(is_second, second, enter)
        follow = jnp.where(is_second, follow, first)

    bottom = ends.shape[0]
    for level in (4, 3, 2, 1, 0):
        rows = enter.shape[0]
        top, bottom = bottom, bottom - rows
        second, first = children(enter, follow, level)
        second = ends[bottom:top] + second
        first = follows[bottom:top] + first
        enter = jnp.concatenate([enter, second], axis=0)
        follow = jnp.concatenate([first, follow], axis=0)
    smoothed = shown[...] + mul(cut(enter), at((lead_h, lead_l), 3)) + follow
    observed, emission = observed[...], emission[...]

    high, low, _ = cut(smoothed)
    cross = dot(observed, high, ((0,), (0,)))
    predicted = dot(high, emission, ((1,), (1,)))
    error = observed.astype(F32) - predicted
    error = jnp.broadcast_to(jnp.sum(error * error, axis=0, keepdims=True), (8, error.shape[1]))
    crossed = dot(high, jnp.concatenate([high, low], axis=1), ((0,), (0,)))
    moment = crossed[:, :width] + (crossed[:, width:] + crossed[:, width:].T)

    channels = cross.shape[0] // N_Y
    share, line = width // N_Y, channels // N_Z
    lane = lax.broadcasted_iota(jnp.int32, (8, width), 1)
    row = lax.broadcasted_iota(jnp.int32, (8, width), 0)
    parts = []
    for y in range(N_Y):
        free = share * ((y + 1) % N_Y)
        is_free = (lane >= free) & (lane < free + share)
        is_error = (lane >= free) & (lane < free + line) & (row == 0)
        tiles = []
        for z in range(N_Z):
            turned = roll_lanes(
                error[:, y * channels : (y + 1) * channels], (free - line * z) % width
            )
            top = y * share + 8 * z
            tile = jnp.where(is_free, 0.0, moment[top : top + 8])
            tiles.append(jnp.where(is_error, turned, tile))
        mine = cross[y * channels : (y + 1) * channels].reshape(N_Z, line, width)
        parts.append(jnp.concatenate([mine, jnp.stack(tiles)], axis=1))
    y = block // N_Z
    for by in (2, 1, 3, 0):
        yield 1 + by, None, chosen(y, [parts[(i + by) % N_Y] for i in range(N_Y)])

    yield 0, None, smoothed


def in_time_order(natural, smoothed):
    rest, out = smoothed[...], None
    for _ in range(3):
        high = rest.astype(BF16)
        rest = rest - high.astype(F32)
        moved = dot(natural[...], high)
        out = moved if out is None else out + moved
    yield 0, None, out


def add_chunks(c0, c1, c2, c3):
    yield 0, None, (c0[...] + c1[...]) + (c2[...] + c3[...])


def add_pieces(pieces):
    total = pieces[0]
    for i in range(1, N_Z):
        total = total + pieces[i]
    yield 0, None, jnp.broadcast_to(total[None], (N_Z,) + total.shape)


def assemble(bins, *sums):
    place = lax.axis_index("y")
    sums = [part[...] for part in sums]
    width = sums[0].shape[2]
    share = width // N_Y
    line = sums[0].shape[1] - 8
    lane = lax.broadcasted_iota(jnp.int32, (8, width), 1)
    cross, moment, errors = [], [], []
    for y in range(N_Y):
        whole = chosen(place, [sums[(i - y) % N_Y] for i in range(N_Y)])
        cross.append(whole[:, :line].reshape(-1, width) * (1.0 / math.sqrt(bins)))
        moment.append(whole[:, line:].reshape(-1, width))
        error = jnp.zeros((8, width), F32)
        for z in range(N_Z):
            turned = roll_lanes(whole[z, line:], (line * z - share * ((y + 1) % N_Y)) % width)
            error = jnp.where((lane >= line * z) & (lane < line * z + line), turned, error)
        errors.append(error[:1] * (1.0 / bins))
    moment = jnp.concatenate(moment, axis=0)
    row = lax.broadcasted_iota(jnp.int32, moment.shape, 0) // share
    column = lax.broadcasted_iota(jnp.int32, moment.shape, 1) // share
    free = column == jnp.where(row == N_Y - 1, 0, row + 1)
    moment = jnp.where(free, moment.T, moment) * (1.0 / bins)
    yield 0, None, jnp.concatenate(cross, axis=0)
    yield 1, None, moment
    yield 2, None, jnp.concatenate(errors, axis=1)


def shift(value, axis, count, by):
    return lax.ppermute(value, axis, [(i, (i + by) % count) for i in range(count)])


def bit_reversed(count):
    bits = count.bit_length() - 1
    return [int(format(i, "0%db" % bits)[::-1], 2) for i in range(count)]


def row_order(bins):
    length = bins // SUB
    times = np.array([[j * length + t for j in range(SUB)] for t in bit_reversed(length)])
    return np.eye(bins, dtype=np.float32)[times.reshape(-1)]


def local(
    observations, emission, noise_precision, transition, info_gain, smoother_gain, smoother_input
):
    bins, channels = observations.shape
    width = transition.shape[0]
    order = jnp.asarray(row_order(bins), BF16)
    natural = jnp.asarray(row_order(bins).T, BF16)

    mine, other, seen = call(
        information_part,
        [((bins // 2, width), F32)] * 2 + [((bins, channels), BF16)],
        order,
        noise_precision.reshape(1, channels),
        emission,
        observations,
        large=(0, 1, 2, 3),
    )
    mine = mine + shift(other, "core", N_CORE, 1)
    moved = [shift(mine, "x", N_X, by) for by in (2, 1, 3)]

    square = (width, width)
    stack = lambda n: [((n,) + square, BF16)] * 2
    small = call(
        small_powers,
        stack(5) + stack(8) * 4 + [(square, F32)] * 3,
        transition,
        info_gain,
        smoother_gain,
        smoother_input,
    )
    moved, small = lax.optimization_barrier((moved, small))
    lead, a_cut, b_cut, m_cut, n_cut = (small[i : i + 2] for i in range(0, 10, 2))
    big = call(big_powers, stack(5) * 2 + [(square, BF16)] * 2, *small[10:])

    total = mine + moved[0] + moved[1] + moved[2]
    theirs = shift(total, "core", N_CORE, 1)
    ends, *tree = call(
        block_tree,
        [
            ((BLOCKS, 2, width), F32),
            ((bins, width), F32),
            ((SUB * 31, width), F32),
            ((SUB * 31, width), F32),
            ((SUB * 3, width), F32),
            ((SUB * 3, width), F32),
        ],
        total,
        theirs,
        *lead,
        *m_cut,
        *b_cut,
        *a_cut,
    )
    ends, big = lax.optimization_barrier((ends, big))
    gathered = lax.all_to_all(ends, ("y", "z"), 0, 0)
    rows = channels // (N_Y * N_Z) + 8
    chunk = ((N_Z, rows, width), F32)
    shown, tree_ends, follows, sub_ends, sub_follows = tree
    smoothed, *chunks = call(
        states_and_sums,
        [((bins, width), F32)] + [chunk] * N_Y,
        gathered,
        *big[:2],
        *lead,
        *big[4:],
        *big[2:4],
        sub_ends,
        sub_follows,
        *a_cut,
        *n_cut,
        *b_cut,
        tree_ends,
        follows,
        shown,
        emission,
        seen,
    )
    far, near, back = (shift(chunks[by], "y", N_Y, by) for by in (2, 1, 3))
    (smoothed,) = call(in_time_order, [((bins, width), F32)], natural, smoothed)
    (payload,) = call(add_chunks, [chunk], chunks[0], near, far, back)
    payload = lax.all_to_all(payload, "z", 0, 0)
    (spread,) = call(add_pieces, [chunk], payload)
    whole = lax.all_to_all(spread, "z", 0, 0)
    far, near, back = (shift(whole, "y", N_Y, by) for by in (2, 1, 3))
    cross, moment, error = call(
        functools.wraps(assemble)(functools.partial(assemble, bins * BLOCKS)),
        [((channels, width), F32), (square, F32), ((1, channels), F32)],
        whole,
        near,
        far,
        back,
        sent=(0, 1, 2),
    )
    return smoothed, cross, error.reshape(channels), moment


def solution(mesh):
    tm, chan = ("y", "z"), ("x", "core")
    split = Mesh(mesh.devices.reshape(N_Y, N_Z, N_X, N_CORE), tm + chan)
    placed = (P(tm, chan), P(chan, None), P(chan), P(), P(), P(), P())
    return jax.shard_map(
        local,
        mesh=split,
        in_specs=placed,
        out_specs=(P(tm, None), P(chan, None), P(chan), P()),
        check_vma=False,
    )
```

```python
import functools
import math

import jax
import jax.numpy as jnp
import numpy as np
from jax import lax
from jax.experimental import pallas as pl
from jax.experimental.pallas import tpu as pltpu
from jax.sharding import Mesh, PartitionSpec as P

N_Y, N_Z, N_X, N_CORE = 4, 8, 4, 2
BLOCKS = N_Y * N_Z
SUB = 8
F32, BF16 = jnp.float32, jnp.bfloat16
KERNELS = True


class Late:
    def __init__(self, buffer, copies):
        self.buffer, self.copies, self.shape = buffer, copies, buffer.shape

    def __getitem__(self, key):
        while self.copies:
            self.copies.pop().wait()
        return self.buffer[key]


def pieces_of(shape):
    count = 4 if shape[0] >= 256 else 1
    return [(i * (shape[0] // count), shape[0] // count) for i in range(count)]


def call(body, outs, *args, large=(), sent=(), aliases={}, limit=16):
    if not KERNELS:
        results = [jnp.zeros(shape, dtype) for shape, dtype in outs]
        for i in aliases:
            results[aliases[i]] = args[i]
        for i, place, value in body(*args):
            if place is None:
                results[i] = value
            elif isinstance(place, int):
                results[i] = results[i].at[place].set(value)
            else:
                results[i] = lax.dynamic_update_slice_in_dim(results[i], value, place[0], 0)
        return results

    n_in, n_out = len(args), len(outs)
    loaded = [i for i in large if i not in aliases]

    def kernel(*refs):
        values, out_refs, rest = list(refs[:n_in]), refs[n_in : n_in + n_out], refs[n_in + n_out :]
        targets = dict(zip(sent, rest[len(loaded) : -2]))
        in_sems, out_sems = rest[-2:]
        number = 0
        for i, buffer in zip(loaded, rest[: len(loaded)]):
            copies = []
            for start, size in pieces_of(buffer.shape):
                rows = pl.ds(start, size)
                copies.append(
                    pltpu.make_async_copy(refs[i].at[rows], buffer.at[rows], in_sems.at[number])
                )
                copies[-1].start()
                number += 1
            values[i] = Late(buffer, copies)
        leaving = []
        for i, place, value in body(*values):
            index = Ellipsis if place is None else place
            if isinstance(place, tuple):
                index = pl.ds(place[0], place[1])
            if i not in sent:
                out_refs[i][index] = value
                continue
            buffer = targets[i]
            buffer[index] = value
            first = 0 if place is None else place[0]
            for start, size in pieces_of(value.shape):
                rows = pl.ds(first + start, size)
                leaving.append(
                    pltpu.make_async_copy(
                        buffer.at[rows], out_refs[i].at[rows], out_sems.at[len(leaving)]
                    )
                )
                leaving[-1].start()
        for copy in leaving:
            copy.wait()

    args = [
        pltpu.with_memory_space_constraint(arg, pltpu.HBM if i in large else pltpu.VMEM)
        for i, arg in enumerate(args)
    ]
    vmem, far = pl.BlockSpec(memory_space=pltpu.VMEM), pl.BlockSpec(memory_space=pltpu.HBM)
    return pl.pallas_call(
        kernel,
        out_shape=[(pltpu.HBM if i in sent else pltpu.VMEM)(*kind) for i, kind in enumerate(outs)],
        in_specs=[far if i in large else vmem for i in range(n_in)],
        out_specs=[far if i in sent else vmem for i in range(n_out)],
        scratch_shapes=[pltpu.VMEM(args[i].shape, args[i].dtype) for i in loaded]
        + [pltpu.VMEM(*outs[i]) for i in sent]
        + [pltpu.SemaphoreType.DMA((32,)), pltpu.SemaphoreType.DMA((32,))],
        input_output_aliases=dict(aliases),
        compiler_params=pltpu.CompilerParams(vmem_limit_bytes=limit * 2**20),
        name=body.__name__,
    )(*args)


def roll(rows, by):
    if KERNELS:
        return pltpu.roll(rows, by % rows.shape[0], 0)
    return jnp.roll(rows, by, 0)


def roll_lanes(rows, by):
    if KERNELS:
        return pltpu.roll(rows, by, 1)
    return jnp.roll(rows, by, 1)


def row_index(rows):
    return lax.broadcasted_iota(jnp.int32, rows.shape, 0)


def dot(left, right, dims=((1,), (0,))):
    return lax.dot_general(left, right, (dims, ((), ())), preferred_element_type=F32)


def cut(value):
    count = value.shape[0]
    if count < 16:
        value = jnp.concatenate([value, value], axis=0)
    high = value.astype(BF16)
    return high, (value - high.astype(F32)).astype(BF16), count


def cut_full(value):
    high = value.astype(BF16)
    rest = value - high.astype(F32)
    middle = rest.astype(BF16)
    return high, middle, (rest - middle.astype(F32)).astype(BF16)


def dot_pairs(pairs):
    left = jnp.concatenate([pair[0] for pair in pairs], axis=1)
    right = jnp.concatenate([pair[1] for pair in pairs], axis=0)
    return dot(left, right)


def dot_full(left, right):
    a, b = left, right
    return dot_pairs(
        [(a[0], b[0]), (a[0], b[1]), (a[1], b[0]), (a[1], b[1]), (a[0], b[2]), (a[2], b[0])]
    )


def mul(rows, matrix):
    count = rows[0].shape[0]
    if count > 128:
        return dot_pairs([(rows[0], matrix[0]), (rows[1], matrix[0]), (rows[0], matrix[1])])
    found = dot(jnp.concatenate(rows[:2], axis=0), matrix[0])
    found = found[:count] + (found[count:] + dot(rows[0], matrix[1]))
    return found[: rows[2]]


def at(matrices, level):
    return matrices[0][level], matrices[1][level]


def put(first, place, value):
    yield first, place, value[0]
    yield first + 1, place, value[1]


def squares(a, b, level):
    if level < 3:
        a, b = cut_full(a), cut_full(b)
        return dot_full(a, a), dot_full(b, b)
    a, b = cut(a), cut(b)
    return mul(a, a), mul(b, b)


def small_powers(transition, info_gain, smoother_gain, smoother_input):
    a, g = transition[...].T, cut(smoother_input[...].T)
    b, k = smoother_gain[...].T, cut(info_gain[...].T)
    a_cut, b_cut = cut(a), cut(b)
    ag = cut(mul(a_cut, g))
    kg = cut(mul(k, g))
    m = mul(ag, b_cut)
    for i, value in enumerate([k, kg, cut(mul(kg, b_cut)), ag, g]):
        yield from put(0, i, value)
    for level in range(8):
        a_cut, b_cut, m_cut = cut(a), cut(b), cut(m)
        yield from put(2, level, a_cut)
        yield from put(4, level, b_cut)
        yield from put(6, level, m_cut)
        n_cut = cut(mul(a_cut, m_cut))
        m = m + mul(n_cut, b_cut)
        a, b = squares(a, b, level)
        yield from put(8, level, n_cut)
    yield 10, None, a
    yield 11, None, b
    yield 12, None, m


def big_powers(a, b, m):
    yield from put(4, None, cut(m[...]))
    a, b = a[...], b[...]
    for level in range(5):
        yield from put(0, level, cut(a))
        yield from put(2, level, cut(b))
        if level < 4:
            a, b = squares(a, b, 8 + level)


def information_part(order, noise_precision, emission, observations):
    scale = jnp.broadcast_to(noise_precision[...], (128, noise_precision.shape[1])).T
    scale = jnp.concatenate([scale] * (emission.shape[1] // 128), axis=1)
    weighted = (emission[...].astype(F32) * scale).astype(BF16)
    rows = dot(order[...], observations[...]).astype(BF16)
    information = dot(rows, weighted)
    half = rows.shape[0] // 2
    first = lax.axis_index("core") == 0
    yield 1, None, jnp.where(first, information[half:], information[:half])
    yield 0, None, jnp.where(first, information[:half], information[half:])
    yield 2, None, rows


def chosen(number, values):
    out = values[0]
    for i in range(1, len(values)):
        out = jnp.where(number == i, values[i], out)
    return out


def up_sweep(lead, a_cut, b_cut, m_cut, information):
    information = cut(information)
    end, shown, start = (mul(information, at(lead, i)) for i in range(3))
    ends, follows = [], []
    for level in range(5):
        half = end.shape[0] // 2
        first, second = end[:half], end[half:]
        first_cut = cut(first)
        follow = start[half:] + mul(first_cut, at(m_cut, level))
        ends.append(first)
        follows.append(follow)
        start = start[:half] + mul(cut(follow), at(b_cut, level))
        end = second + mul(first_cut, at(a_cut, level))
    return shown, end, start, ends, follows


def sub_sweep(a_cut, b_cut, m_cut, end, start):
    ends, follows = [], []
    for level in range(5, 8):
        by = 2 ** (level - 5)
        end_cut = cut(end)
        follow = roll(start, -by) + mul(end_cut, at(m_cut, level))
        ends.append(end)
        follows.append(follow)
        start = start + mul(cut(follow), at(b_cut, level))
        end = mul(end_cut, at(a_cut, level)) + roll(end, -by)
    return end, start, ends, follows


def both_halves(total, theirs):
    first = lax.axis_index("core") == 0
    total, theirs = total[...], theirs[...]
    return jnp.concatenate(
        [jnp.where(first, total, theirs), jnp.where(first, theirs, total)], axis=0
    )


def block_tree(total, theirs, lead_h, lead_l, m_h, m_l, b_h, b_l, a_h, a_l):
    information = both_halves(total, theirs)
    a_cut, b_cut, m_cut = (a_h, a_l), (b_h, b_l), (m_h, m_l)
    shown, end, start, ends, follows = up_sweep(
        (lead_h, lead_l), a_cut, b_cut, m_cut, information
    )
    end, start, sub_ends, sub_follows = sub_sweep(a_cut, b_cut, m_cut, end, start)
    pair = jnp.concatenate([end[None, :1], start[None, :1]], axis=1)
    yield 0, None, jnp.broadcast_to(pair, (BLOCKS, 2, end.shape[1]))
    yield 1, None, shown
    place = 0
    for i in range(5):
        yield 2, (place, ends[i].shape[0]), ends[i]
        yield 3, (place, ends[i].shape[0]), follows[i]
        place += ends[i].shape[0]
    for i in range(3):
        yield 4, (i * SUB, SUB), spread_first(sub_ends[i], 2**i)
        yield 5, (i * SUB, SUB), spread_first(sub_follows[i], 2**i)


def spread_first(rows, by):
    rows = jnp.where(row_index(rows) % (2 * by) == 0, rows, 0.0)
    step = 1
    while step < 2 * by:
        rows = rows + roll(rows, step)
        step *= 2
    return rows


def states_and_sums(
    gathered,
    a_big_h,
    a_big_l,
    lead_h,
    lead_l,
    m_h,
    m_l,
    b_big_h,
    b_big_l,
    sub_ends,
    sub_follows,
    a_h,
    a_l,
    n_h,
    n_l,
    b_h,
    b_l,
    ends,
    follows,
    shown,
    emission,
    observed,
):
    block = lax.axis_index("y") * N_Z + lax.axis_index("z")
    width = shown.shape[1]
    gathered = gathered[...]
    after = gathered[:, 0]
    index = row_index(after)
    for level in range(5):
        by = 2**level
        before = jnp.where(index >= by, roll(after, by), 0.0)
        after = after + mul(cut(before), at((a_big_h, a_big_l), level))
    enter = jnp.where(index >= 1, roll(after, 1), 0.0)
    follow = gathered[:, 1] + mul(cut(enter), (m_h[...], m_l[...]))
    final = after - mul(cut(after), at((lead_h, lead_l), 4))
    follow = jnp.where(index < BLOCKS - 1, roll(follow, -1), final)
    for level in range(5):
        by = 2**level
        later = jnp.where(index < BLOCKS - by, roll(follow, -by), 0.0)
        follow = follow + mul(cut(later), at((b_big_h, b_big_l), level))

    source = lax.broadcasted_iota(jnp.int32, (16, BLOCKS), 1)
    pick = (source == block).astype(BF16)

    def picked(rows):
        high, low, _ = cut(rows)
        return (dot(pick, high) + dot(pick, low))[:SUB]

    def children(enter, follow, level):
        enter = cut(enter)
        first = mul(enter, at((n_h, n_l), level)) + mul(cut(follow), at((b_h, b_l), level))
        return mul(enter, at((a_h, a_l), level)), first

    enter, follow = picked(enter), picked(follow)
    count = SUB
    index = row_index(enter)
    for level in (7, 6, 5):
        by = 2 ** (level - 5)
        part = (level - 5) * count
        second, first = children(enter, follow, level)
        second = sub_ends[part : part + count] + second
        first = sub_follows[part : part + count] + first
        is_second = (index // by) % 2 == 1
        enter = jnp.where(is_second, second, enter)
        follow = jnp.where(is_second, follow, first)

    bottom = ends.shape[0]
    for level in (4, 3, 2, 1, 0):
        rows = enter.shape[0]
        top, bottom = bottom, bottom - rows
        second, first = children(enter, follow, level)
        second = ends[bottom:top] + second
        first = follows[bottom:top] + first
        enter = jnp.concatenate([enter, second], axis=0)
        follow = jnp.concatenate([first, follow], axis=0)
    smoothed = shown[...] + mul(cut(enter), at((lead_h, lead_l), 3)) + follow
    observed, emission = observed[...], emission[...]

    high, low, _ = cut(smoothed)
    cross = dot(observed, high, ((0,), (0,)))
    predicted = dot(high, emission, ((1,), (1,)))
    error = observed.astype(F32) - predicted
    error = jnp.broadcast_to(jnp.sum(error * error, axis=0, keepdims=True), (8, error.shape[1]))
    crossed = dot(high, jnp.concatenate([high, low], axis=1), ((0,), (0,)))
    moment = crossed[:, :width] + (crossed[:, width:] + crossed[:, width:].T)

    channels = cross.shape[0] // N_Y
    share, line = width // N_Y, channels // N_Z
    lane = lax.broadcasted_iota(jnp.int32, (8, width), 1)
    row = lax.broadcasted_iota(jnp.int32, (8, width), 0)
    parts = []
    for y in range(N_Y):
        free = share * ((y + 1) % N_Y)
        is_free = (lane >= free) & (lane < free + share)
        is_error = (lane >= free) & (lane < free + line) & (row == 0)
        tiles = []
        for z in range(N_Z):
            turned = roll_lanes(
                error[:, y * channels : (y + 1) * channels], (free - line * z) % width
            )
            top = y * share + 8 * z
            tile = jnp.where(is_free, 0.0, moment[top : top + 8])
            tiles.append(jnp.where(is_error, turned, tile))
        mine = cross[y * channels : (y + 1) * channels].reshape(N_Z, line, width)
        parts.append(jnp.concatenate([mine, jnp.stack(tiles)], axis=1))
    y = block // N_Z
    for by in (2, 1, 3, 0):
        yield 1 + by, None, chosen(y, [parts[(i + by) % N_Y] for i in range(N_Y)])

    yield 0, None, smoothed


def in_time_order(natural, smoothed):
    rest, out = smoothed[...], None
    for _ in range(3):
        high = rest.astype(BF16)
        rest = rest - high.astype(F32)
        moved = dot(natural[...], high)
        out = moved if out is None else out + moved
    yield 0, None, out


def add_chunks(c0, c1, c2, c3):
    yield 0, None, (c0[...] + c1[...]) + (c2[...] + c3[...])


def add_pieces(pieces):
    total = pieces[0]
    for i in range(1, N_Z):
        total = total + pieces[i]
    yield 0, None, jnp.broadcast_to(total[None], (N_Z,) + total.shape)


def blocks_of(bins, by_pieces):
    y = lax.axis_index("y")
    for by, piece in by_pieces:
        place = y - by
        place = jnp.where(place < 0, place + N_Y, place)
        width = piece.shape[2]
        share, line = width // N_Y, piece.shape[1] - 8
        cross = piece[:, :line].reshape(-1, width) * (1.0 / math.sqrt(bins))
        moment = piece[:, line:].reshape(-1, width)
        lane = lax.broadcasted_iota(jnp.int32, (8, width), 1)
        free = share * jnp.where(place == N_Y - 1, 0, place + 1)
        error = jnp.zeros((8, width), F32)
        for z in range(N_Z):
            turned = roll_lanes(moment[8 * z : 8 * z + 8], width + line * z - free)
            error = jnp.where((lane >= line * z) & (lane < line * z + line), turned, error)
        yield 0, (tiled(place * cross.shape[0]), cross.shape[0]), cross
        yield 1, (tiled(place * share), share), moment
        yield 2, (tiled(place * 8), 8), error


def tiled(start):
    return pl.multiple_of(start, 8) if KERNELS else start


def first_blocks(bins, own, far):
    yield from blocks_of(bins, [(0, own[...]), (2, far[...])])


def last_blocks(bins, near, back, cross, moments, errors):
    moment, error = moments[...], errors[...]
    for i, (start, size), value in blocks_of(bins, [(1, near[...]), (3, back[...])]):
        if i == 0:
            yield 0, (start, size), value
            continue
        rows = moment if i == 1 else error
        mine = (row_index(rows) >= start) & (row_index(rows) < start + size)
        rows = jnp.where(mine, jnp.concatenate([value] * N_Y, axis=0), rows)
        if i == 1:
            moment = rows
        else:
            error = rows
    share = moment.shape[0] // N_Y
    row = lax.broadcasted_iota(jnp.int32, moment.shape, 0) // share
    column = lax.broadcasted_iota(jnp.int32, moment.shape, 1) // share
    free = column == jnp.where(row == N_Y - 1, 0, row + 1)
    yield 1, None, jnp.where(free, moment.T, moment) * (1.0 / bins)
    error = jnp.concatenate([error[8 * i : 8 * i + 1] for i in range(N_Y)], axis=1)
    yield 2, None, error * (1.0 / bins)


def shift(value, axis, count, by):
    return lax.ppermute(value, axis, [(i, (i + by) % count) for i in range(count)])


def bit_reversed(count):
    bits = count.bit_length() - 1
    return [int(format(i, "0%db" % bits)[::-1], 2) for i in range(count)]


def row_order(bins):
    length = bins // SUB
    times = np.array([[j * length + t for j in range(SUB)] for t in bit_reversed(length)])
    return np.eye(bins, dtype=np.float32)[times.reshape(-1)]


def local(
    observations, emission, noise_precision, transition, info_gain, smoother_gain, smoother_input
):
    bins, channels = observations.shape
    width = transition.shape[0]
    order = jnp.asarray(row_order(bins), BF16)
    natural = jnp.asarray(row_order(bins).T, BF16)

    mine, other, seen = call(
        information_part,
        [((bins // 2, width), F32)] * 2 + [((bins, channels), BF16)],
        order,
        noise_precision.reshape(1, channels),
        emission,
        observations,
        large=(0, 1, 2, 3),
    )
    mine = mine + shift(other, "core", N_CORE, 1)
    moved = [shift(mine, "x", N_X, by) for by in (2, 1, 3)]

    square = (width, width)
    stack = lambda n: [((n,) + square, BF16)] * 2
    small = call(
        small_powers,
        stack(5) + stack(8) * 4 + [(square, F32)] * 3,
        transition,
        info_gain,
        smoother_gain,
        smoother_input,
    )
    moved, small = lax.optimization_barrier((moved, small))
    lead, a_cut, b_cut, m_cut, n_cut = (small[i : i + 2] for i in range(0, 10, 2))
    big = call(big_powers, stack(5) * 2 + [(square, BF16)] * 2, *small[10:])

    total = mine + moved[0] + moved[1] + moved[2]
    theirs = shift(total, "core", N_CORE, 1)
    ends, *tree = call(
        block_tree,
        [
            ((BLOCKS, 2, width), F32),
            ((bins, width), F32),
            ((SUB * 31, width), F32),
            ((SUB * 31, width), F32),
            ((SUB * 3, width), F32),
            ((SUB * 3, width), F32),
        ],
        total,
        theirs,
        *lead,
        *m_cut,
        *b_cut,
        *a_cut,
    )
    ends, big = lax.optimization_barrier((ends, big))
    gathered = lax.all_to_all(ends, ("y", "z"), 0, 0)
    rows = channels // (N_Y * N_Z) + 8
    chunk = ((N_Z, rows, width), F32)
    shown, tree_ends, follows, sub_ends, sub_follows = tree
    smoothed, *chunks = call(
        states_and_sums,
        [((bins, width), F32)] + [chunk] * N_Y,
        gathered,
        *big[:2],
        *lead,
        *big[4:],
        *big[2:4],
        sub_ends,
        sub_follows,
        *a_cut,
        *n_cut,
        *b_cut,
        tree_ends,
        follows,
        shown,
        emission,
        seen,
    )
    far, near, back = (shift(chunks[by], "y", N_Y, by) for by in (2, 1, 3))
    (smoothed,) = call(in_time_order, [((bins, width), F32)], natural, smoothed)
    (payload,) = call(add_chunks, [chunk], chunks[0], near, far, back)
    payload = lax.all_to_all(payload, "z", 0, 0)
    (spread,) = call(add_pieces, [chunk], payload)
    whole = lax.all_to_all(spread, "z", 0, 0)
    far, near, back = (shift(whole, "y", N_Y, by) for by in (2, 1, 3))
    named = lambda body: functools.wraps(body)(functools.partial(body, bins * BLOCKS))
    kinds = [((channels, width), F32), (square, F32)]
    cross, moment, error = call(
        named(first_blocks), kinds + [((8 * N_Y, width), F32)], whole, far, sent=(0,)
    )
    cross, moment, error = call(
        named(last_blocks),
        kinds + [((1, channels), F32)],
        near,
        back,
        cross,
        moment,
        error,
        large=(2,),
        sent=(0, 1, 2),
        aliases={2: 0},
    )
    return smoothed, cross, error.reshape(channels), moment


def solution(mesh):
    tm, chan = ("y", "z"), ("x", "core")
    split = Mesh(mesh.devices.reshape(N_Y, N_Z, N_X, N_CORE), tm + chan)
    placed = (P(tm, chan), P(chan, None), P(chan), P(), P(), P(), P())
    return jax.shard_map(
        local,
        mesh=split,
        in_specs=placed,
        out_specs=(P(tm, None), P(chan, None), P(chan), P()),
        check_vma=False,
    )
```

```python
import functools
import math

import jax
import jax.numpy as jnp
import numpy as np
from jax import lax
from jax.experimental import pallas as pl
from jax.experimental.pallas import tpu as pltpu
from jax.sharding import Mesh, PartitionSpec as P

N_Y, N_Z, N_X, N_CORE = 4, 8, 4, 2
BLOCKS = N_Y * N_Z
SUB = 8
F32, BF16 = jnp.float32, jnp.bfloat16
KERNELS = True


class Late:
    def __init__(self, buffer, copies):
        self.buffer, self.copies, self.shape = buffer, copies, buffer.shape

    def __getitem__(self, key):
        while self.copies:
            self.copies.pop().wait()
        return self.buffer[key]


def pieces_of(shape):
    count = 4 if shape[0] >= 256 else 1
    return [(i * (shape[0] // count), shape[0] // count) for i in range(count)]


def call(body, outs, *args, large=(), sent=(), aliases={}, limit=16):
    if not KERNELS:
        results = [jnp.zeros(shape, dtype) for shape, dtype in outs]
        for i in aliases:
            results[aliases[i]] = args[i]
        for i, place, value in body(*args):
            if place is None:
                results[i] = value
            elif isinstance(place, int):
                results[i] = results[i].at[place].set(value)
            else:
                results[i] = lax.dynamic_update_slice_in_dim(results[i], value, place[0], 0)
        return results

    n_in, n_out = len(args), len(outs)
    loaded = [i for i in large if i not in aliases]

    def kernel(*refs):
        values, out_refs, rest = list(refs[:n_in]), refs[n_in : n_in + n_out], refs[n_in + n_out :]
        targets = dict(zip(sent, rest[len(loaded) : -2]))
        in_sems, out_sems = rest[-2:]
        number = 0
        for i, buffer in zip(loaded, rest[: len(loaded)]):
            copies = []
            for start, size in pieces_of(buffer.shape):
                rows = pl.ds(start, size)
                copies.append(
                    pltpu.make_async_copy(refs[i].at[rows], buffer.at[rows], in_sems.at[number])
                )
                copies[-1].start()
                number += 1
            values[i] = Late(buffer, copies)
        leaving = []
        for i, place, value in body(*values):
            index = Ellipsis if place is None else place
            if isinstance(place, tuple):
                index = pl.ds(place[0], place[1])
            if i not in sent:
                out_refs[i][index] = value
                continue
            buffer = targets[i]
            buffer[index] = value
            first = 0 if place is None else place[0]
            for start, size in pieces_of(value.shape):
                rows = pl.ds(first + start, size)
                leaving.append(
                    pltpu.make_async_copy(
                        buffer.at[rows], out_refs[i].at[rows], out_sems.at[len(leaving)]
                    )
                )
                leaving[-1].start()
        for copy in leaving:
            copy.wait()

    args = [
        pltpu.with_memory_space_constraint(arg, pltpu.HBM if i in large else pltpu.VMEM)
        for i, arg in enumerate(args)
    ]
    vmem, far = pl.BlockSpec(memory_space=pltpu.VMEM), pl.BlockSpec(memory_space=pltpu.HBM)
    return pl.pallas_call(
        kernel,
        out_shape=[(pltpu.HBM if i in sent else pltpu.VMEM)(*kind) for i, kind in enumerate(outs)],
        in_specs=[far if i in large else vmem for i in range(n_in)],
        out_specs=[far if i in sent else vmem for i in range(n_out)],
        scratch_shapes=[pltpu.VMEM(args[i].shape, args[i].dtype) for i in loaded]
        + [pltpu.VMEM(*outs[i]) for i in sent]
        + [pltpu.SemaphoreType.DMA((32,)), pltpu.SemaphoreType.DMA((32,))],
        input_output_aliases=dict(aliases),
        compiler_params=pltpu.CompilerParams(vmem_limit_bytes=limit * 2**20),
        name=body.__name__,
    )(*args)


def roll(rows, by):
    if KERNELS:
        return pltpu.roll(rows, by % rows.shape[0], 0)
    return jnp.roll(rows, by, 0)


def roll_lanes(rows, by):
    if KERNELS:
        return pltpu.roll(rows, by, 1)
    return jnp.roll(rows, by, 1)


def row_index(rows):
    return lax.broadcasted_iota(jnp.int32, rows.shape, 0)


def dot(left, right, dims=((1,), (0,))):
    return lax.dot_general(left, right, (dims, ((), ())), preferred_element_type=F32)


def cut(value):
    count = value.shape[0]
    if count < 16:
        value = jnp.concatenate([value, value], axis=0)
    high = value.astype(BF16)
    return high, (value - high.astype(F32)).astype(BF16), count


def cut_full(value):
    high = value.astype(BF16)
    rest = value - high.astype(F32)
    middle = rest.astype(BF16)
    return high, middle, (rest - middle.astype(F32)).astype(BF16)


def dot_pairs(pairs):
    left = jnp.concatenate([pair[0] for pair in pairs], axis=1)
    right = jnp.concatenate([pair[1] for pair in pairs], axis=0)
    return dot(left, right)


def dot_full(left, right):
    a, b = left, right
    return dot_pairs(
        [(a[0], b[0]), (a[0], b[1]), (a[1], b[0]), (a[1], b[1]), (a[0], b[2]), (a[2], b[0])]
    )


def mul(rows, matrix):
    count = rows[0].shape[0]
    if count > 128:
        return dot_pairs([(rows[0], matrix[0]), (rows[1], matrix[0]), (rows[0], matrix[1])])
    found = dot(jnp.concatenate(rows[:2], axis=0), matrix[0])
    found = found[:count] + (found[count:] + dot(rows[0], matrix[1]))
    return found[: rows[2]]


def at(stacks, level):
    for high, low in stacks:
        if level < high.shape[0]:
            return high[level], low[level]
        level -= high.shape[0]


def put(first, place, value):
    yield first, place, value[0]
    yield first + 1, place, value[1]


def squares(a, b, level):
    if level < 3:
        a, b = cut_full(a), cut_full(b)
        return dot_full(a, a), dot_full(b, b)
    a, b = cut(a), cut(b)
    return mul(a, a), mul(b, b)


FIRST = 6


def powers(transition, info_gain, smoother_gain, smoother_input):
    a, g = transition[...].T, cut(smoother_input[...].T)
    b, k = smoother_gain[...].T, cut(info_gain[...].T)
    a_cut, b_cut = cut(a), cut(b)
    ag = cut(mul(a_cut, g))
    kg = cut(mul(k, g))
    m_cut = None
    for level in range(13):
        a_cut, b_cut = cut(a), cut(b)
        place = level if level < 8 else level - 8
        yield from put(2 if level < 8 else 10, place, a_cut)
        yield from put(4 if level < 8 else 12, place, b_cut)
        if level < 12:
            a, b = squares(a, b, level)
        if level == 0:
            m = mul(ag, b_cut)
            for i, value in enumerate([k, kg, cut(mul(kg, b_cut)), ag, g]):
                yield from put(0, i, value)
        if level <= FIRST:
            m_cut = cut(m)
            yield from put(6, level, m_cut)
        if level < FIRST:
            n_cut = cut(mul(a_cut, m_cut))
            m = m + mul(n_cut, b_cut)
            yield from put(8, level, n_cut)
    yield 14, None, m


def last_effects(a_h, a_l, b_h, b_l, m):
    m = m[...]
    for level in range(FIRST, 8):
        m_cut = cut(m)
        if level > FIRST:
            yield from put(0, level - FIRST - 1, m_cut)
        a_cut = (a_h[level], a_l[level], m.shape[0])
        n_cut = cut(mul(a_cut, m_cut))
        yield from put(2, level - FIRST, n_cut)
        m = m + mul(n_cut, (b_h[level], b_l[level]))
    yield from put(4, None, cut(m))


def information_part(order, noise_precision, emission, observations):
    scale = jnp.broadcast_to(noise_precision[...], (128, noise_precision.shape[1])).T
    scale = jnp.concatenate([scale] * (emission.shape[1] // 128), axis=1)
    weighted = (emission[...].astype(F32) * scale).astype(BF16)
    rows = dot(order[...], observations[...]).astype(BF16)
    information = dot(rows, weighted)
    half = rows.shape[0] // 2
    first = lax.axis_index("core") == 0
    yield 1, None, jnp.where(first, information[half:], information[:half])
    yield 0, None, jnp.where(first, information[:half], information[half:])
    yield 2, None, rows


def chosen(number, values):
    out = values[0]
    for i in range(1, len(values)):
        out = jnp.where(number == i, values[i], out)
    return out


def up_sweep(lead, a_cut, b_cut, m_cut, information):
    information = cut(information)
    end, shown, start = (mul(information, at(lead, i)) for i in range(3))
    ends, follows = [], []
    for level in range(5):
        half = end.shape[0] // 2
        first, second = end[:half], end[half:]
        first_cut = cut(first)
        follow = start[half:] + mul(first_cut, at(m_cut, level))
        ends.append(first)
        follows.append(follow)
        start = start[:half] + mul(cut(follow), at(b_cut, level))
        end = second + mul(first_cut, at(a_cut, level))
    return shown, end, start, ends, follows


def sub_sweep(a_cut, b_cut, m_cut, end, start):
    ends, follows = [], []
    for level in range(5, 8):
        by = 2 ** (level - 5)
        end_cut = cut(end)
        follow = roll(start, -by) + mul(end_cut, at(m_cut, level))
        ends.append(end)
        follows.append(follow)
        start = start + mul(cut(follow), at(b_cut, level))
        end = mul(end_cut, at(a_cut, level)) + roll(end, -by)
    return end, start, ends, follows


def both_halves(total, theirs):
    first = lax.axis_index("core") == 0
    total, theirs = total[...], theirs[...]
    return jnp.concatenate(
        [jnp.where(first, total, theirs), jnp.where(first, theirs, total)], axis=0
    )


def block_tree(
    total, theirs, lead_h, lead_l, m_h, m_l, m_last_h, m_last_l, b_h, b_l, a_h, a_l
):
    information = both_halves(total, theirs)
    a_cut, b_cut = [(a_h, a_l)], [(b_h, b_l)]
    m_cut = [(m_h, m_l), (m_last_h, m_last_l)]
    shown, end, start, ends, follows = up_sweep(
        [(lead_h, lead_l)], a_cut, b_cut, m_cut, information
    )
    end, start, sub_ends, sub_follows = sub_sweep(a_cut, b_cut, m_cut, end, start)
    pair = jnp.concatenate([end[None, :1], start[None, :1]], axis=1)
    yield 0, None, jnp.broadcast_to(pair, (BLOCKS, 2, end.shape[1]))
    yield 1, None, shown
    place = 0
    for i in range(5):
        yield 2, (place, ends[i].shape[0]), ends[i]
        yield 3, (place, ends[i].shape[0]), follows[i]
        place += ends[i].shape[0]
    for i in range(3):
        yield 4, (i * SUB, SUB), spread_first(sub_ends[i], 2**i)
        yield 5, (i * SUB, SUB), spread_first(sub_follows[i], 2**i)


def spread_first(rows, by):
    rows = jnp.where(row_index(rows) % (2 * by) == 0, rows, 0.0)
    step = 1
    while step < 2 * by:
        rows = rows + roll(rows, step)
        step *= 2
    return rows


def states_and_sums(
    gathered,
    a_big_h,
    a_big_l,
    lead_h,
    lead_l,
    m_h,
    m_l,
    b_big_h,
    b_big_l,
    sub_ends,
    sub_follows,
    a_h,
    a_l,
    n_h,
    n_l,
    n_last_h,
    n_last_l,
    b_h,
    b_l,
    ends,
    follows,
    shown,
    emission,
    observed,
):
    block = lax.axis_index("y") * N_Z + lax.axis_index("z")
    width = shown.shape[1]
    gathered = gathered[...]
    after = gathered[:, 0]
    index = row_index(after)
    for level in range(5):
        by = 2**level
        before = jnp.where(index >= by, roll(after, by), 0.0)
        after = after + mul(cut(before), at([(a_big_h, a_big_l)], level))
    enter = jnp.where(index >= 1, roll(after, 1), 0.0)
    follow = gathered[:, 1] + mul(cut(enter), (m_h[...], m_l[...]))
    final = after - mul(cut(after), at([(lead_h, lead_l)], 4))
    follow = jnp.where(index < BLOCKS - 1, roll(follow, -1), final)
    for level in range(5):
        by = 2**level
        later = jnp.where(index < BLOCKS - by, roll(follow, -by), 0.0)
        follow = follow + mul(cut(later), at([(b_big_h, b_big_l)], level))

    source = lax.broadcasted_iota(jnp.int32, (16, BLOCKS), 1)
    pick = (source == block).astype(BF16)

    def picked(rows):
        high, low, _ = cut(rows)
        return (dot(pick, high) + dot(pick, low))[:SUB]

    def children(enter, follow, level):
        enter = cut(enter)
        first = mul(enter, at([(n_h, n_l), (n_last_h, n_last_l)], level)) + mul(cut(follow), at([(b_h, b_l)], level))
        return mul(enter, at([(a_h, a_l)], level)), first

    enter, follow = picked(enter), picked(follow)
    count = SUB
    index = row_index(enter)
    for level in (7, 6, 5):
        by = 2 ** (level - 5)
        part = (level - 5) * count
        second, first = children(enter, follow, level)
        second = sub_ends[part : part + count] + second
        first = sub_follows[part : part + count] + first
        is_second = (index // by) % 2 == 1
        enter = jnp.where(is_second, second, enter)
        follow = jnp.where(is_second, follow, first)

    bottom = ends.shape[0]
    for level in (4, 3, 2, 1, 0):
        rows = enter.shape[0]
        top, bottom = bottom, bottom - rows
        second, first = children(enter, follow, level)
        second = ends[bottom:top] + second
        first = follows[bottom:top] + first
        enter = jnp.concatenate([enter, second], axis=0)
        follow = jnp.concatenate([first, follow], axis=0)
    smoothed = shown[...] + mul(cut(enter), at([(lead_h, lead_l)], 3)) + follow
    observed, emission = observed[...], emission[...]

    high, low, _ = cut(smoothed)
    cross = dot(observed, high, ((0,), (0,)))
    predicted = dot(high, emission, ((1,), (1,)))
    error = observed.astype(F32) - predicted
    error = jnp.broadcast_to(jnp.sum(error * error, axis=0, keepdims=True), (8, error.shape[1]))
    crossed = dot(high, jnp.concatenate([high, low], axis=1), ((0,), (0,)))
    moment = crossed[:, :width] + (crossed[:, width:] + crossed[:, width:].T)

    channels = cross.shape[0] // N_Y
    share, line = width // N_Y, channels // N_Z
    lane = lax.broadcasted_iota(jnp.int32, (8, width), 1)
    row = lax.broadcasted_iota(jnp.int32, (8, width), 0)
    parts = []
    for y in range(N_Y):
        free = share * ((y + 1) % N_Y)
        is_free = (lane >= free) & (lane < free + share)
        is_error = (lane >= free) & (lane < free + line) & (row == 0)
        tiles = []
        for z in range(N_Z):
            turned = roll_lanes(
                error[:, y * channels : (y + 1) * channels], (free - line * z) % width
            )
            top = y * share + 8 * z
            tile = jnp.where(is_free, 0.0, moment[top : top + 8])
            tiles.append(jnp.where(is_error, turned, tile))
        mine = cross[y * channels : (y + 1) * channels].reshape(N_Z, line, width)
        parts.append(jnp.concatenate([mine, jnp.stack(tiles)], axis=1))
    y = block // N_Z
    for by in (2, 1, 3, 0):
        yield 1 + by, None, chosen(y, [parts[(i + by) % N_Y] for i in range(N_Y)])

    yield 0, None, smoothed


def in_time_order(natural, smoothed):
    rest, out = smoothed[...], None
    for _ in range(3):
        high = rest.astype(BF16)
        rest = rest - high.astype(F32)
        moved = dot(natural[...], high)
        out = moved if out is None else out + moved
    yield 0, None, out


def add_chunks(c0, c1, c2, c3):
    yield 0, None, (c0[...] + c1[...]) + (c2[...] + c3[...])


def add_pieces(pieces):
    total = pieces[0]
    for i in range(1, N_Z):
        total = total + pieces[i]
    yield 0, None, jnp.broadcast_to(total[None], (N_Z,) + total.shape)


def blocks_of(bins, by_pieces):
    y = lax.axis_index("y")
    for by, piece in by_pieces:
        place = y - by
        place = jnp.where(place < 0, place + N_Y, place)
        width = piece.shape[2]
        share, line = width // N_Y, piece.shape[1] - 8
        cross = piece[:, :line].reshape(-1, width) * (1.0 / math.sqrt(bins))
        moment = piece[:, line:].reshape(-1, width)
        lane = lax.broadcasted_iota(jnp.int32, (8, width), 1)
        free = share * jnp.where(place == N_Y - 1, 0, place + 1)
        error = jnp.zeros((8, width), F32)
        for z in range(N_Z):
            turned = roll_lanes(moment[8 * z : 8 * z + 8], width + line * z - free)
            error = jnp.where((lane >= line * z) & (lane < line * z + line), turned, error)
        yield 0, (tiled(place * cross.shape[0]), cross.shape[0]), cross
        yield 1, (tiled(place * share), share), moment
        yield 2, (tiled(place * 8), 8), error


def tiled(start):
    return pl.multiple_of(start, 8) if KERNELS else start


def first_blocks(bins, own, near):
    yield from blocks_of(bins, [(0, own[...]), (1, near[...])])


def last_blocks(bins, back, far, cross, moments, errors):
    moment, error = moments[...], errors[...]
    for i, (start, size), value in blocks_of(bins, [(3, back[...]), (2, far[...])]):
        if i == 0:
            yield 0, (start, size), value
            continue
        rows = moment if i == 1 else error
        mine = (row_index(rows) >= start) & (row_index(rows) < start + size)
        rows = jnp.where(mine, jnp.concatenate([value] * N_Y, axis=0), rows)
        if i == 1:
            moment = rows
        else:
            error = rows
    share = moment.shape[0] // N_Y
    row = lax.broadcasted_iota(jnp.int32, moment.shape, 0) // share
    column = lax.broadcasted_iota(jnp.int32, moment.shape, 1) // share
    free = column == jnp.where(row == N_Y - 1, 0, row + 1)
    yield 1, None, jnp.where(free, moment.T, moment) * (1.0 / bins)
    error = jnp.concatenate([error[8 * i : 8 * i + 1] for i in range(N_Y)], axis=1)
    yield 2, None, error * (1.0 / bins)


def shift(value, axis, count, by):
    return lax.ppermute(value, axis, [(i, (i + by) % count) for i in range(count)])


def shift_flat(value, axis, count, by):
    return shift(value.reshape(-1, value.shape[-1]), axis, count, by).reshape(value.shape)


def bit_reversed(count):
    bits = count.bit_length() - 1
    return [int(format(i, "0%db" % bits)[::-1], 2) for i in range(count)]


def row_order(bins):
    length = bins // SUB
    times = np.array([[j * length + t for j in range(SUB)] for t in bit_reversed(length)])
    return np.eye(bins, dtype=np.float32)[times.reshape(-1)]


def local(
    observations, emission, noise_precision, transition, info_gain, smoother_gain, smoother_input
):
    bins, channels = observations.shape
    width = transition.shape[0]
    order = jnp.asarray(row_order(bins), BF16)
    natural = jnp.asarray(row_order(bins).T, BF16)

    mine, other, seen = call(
        information_part,
        [((bins // 2, width), F32)] * 2 + [((bins, channels), BF16)],
        order,
        noise_precision.reshape(1, channels),
        emission,
        observations,
        large=(0, 1, 2, 3),
    )
    mine = mine + shift(other, "core", N_CORE, 1)
    moved = [shift(mine, "x", N_X, by) for by in (2, 1, 3)]

    square = (width, width)
    stack = lambda n: [((n,) + square, BF16)] * 2
    known = call(
        powers,
        stack(5) + stack(8) * 2 + stack(FIRST + 1) + stack(FIRST) + stack(5) * 2 + [(square, F32)],
        transition,
        info_gain,
        smoother_gain,
        smoother_input,
    )
    moved, known = lax.optimization_barrier((moved, known))
    lead, a_cut, b_cut, m_cut, n_cut, a_big, b_big = (known[i : i + 2] for i in range(0, 14, 2))
    late = call(
        last_effects,
        stack(7 - FIRST) + stack(8 - FIRST) + [(square, BF16)] * 2,
        *a_cut,
        *b_cut,
        known[14],
    )

    total = mine + moved[0] + moved[1] + moved[2]
    theirs = shift(total, "core", N_CORE, 1)
    ends, *tree = call(
        block_tree,
        [
            ((BLOCKS, 2, width), F32),
            ((bins, width), F32),
            ((SUB * 31, width), F32),
            ((SUB * 31, width), F32),
            ((SUB * 3, width), F32),
            ((SUB * 3, width), F32),
        ],
        total,
        theirs,
        *lead,
        *m_cut,
        *late[:2],
        *b_cut,
        *a_cut,
    )
    ends, late = lax.optimization_barrier((ends, late))
    gathered = lax.all_to_all(ends, ("y", "z"), 0, 0)
    rows = channels // (N_Y * N_Z) + 8
    chunk = ((N_Z, rows, width), F32)
    shown, tree_ends, follows, sub_ends, sub_follows = tree
    smoothed, *chunks = call(
        states_and_sums,
        [((bins, width), F32)] + [chunk] * N_Y,
        gathered,
        *a_big,
        *lead,
        *late[4:],
        *b_big,
        sub_ends,
        sub_follows,
        *a_cut,
        *n_cut,
        *late[2:4],
        *b_cut,
        tree_ends,
        follows,
        shown,
        emission,
        seen,
    )
    back, near, far = (shift_flat(chunks[by], "y", N_Y, by) for by in (3, 1, 2))
    (smoothed,) = call(in_time_order, [((bins, width), F32)], natural, smoothed)
    (payload,) = call(add_chunks, [chunk], chunks[0], near, back, far)
    payload = lax.all_to_all(payload, "z", 0, 0)
    (spread,) = call(add_pieces, [chunk], payload)
    whole = lax.all_to_all(spread, "z", 0, 0)
    far, near, back = (shift_flat(whole, "y", N_Y, by) for by in (2, 1, 3))
    named = lambda body: functools.wraps(body)(functools.partial(body, bins * BLOCKS))
    kinds = [((channels, width), F32), (square, F32)]
    cross, moment, error = call(
        named(first_blocks), kinds + [((8 * N_Y, width), F32)], whole, near, sent=(0,)
    )
    cross, moment, error = call(
        named(last_blocks),
        kinds + [((1, channels), F32)],
        back,
        far,
        cross,
        moment,
        error,
        large=(2,),
        sent=(0, 1, 2),
        aliases={2: 0},
    )
    return smoothed, cross, error.reshape(channels), moment


def solution(mesh):
    tm, chan = ("y", "z"), ("x", "core")
    split = Mesh(mesh.devices.reshape(N_Y, N_Z, N_X, N_CORE), tm + chan)
    placed = (P(tm, chan), P(chan, None), P(chan), P(), P(), P(), P())
    return jax.shard_map(
        local,
        mesh=split,
        in_specs=placed,
        out_specs=(P(tm, None), P(chan, None), P(chan), P()),
        check_vma=False,
    )
```

```python
import functools
import math

import jax
import jax.numpy as jnp
import numpy as np
from jax import lax
from jax.experimental import pallas as pl
from jax.experimental.pallas import tpu as pltpu
from jax.sharding import Mesh, PartitionSpec as P

N_Y, N_Z, N_X, N_CORE = 4, 8, 4, 2
BLOCKS = N_Y * N_Z
SUB = 8
F32, BF16 = jnp.float32, jnp.bfloat16
KERNELS = True


class Late:
    def __init__(self, buffer, copies):
        self.buffer, self.copies, self.shape = buffer, copies, buffer.shape

    def __getitem__(self, key):
        while self.copies:
            self.copies.pop().wait()
        return self.buffer[key]


def pieces_of(shape):
    count = 4 if shape[0] >= 256 else 1
    return [(i * (shape[0] // count), shape[0] // count) for i in range(count)]


def call(body, outs, *args, large=(), sent=(), aliases={}, limit=16):
    if not KERNELS:
        results = [jnp.zeros(shape, dtype) for shape, dtype in outs]
        for i in aliases:
            results[aliases[i]] = args[i]
        for i, place, value in body(*args):
            if place is None:
                results[i] = value
            elif isinstance(place, int):
                results[i] = results[i].at[place].set(value)
            else:
                results[i] = lax.dynamic_update_slice_in_dim(results[i], value, place[0], 0)
        return results

    n_in, n_out = len(args), len(outs)
    loaded = [i for i in large if i not in aliases]

    def kernel(*refs):
        values, out_refs, rest = list(refs[:n_in]), refs[n_in : n_in + n_out], refs[n_in + n_out :]
        targets = dict(zip(sent, rest[len(loaded) : -2]))
        in_sems, out_sems = rest[-2:]
        number = 0
        for i, buffer in zip(loaded, rest[: len(loaded)]):
            copies = []
            for start, size in pieces_of(buffer.shape):
                rows = pl.ds(start, size)
                copies.append(
                    pltpu.make_async_copy(refs[i].at[rows], buffer.at[rows], in_sems.at[number])
                )
                copies[-1].start()
                number += 1
            values[i] = Late(buffer, copies)
        leaving = []
        for i, place, value in body(*values):
            index = Ellipsis if place is None else place
            if isinstance(place, tuple):
                index = pl.ds(place[0], place[1])
            if i not in sent:
                out_refs[i][index] = value
                continue
            buffer = targets[i]
            buffer[index] = value
            first = 0 if place is None else place[0]
            for start, size in pieces_of(value.shape):
                rows = pl.ds(first + start, size)
                leaving.append(
                    pltpu.make_async_copy(
                        buffer.at[rows], out_refs[i].at[rows], out_sems.at[len(leaving)]
                    )
                )
                leaving[-1].start()
        for copy in leaving:
            copy.wait()

    args = [
        pltpu.with_memory_space_constraint(arg, pltpu.HBM if i in large else pltpu.VMEM)
        for i, arg in enumerate(args)
    ]
    vmem, far = pl.BlockSpec(memory_space=pltpu.VMEM), pl.BlockSpec(memory_space=pltpu.HBM)
    return pl.pallas_call(
        kernel,
        out_shape=[(pltpu.HBM if i in sent else pltpu.VMEM)(*kind) for i, kind in enumerate(outs)],
        in_specs=[far if i in large else vmem for i in range(n_in)],
        out_specs=[far if i in sent else vmem for i in range(n_out)],
        scratch_shapes=[pltpu.VMEM(args[i].shape, args[i].dtype) for i in loaded]
        + [pltpu.VMEM(*outs[i]) for i in sent]
        + [pltpu.SemaphoreType.DMA((32,)), pltpu.SemaphoreType.DMA((32,))],
        input_output_aliases=dict(aliases),
        compiler_params=pltpu.CompilerParams(vmem_limit_bytes=limit * 2**20),
        name=body.__name__,
    )(*args)


def roll(rows, by):
    if KERNELS:
        return pltpu.roll(rows, by % rows.shape[0], 0)
    return jnp.roll(rows, by, 0)


def roll_lanes(rows, by):
    if KERNELS:
        return pltpu.roll(rows, by, 1)
    return jnp.roll(rows, by, 1)


def row_index(rows):
    return lax.broadcasted_iota(jnp.int32, rows.shape, 0)


def dot(left, right, dims=((1,), (0,))):
    return lax.dot_general(left, right, (dims, ((), ())), preferred_element_type=F32)


def cut(value):
    count = value.shape[0]
    if count < 16:
        value = jnp.concatenate([value, value], axis=0)
    high = value.astype(BF16)
    return high, (value - high.astype(F32)).astype(BF16), count


def cut_full(value):
    high = value.astype(BF16)
    rest = value - high.astype(F32)
    middle = rest.astype(BF16)
    return high, middle, (rest - middle.astype(F32)).astype(BF16)


def dot_pairs(pairs):
    left = jnp.concatenate([pair[0] for pair in pairs], axis=1)
    right = jnp.concatenate([pair[1] for pair in pairs], axis=0)
    return dot(left, right)


def dot_full(left, right):
    a, b = left, right
    return dot_pairs(
        [(a[0], b[0]), (a[0], b[1]), (a[1], b[0]), (a[1], b[1]), (a[0], b[2]), (a[2], b[0])]
    )


def mul(rows, matrix):
    count = rows[0].shape[0]
    if count > 128:
        return dot_pairs([(rows[0], matrix[0]), (rows[1], matrix[0]), (rows[0], matrix[1])])
    found = dot(jnp.concatenate(rows[:2], axis=0), matrix[0])
    found = found[:count] + (found[count:] + dot(rows[0], matrix[1]))
    return found[: rows[2]]


def at(stacks, level):
    for high, low in stacks:
        if level < high.shape[0]:
            return high[level], low[level]
        level -= high.shape[0]


def put(first, place, value):
    yield first, place, value[0]
    yield first + 1, place, value[1]


def squares(a, b, level):
    if level < 3:
        a, b = cut_full(a), cut_full(b)
        return dot_full(a, a), dot_full(b, b)
    a, b = cut(a), cut(b)
    return mul(a, a), mul(b, b)


FIRST = 6


def powers(transition, info_gain, smoother_gain, smoother_input):
    a, g = transition[...].T, cut(smoother_input[...].T)
    b, k = smoother_gain[...].T, cut(info_gain[...].T)
    a_cut, b_cut = cut(a), cut(b)
    ag = cut(mul(a_cut, g))
    kg = cut(mul(k, g))
    m_cut = None
    for level in range(13):
        a_cut, b_cut = cut(a), cut(b)
        place = level if level < 8 else level - 8
        yield from put(2 if level < 8 else 10, place, a_cut)
        yield from put(4 if level < 8 else 12, place, b_cut)
        if level < 12:
            a, b = squares(a, b, level)
        if level == 0:
            m = mul(ag, b_cut)
            for i, value in enumerate([k, kg, cut(mul(kg, b_cut)), ag, g]):
                yield from put(0, i, value)
        if level <= FIRST:
            m_cut = cut(m)
            yield from put(6, level, m_cut)
        if level < FIRST:
            n_cut = cut(mul(a_cut, m_cut))
            m = m + mul(n_cut, b_cut)
            yield from put(8, level, n_cut)
    yield 14, None, m


def last_effects(a_h, a_l, b_h, b_l, m):
    m = m[...]
    for level in range(FIRST, 8):
        m_cut = cut(m)
        if level > FIRST:
            yield from put(0, level - FIRST - 1, m_cut)
        a_cut = (a_h[level], a_l[level], m.shape[0])
        n_cut = cut(mul(a_cut, m_cut))
        yield from put(2, level - FIRST, n_cut)
        m = m + mul(n_cut, (b_h[level], b_l[level]))
    yield from put(4, None, cut(m))


def information_part(order, noise_precision, emission, observations):
    scale = jnp.broadcast_to(noise_precision[...], (128, noise_precision.shape[1])).T
    scale = jnp.concatenate([scale] * (emission.shape[1] // 128), axis=1)
    weighted = (emission[...].astype(F32) * scale).astype(BF16)
    rows = dot(order[...], observations[...]).astype(BF16)
    information = dot(rows, weighted)
    half = rows.shape[0] // 2
    first = lax.axis_index("core") == 0
    yield 1, None, jnp.where(first, information[half:], information[:half])
    yield 0, None, jnp.where(first, information[:half], information[half:])
    yield 2, None, rows


def chosen(number, values):
    out = values[0]
    for i in range(1, len(values)):
        out = jnp.where(number == i, values[i], out)
    return out


def up_sweep(lead, a_cut, b_cut, m_cut, information):
    information = cut(information)
    end, shown, start = (mul(information, at(lead, i)) for i in range(3))
    ends, follows = [], []
    for level in range(5):
        half = end.shape[0] // 2
        first, second = end[:half], end[half:]
        first_cut = cut(first)
        follow = start[half:] + mul(first_cut, at(m_cut, level))
        ends.append(first)
        follows.append(follow)
        start = start[:half] + mul(cut(follow), at(b_cut, level))
        end = second + mul(first_cut, at(a_cut, level))
    return shown, end, start, ends, follows


def sub_sweep(a_cut, b_cut, m_cut, end, start):
    ends, follows = [], []
    for level in range(5, 8):
        by = 2 ** (level - 5)
        end_cut = cut(end)
        follow = roll(start, -by) + mul(end_cut, at(m_cut, level))
        ends.append(end)
        follows.append(follow)
        start = start + mul(cut(follow), at(b_cut, level))
        end = mul(end_cut, at(a_cut, level)) + roll(end, -by)
    return end, start, ends, follows


def both_halves(total, theirs):
    first = lax.axis_index("core") == 0
    total, theirs = total[...], theirs[...]
    return jnp.concatenate(
        [jnp.where(first, total, theirs), jnp.where(first, theirs, total)], axis=0
    )


def block_tree(
    total, theirs, lead_h, lead_l, m_h, m_l, m_last_h, m_last_l, b_h, b_l, a_h, a_l
):
    information = both_halves(total, theirs)
    a_cut, b_cut = [(a_h, a_l)], [(b_h, b_l)]
    m_cut = [(m_h, m_l), (m_last_h, m_last_l)]
    shown, end, start, ends, follows = up_sweep(
        [(lead_h, lead_l)], a_cut, b_cut, m_cut, information
    )
    end, start, sub_ends, sub_follows = sub_sweep(a_cut, b_cut, m_cut, end, start)
    pair = jnp.concatenate([end[None, :1], start[None, :1]], axis=1)
    yield 0, None, jnp.broadcast_to(pair, (BLOCKS, 2, end.shape[1]))
    yield 1, None, shown
    place = 0
    for i in range(5):
        yield 2, (place, ends[i].shape[0]), ends[i]
        yield 3, (place, ends[i].shape[0]), follows[i]
        place += ends[i].shape[0]
    for i in range(3):
        yield 4, (i * SUB, SUB), spread_first(sub_ends[i], 2**i)
        yield 5, (i * SUB, SUB), spread_first(sub_follows[i], 2**i)


def spread_first(rows, by):
    rows = jnp.where(row_index(rows) % (2 * by) == 0, rows, 0.0)
    step = 1
    while step < 2 * by:
        rows = rows + roll(rows, step)
        step *= 2
    return rows


def states_and_sums(
    gathered,
    a_big_h,
    a_big_l,
    lead_h,
    lead_l,
    m_h,
    m_l,
    b_big_h,
    b_big_l,
    sub_ends,
    sub_follows,
    a_h,
    a_l,
    n_h,
    n_l,
    n_last_h,
    n_last_l,
    b_h,
    b_l,
    ends,
    follows,
    shown,
    emission,
    observed,
):
    block = lax.axis_index("y") * N_Z + lax.axis_index("z")
    width = shown.shape[1]
    gathered = gathered[...]
    after = gathered[:, 0]
    index = row_index(after)
    for level in range(5):
        by = 2**level
        before = jnp.where(index >= by, roll(after, by), 0.0)
        after = after + mul(cut(before), at([(a_big_h, a_big_l)], level))
    enter = jnp.where(index >= 1, roll(after, 1), 0.0)
    follow = gathered[:, 1] + mul(cut(enter), (m_h[...], m_l[...]))
    final = after - mul(cut(after), at([(lead_h, lead_l)], 4))
    follow = jnp.where(index < BLOCKS - 1, roll(follow, -1), final)
    for level in range(5):
        by = 2**level
        later = jnp.where(index < BLOCKS - by, roll(follow, -by), 0.0)
        follow = follow + mul(cut(later), at([(b_big_h, b_big_l)], level))

    source = lax.broadcasted_iota(jnp.int32, (16, BLOCKS), 1)
    pick = (source == block).astype(BF16)

    def picked(rows):
        high, low, _ = cut(rows)
        return (dot(pick, high) + dot(pick, low))[:SUB]

    def children(enter, follow, level):
        enter = cut(enter)
        first = mul(enter, at([(n_h, n_l), (n_last_h, n_last_l)], level)) + mul(cut(follow), at([(b_h, b_l)], level))
        return mul(enter, at([(a_h, a_l)], level)), first

    enter, follow = picked(enter), picked(follow)
    count = SUB
    index = row_index(enter)
    for level in (7, 6, 5):
        by = 2 ** (level - 5)
        part = (level - 5) * count
        second, first = children(enter, follow, level)
        second = sub_ends[part : part + count] + second
        first = sub_follows[part : part + count] + first
        is_second = (index // by) % 2 == 1
        enter = jnp.where(is_second, second, enter)
        follow = jnp.where(is_second, follow, first)

    bottom = ends.shape[0]
    for level in (4, 3, 2, 1, 0):
        rows = enter.shape[0]
        top, bottom = bottom, bottom - rows
        second, first = children(enter, follow, level)
        second = ends[bottom:top] + second
        first = follows[bottom:top] + first
        enter = jnp.concatenate([enter, second], axis=0)
        follow = jnp.concatenate([first, follow], axis=0)
    smoothed = shown[...] + mul(cut(enter), at([(lead_h, lead_l)], 3)) + follow
    observed, emission = observed[...], emission[...]

    high, low, _ = cut(smoothed)
    cross = dot(observed, high, ((0,), (0,)))
    predicted = dot(high, emission, ((1,), (1,)))
    error = observed.astype(F32) - predicted
    error = jnp.broadcast_to(jnp.sum(error * error, axis=0, keepdims=True), (8, error.shape[1]))
    crossed = dot(high, jnp.concatenate([high, low], axis=1), ((0,), (0,)))
    moment = crossed[:, :width] + (crossed[:, width:] + crossed[:, width:].T)

    channels = cross.shape[0] // N_Y
    share, line = width // N_Y, channels // N_Z
    lane = lax.broadcasted_iota(jnp.int32, (8, width), 1)
    row = lax.broadcasted_iota(jnp.int32, (8, width), 0)
    parts = []
    for y in range(N_Y):
        free = share * ((y + 1) % N_Y)
        is_free = (lane >= free) & (lane < free + share)
        is_error = (lane >= free) & (lane < free + line) & (row == 0)
        tiles = []
        for z in range(N_Z):
            turned = roll_lanes(
                error[:, y * channels : (y + 1) * channels], (free - line * z) % width
            )
            top = y * share + 8 * z
            tile = jnp.where(is_free, 0.0, moment[top : top + 8])
            tiles.append(jnp.where(is_error, turned, tile))
        mine = cross[y * channels : (y + 1) * channels].reshape(N_Z, line, width)
        parts.append(jnp.concatenate([mine, jnp.stack(tiles)], axis=1))
    y = block // N_Z
    for by in (2, 1, 3, 0):
        yield 1 + by, None, chosen(y, [parts[(i + by) % N_Y] for i in range(N_Y)])

    yield 0, None, smoothed


def in_time_order(natural, smoothed):
    rest, out = smoothed[...], None
    for _ in range(3):
        high = rest.astype(BF16)
        rest = rest - high.astype(F32)
        moved = dot(natural[...], high)
        out = moved if out is None else out + moved
    yield 0, None, out


def add_chunks(c0, c1, c2, c3):
    yield 0, None, (c0[...] + c1[...]) + (c2[...] + c3[...])


def add_pieces(pieces):
    total = pieces[0]
    for i in range(1, N_Z):
        total = total + pieces[i]
    yield 0, None, jnp.broadcast_to(total[None], (N_Z,) + total.shape)


def blocks_of(bins, by_pieces):
    y = lax.axis_index("y")
    for by, piece in by_pieces:
        place = y - by
        place = jnp.where(place < 0, place + N_Y, place)
        width = piece.shape[2]
        share, line = width // N_Y, piece.shape[1] - 8
        cross = piece[:, :line].reshape(-1, width) * (1.0 / math.sqrt(bins))
        moment = piece[:, line:].reshape(-1, width)
        lane = lax.broadcasted_iota(jnp.int32, (8, width), 1)
        free = share * jnp.where(place == N_Y - 1, 0, place + 1)
        error = jnp.zeros((8, width), F32)
        for z in range(N_Z):
            turned = roll_lanes(moment[8 * z : 8 * z + 8], width + line * z - free)
            error = jnp.where((lane >= line * z) & (lane < line * z + line), turned, error)
        yield 0, (tiled(place * cross.shape[0]), cross.shape[0]), cross
        yield 1, (tiled(place * share), share), moment
        yield 2, (tiled(place * 8), 8), error


def tiled(start):
    return pl.multiple_of(start, 8) if KERNELS else start


def first_blocks(bins, own, near):
    yield from blocks_of(bins, [(0, own[...]), (1, near[...])])


def last_blocks(bins, far, back, cross, moments, errors):
    moment, error = moments[...], errors[...]
    for i, (start, size), value in blocks_of(bins, [(3, back[...]), (2, far[...])]):
        if i == 0:
            yield 0, (start, size), value
            continue
        rows = moment if i == 1 else error
        mine = (row_index(rows) >= start) & (row_index(rows) < start + size)
        rows = jnp.where(mine, jnp.concatenate([value] * N_Y, axis=0), rows)
        if i == 1:
            moment = rows
        else:
            error = rows
    share = moment.shape[0] // N_Y
    row = lax.broadcasted_iota(jnp.int32, moment.shape, 0) // share
    column = lax.broadcasted_iota(jnp.int32, moment.shape, 1) // share
    free = column == jnp.where(row == N_Y - 1, 0, row + 1)
    yield 1, None, jnp.where(free, moment.T, moment) * (1.0 / bins)
    error = jnp.concatenate([error[8 * i : 8 * i + 1] for i in range(N_Y)], axis=1)
    yield 2, None, error * (1.0 / bins)


def shift(value, axis, count, by):
    return lax.ppermute(value, axis, [(i, (i + by) % count) for i in range(count)])


def shift_flat(value, axis, count, by):
    return shift(value.reshape(-1, value.shape[-1]), axis, count, by).reshape(value.shape)


def bit_reversed(count):
    bits = count.bit_length() - 1
    return [int(format(i, "0%db" % bits)[::-1], 2) for i in range(count)]


def row_order(bins):
    length = bins // SUB
    times = np.array([[j * length + t for j in range(SUB)] for t in bit_reversed(length)])
    return np.eye(bins, dtype=np.float32)[times.reshape(-1)]


def local(
    observations, emission, noise_precision, transition, info_gain, smoother_gain, smoother_input
):
    bins, channels = observations.shape
    width = transition.shape[0]
    order = jnp.asarray(row_order(bins), BF16)
    natural = jnp.asarray(row_order(bins).T, BF16)

    mine, other, seen = call(
        information_part,
        [((bins // 2, width), F32)] * 2 + [((bins, channels), BF16)],
        order,
        noise_precision.reshape(1, channels),
        emission,
        observations,
        large=(0, 1, 2, 3),
    )
    mine = mine + shift(other, "core", N_CORE, 1)
    moved = [shift(mine, "x", N_X, by) for by in (2, 1, 3)]

    square = (width, width)
    stack = lambda n: [((n,) + square, BF16)] * 2
    known = call(
        powers,
        stack(5) + stack(8) * 2 + stack(FIRST + 1) + stack(FIRST) + stack(5) * 2 + [(square, F32)],
        transition,
        info_gain,
        smoother_gain,
        smoother_input,
    )
    moved, known = lax.optimization_barrier((moved, known))
    lead, a_cut, b_cut, m_cut, n_cut, a_big, b_big = (known[i : i + 2] for i in range(0, 14, 2))
    late = call(
        last_effects,
        stack(7 - FIRST) + stack(8 - FIRST) + [(square, BF16)] * 2,
        *a_cut,
        *b_cut,
        known[14],
    )

    total = mine + moved[0] + moved[1] + moved[2]
    theirs = shift(total, "core", N_CORE, 1)
    ends, *tree = call(
        block_tree,
        [
            ((BLOCKS, 2, width), F32),
            ((bins, width), F32),
            ((SUB * 31, width), F32),
            ((SUB * 31, width), F32),
            ((SUB * 3, width), F32),
            ((SUB * 3, width), F32),
        ],
        total,
        theirs,
        *lead,
        *m_cut,
        *late[:2],
        *b_cut,
        *a_cut,
    )
    ends, late = lax.optimization_barrier((ends, late))
    gathered = lax.all_to_all(ends, ("y", "z"), 0, 0)
    rows = channels // (N_Y * N_Z) + 8
    chunk = ((N_Z, rows, width), F32)
    shown, tree_ends, follows, sub_ends, sub_follows = tree
    smoothed, *chunks = call(
        states_and_sums,
        [((bins, width), F32)] + [chunk] * N_Y,
        gathered,
        *a_big,
        *lead,
        *late[4:],
        *b_big,
        sub_ends,
        sub_follows,
        *a_cut,
        *n_cut,
        *late[2:4],
        *b_cut,
        tree_ends,
        follows,
        shown,
        emission,
        seen,
    )
    back, near, far = (shift_flat(chunks[by], "y", N_Y, by) for by in (3, 1, 2))
    (smoothed,) = call(in_time_order, [((bins, width), F32)], natural, smoothed)
    (payload,) = call(add_chunks, [chunk], chunks[0], near, back, far)
    payload = lax.all_to_all(payload, "z", 0, 0)
    (spread,) = call(add_pieces, [chunk], payload)
    whole = lax.all_to_all(spread, "z", 0, 0)
    far, near, back = (shift_flat(whole, "y", N_Y, by) for by in (2, 1, 3))
    named = lambda body: functools.wraps(body)(functools.partial(body, bins * BLOCKS))
    kinds = [((channels, width), F32), (square, F32)]
    cross, moment, error = call(
        named(first_blocks), kinds + [((8 * N_Y, width), F32)], whole, near, sent=(0,)
    )
    cross, moment, error = call(
        named(last_blocks),
        kinds + [((1, channels), F32)],
        far,
        back,
        cross,
        moment,
        error,
        large=(2,),
        sent=(0, 1, 2),
        aliases={2: 0},
    )
    return smoothed, cross, error.reshape(channels), moment


def solution(mesh):
    tm, chan = ("y", "z"), ("x", "core")
    split = Mesh(mesh.devices.reshape(N_Y, N_Z, N_X, N_CORE), tm + chan)
    placed = (P(tm, chan), P(chan, None), P(chan), P(), P(), P(), P())
    return jax.shard_map(
        local,
        mesh=split,
        in_specs=placed,
        out_specs=(P(tm, None), P(chan, None), P(chan), P()),
        check_vma=False,
    )
```

```python
import functools
import math

import jax
import jax.numpy as jnp
import numpy as np
from jax import lax
from jax.experimental import pallas as pl
from jax.experimental.pallas import tpu as pltpu
from jax.sharding import Mesh, PartitionSpec as P

N_Y, N_Z, N_X, N_CORE = 4, 8, 4, 2
BLOCKS = N_Y * N_Z
SUB = 8
F32, BF16 = jnp.float32, jnp.bfloat16
KERNELS = True


class Late:
    def __init__(self, buffer, copies):
        self.buffer, self.copies, self.shape = buffer, copies, buffer.shape

    def __getitem__(self, key):
        while self.copies:
            self.copies.pop().wait()
        return self.buffer[key]


def pieces_of(shape):
    count = 4 if shape[0] >= 256 else 1
    return [(i * (shape[0] // count), shape[0] // count) for i in range(count)]


def call(body, outs, *args, large=(), sent=(), aliases={}, limit=16):
    if not KERNELS:
        results = [jnp.zeros(shape, dtype) for shape, dtype in outs]
        for i in aliases:
            results[aliases[i]] = args[i]
        for i, place, value in body(*args):
            if place is None:
                results[i] = value
            elif isinstance(place, int):
                results[i] = results[i].at[place].set(value)
            else:
                results[i] = lax.dynamic_update_slice_in_dim(results[i], value, place[0], 0)
        return results

    n_in, n_out = len(args), len(outs)
    loaded = [i for i in large if i not in aliases]

    def kernel(*refs):
        values, out_refs, rest = list(refs[:n_in]), refs[n_in : n_in + n_out], refs[n_in + n_out :]
        targets = dict(zip(sent, rest[len(loaded) : -2]))
        in_sems, out_sems = rest[-2:]
        number = 0
        for i, buffer in zip(loaded, rest[: len(loaded)]):
            copies = []
            for start, size in pieces_of(buffer.shape):
                rows = pl.ds(start, size)
                copies.append(
                    pltpu.make_async_copy(refs[i].at[rows], buffer.at[rows], in_sems.at[number])
                )
                copies[-1].start()
                number += 1
            values[i] = Late(buffer, copies)
        leaving = []
        for i, place, value in body(*values):
            index = Ellipsis if place is None else place
            if isinstance(place, tuple):
                index = pl.ds(place[0], place[1])
            if i not in sent:
                out_refs[i][index] = value
                continue
            buffer = targets[i]
            buffer[index] = value
            first = 0 if place is None else place[0]
            for start, size in pieces_of(value.shape):
                rows = pl.ds(first + start, size)
                leaving.append(
                    pltpu.make_async_copy(
                        buffer.at[rows], out_refs[i].at[rows], out_sems.at[len(leaving)]
                    )
                )
                leaving[-1].start()
        for copy in leaving:
            copy.wait()

    args = [
        pltpu.with_memory_space_constraint(arg, pltpu.HBM if i in large else pltpu.VMEM)
        for i, arg in enumerate(args)
    ]
    vmem, far = pl.BlockSpec(memory_space=pltpu.VMEM), pl.BlockSpec(memory_space=pltpu.HBM)
    return pl.pallas_call(
        kernel,
        out_shape=[(pltpu.HBM if i in sent else pltpu.VMEM)(*kind) for i, kind in enumerate(outs)],
        in_specs=[far if i in large else vmem for i in range(n_in)],
        out_specs=[far if i in sent else vmem for i in range(n_out)],
        scratch_shapes=[pltpu.VMEM(args[i].shape, args[i].dtype) for i in loaded]
        + [pltpu.VMEM(*outs[i]) for i in sent]
        + [pltpu.SemaphoreType.DMA((32,)), pltpu.SemaphoreType.DMA((32,))],
        input_output_aliases=dict(aliases),
        compiler_params=pltpu.CompilerParams(vmem_limit_bytes=limit * 2**20),
        name=body.__name__,
    )(*args)


def roll(rows, by):
    if KERNELS:
        return pltpu.roll(rows, by % rows.shape[0], 0)
    return jnp.roll(rows, by, 0)


def roll_lanes(rows, by):
    if KERNELS:
        return pltpu.roll(rows, by, 1)
    return jnp.roll(rows, by, 1)


def row_index(rows):
    return lax.broadcasted_iota(jnp.int32, rows.shape, 0)


def dot(left, right, dims=((1,), (0,))):
    return lax.dot_general(left, right, (dims, ((), ())), preferred_element_type=F32)


def cut(value):
    count = value.shape[0]
    if count < 16:
        value = jnp.concatenate([value, value], axis=0)
    high = value.astype(BF16)
    return high, (value - high.astype(F32)).astype(BF16), count


def cut_full(value):
    high = value.astype(BF16)
    rest = value - high.astype(F32)
    middle = rest.astype(BF16)
    return high, middle, (rest - middle.astype(F32)).astype(BF16)


def dot_pairs(pairs):
    left = jnp.concatenate([pair[0] for pair in pairs], axis=1)
    right = jnp.concatenate([pair[1] for pair in pairs], axis=0)
    return dot(left, right)


def dot_full(left, right):
    a, b = left, right
    return dot_pairs(
        [(a[0], b[0]), (a[0], b[1]), (a[1], b[0]), (a[1], b[1]), (a[0], b[2]), (a[2], b[0])]
    )


def mul(rows, matrix):
    count = rows[0].shape[0]
    if count > 128:
        return dot_pairs([(rows[0], matrix[0]), (rows[1], matrix[0]), (rows[0], matrix[1])])
    found = dot(jnp.concatenate(rows[:2], axis=0), matrix[0])
    found = found[:count] + (found[count:] + dot(rows[0], matrix[1]))
    return found[: rows[2]]


def at(stacks, level):
    for high, low in stacks:
        if level < high.shape[0]:
            return high[level], low[level]
        level -= high.shape[0]


def put(first, place, value):
    yield first, place, value[0]
    yield first + 1, place, value[1]


def squares(a, b, level):
    if level < 3:
        a, b = cut_full(a), cut_full(b)
        return dot_full(a, a), dot_full(b, b)
    a, b = cut(a), cut(b)
    return mul(a, a), mul(b, b)


FIRST = 6


def powers(transition, info_gain, smoother_gain, smoother_input):
    a, g = transition[...].T, cut(smoother_input[...].T)
    b, k = smoother_gain[...].T, cut(info_gain[...].T)
    a_cut, b_cut = cut(a), cut(b)
    ag = cut(mul(a_cut, g))
    kg = cut(mul(k, g))
    m_cut = None
    for level in range(13):
        a_cut, b_cut = cut(a), cut(b)
        place = level if level < 8 else level - 8
        yield from put(2 if level < 8 else 10, place, a_cut)
        yield from put(4 if level < 8 else 12, place, b_cut)
        if level < 12:
            a, b = squares(a, b, level)
        if level == 0:
            m = mul(ag, b_cut)
            for i, value in enumerate([k, kg, cut(mul(kg, b_cut)), ag, g]):
                yield from put(0, i, value)
        if level <= FIRST:
            m_cut = cut(m)
            yield from put(6, level, m_cut)
        if level < FIRST:
            n_cut = cut(mul(a_cut, m_cut))
            m = m + mul(n_cut, b_cut)
            yield from put(8, level, n_cut)
    yield 14, None, m


def last_effects(a_h, a_l, b_h, b_l, m):
    m = m[...]
    for level in range(FIRST, 8):
        m_cut = cut(m)
        if level > FIRST:
            yield from put(0, level - FIRST - 1, m_cut)
        a_cut = (a_h[level], a_l[level], m.shape[0])
        n_cut = cut(mul(a_cut, m_cut))
        yield from put(2, level - FIRST, n_cut)
        m = m + mul(n_cut, (b_h[level], b_l[level]))
    yield from put(4, None, cut(m))


def information_part(order, noise_precision, emission, observations):
    scale = jnp.broadcast_to(noise_precision[...], (128, noise_precision.shape[1])).T
    scale = jnp.concatenate([scale] * (emission.shape[1] // 128), axis=1)
    weighted = (emission[...].astype(F32) * scale).astype(BF16)
    rows = dot(order[...], observations[...]).astype(BF16)
    information = dot(rows, weighted)
    half = rows.shape[0] // 2
    first = lax.axis_index("core") == 0
    yield 1, None, jnp.where(first, information[half:], information[:half])
    yield 0, None, jnp.where(first, information[:half], information[half:])
    yield 2, None, rows


def chosen(number, values):
    out = values[0]
    for i in range(1, len(values)):
        out = jnp.where(number == i, values[i], out)
    return out


def up_sweep(lead, a_cut, b_cut, m_cut, information):
    information = cut(information)
    end, shown, start = (mul(information, at(lead, i)) for i in range(3))
    ends, follows = [], []
    for level in range(5):
        half = end.shape[0] // 2
        first, second = end[:half], end[half:]
        first_cut = cut(first)
        follow = start[half:] + mul(first_cut, at(m_cut, level))
        ends.append(first)
        follows.append(follow)
        start = start[:half] + mul(cut(follow), at(b_cut, level))
        end = second + mul(first_cut, at(a_cut, level))
    return shown, end, start, ends, follows


def sub_sweep(a_cut, b_cut, m_cut, end, start):
    ends, follows = [], []
    for level in range(5, 8):
        by = 2 ** (level - 5)
        end_cut = cut(end)
        follow = roll(start, -by) + mul(end_cut, at(m_cut, level))
        ends.append(end)
        follows.append(follow)
        start = start + mul(cut(follow), at(b_cut, level))
        end = mul(end_cut, at(a_cut, level)) + roll(end, -by)
    return end, start, ends, follows


def both_halves(total, theirs):
    first = lax.axis_index("core") == 0
    total, theirs = total[...], theirs[...]
    return jnp.concatenate(
        [jnp.where(first, total, theirs), jnp.where(first, theirs, total)], axis=0
    )


def block_tree(
    total, theirs, lead_h, lead_l, m_h, m_l, m_last_h, m_last_l, b_h, b_l, a_h, a_l
):
    information = both_halves(total, theirs)
    a_cut, b_cut = [(a_h, a_l)], [(b_h, b_l)]
    m_cut = [(m_h, m_l), (m_last_h, m_last_l)]
    shown, end, start, ends, follows = up_sweep(
        [(lead_h, lead_l)], a_cut, b_cut, m_cut, information
    )
    end, start, sub_ends, sub_follows = sub_sweep(a_cut, b_cut, m_cut, end, start)
    pair = jnp.concatenate([end[None, :1], start[None, :1]], axis=1)
    yield 0, None, jnp.broadcast_to(pair, (BLOCKS, 2, end.shape[1]))
    yield 1, None, shown
    place = 0
    for i in range(5):
        yield 2, (place, ends[i].shape[0]), ends[i]
        yield 3, (place, ends[i].shape[0]), follows[i]
        place += ends[i].shape[0]
    for i in range(3):
        yield 4, (i * SUB, SUB), spread_first(sub_ends[i], 2**i)
        yield 5, (i * SUB, SUB), spread_first(sub_follows[i], 2**i)


def spread_first(rows, by):
    rows = jnp.where(row_index(rows) % (2 * by) == 0, rows, 0.0)
    step = 1
    while step < 2 * by:
        rows = rows + roll(rows, step)
        step *= 2
    return rows


def states_and_sums(
    gathered,
    a_big_h,
    a_big_l,
    lead_h,
    lead_l,
    m_h,
    m_l,
    b_big_h,
    b_big_l,
    sub_ends,
    sub_follows,
    a_h,
    a_l,
    n_h,
    n_l,
    n_last_h,
    n_last_l,
    b_h,
    b_l,
    ends,
    follows,
    shown,
    emission,
    observed,
):
    block = lax.axis_index("y") * N_Z + lax.axis_index("z")
    width = shown.shape[1]
    gathered = gathered[...]
    after = gathered[:, 0]
    index = row_index(after)
    for level in range(5):
        by = 2**level
        before = jnp.where(index >= by, roll(after, by), 0.0)
        after = after + mul(cut(before), at([(a_big_h, a_big_l)], level))
    enter = jnp.where(index >= 1, roll(after, 1), 0.0)
    follow = gathered[:, 1] + mul(cut(enter), (m_h[...], m_l[...]))
    final = after - mul(cut(after), at([(lead_h, lead_l)], 4))
    follow = jnp.where(index < BLOCKS - 1, roll(follow, -1), final)
    for level in range(5):
        by = 2**level
        later = jnp.where(index < BLOCKS - by, roll(follow, -by), 0.0)
        follow = follow + mul(cut(later), at([(b_big_h, b_big_l)], level))

    source = lax.broadcasted_iota(jnp.int32, (16, BLOCKS), 1)
    pick = (source == block).astype(BF16)

    def picked(rows):
        high, low, _ = cut(rows)
        return (dot(pick, high) + dot(pick, low))[:SUB]

    def children(enter, follow, level):
        enter = cut(enter)
        first = mul(enter, at([(n_h, n_l), (n_last_h, n_last_l)], level)) + mul(cut(follow), at([(b_h, b_l)], level))
        return mul(enter, at([(a_h, a_l)], level)), first

    enter, follow = picked(enter), picked(follow)
    count = SUB
    index = row_index(enter)
    for level in (7, 6, 5):
        by = 2 ** (level - 5)
        part = (level - 5) * count
        second, first = children(enter, follow, level)
        second = sub_ends[part : part + count] + second
        first = sub_follows[part : part + count] + first
        is_second = (index // by) % 2 == 1
        enter = jnp.where(is_second, second, enter)
        follow = jnp.where(is_second, follow, first)

    bottom = ends.shape[0]
    for level in (4, 3, 2, 1, 0):
        rows = enter.shape[0]
        top, bottom = bottom, bottom - rows
        second, first = children(enter, follow, level)
        second = ends[bottom:top] + second
        first = follows[bottom:top] + first
        enter = jnp.concatenate([enter, second], axis=0)
        follow = jnp.concatenate([first, follow], axis=0)
    smoothed = shown[...] + mul(cut(enter), at([(lead_h, lead_l)], 3)) + follow
    observed, emission = observed[...], emission[...]

    high, low, _ = cut(smoothed)
    cross = dot(observed, high, ((0,), (0,)))
    predicted = dot(high, emission, ((1,), (1,)))
    error = observed.astype(F32) - predicted
    error = jnp.broadcast_to(jnp.sum(error * error, axis=0, keepdims=True), (8, error.shape[1]))
    crossed = dot(high, jnp.concatenate([high, low], axis=1), ((0,), (0,)))
    moment = crossed[:, :width] + (crossed[:, width:] + crossed[:, width:].T)

    channels = cross.shape[0] // N_Y
    share, line = width // N_Y, channels // N_Z
    lane = lax.broadcasted_iota(jnp.int32, (8, width), 1)
    row = lax.broadcasted_iota(jnp.int32, (8, width), 0)
    parts = []
    for y in range(N_Y):
        free = share * ((y + 1) % N_Y)
        is_free = (lane >= free) & (lane < free + share)
        is_error = (lane >= free) & (lane < free + line) & (row == 0)
        tiles = []
        for z in range(N_Z):
            turned = roll_lanes(
                error[:, y * channels : (y + 1) * channels], (free - line * z) % width
            )
            top = y * share + 8 * z
            tile = jnp.where(is_free, 0.0, moment[top : top + 8])
            tiles.append(jnp.where(is_error, turned, tile))
        mine = cross[y * channels : (y + 1) * channels].reshape(N_Z, line, width)
        parts.append(jnp.concatenate([mine, jnp.stack(tiles)], axis=1))
    y = block // N_Z
    for by in (2, 1, 3, 0):
        yield 1 + by, None, chosen(y, [parts[(i + by) % N_Y] for i in range(N_Y)])

    yield 0, None, smoothed


def in_time_order(natural, smoothed):
    rest, out = smoothed[...], None
    for _ in range(3):
        high = rest.astype(BF16)
        rest = rest - high.astype(F32)
        moved = dot(natural[...], high)
        out = moved if out is None else out + moved
    yield 0, None, out


def add_chunks(c0, c1, c2, c3):
    yield 0, None, (c0[...] + c1[...]) + (c2[...] + c3[...])


def add_pieces(pieces):
    total = pieces[0]
    for i in range(1, N_Z):
        total = total + pieces[i]
    yield 0, None, jnp.broadcast_to(total[None], (N_Z,) + total.shape)


def blocks_of(bins, by_pieces):
    y = lax.axis_index("y")
    for by, piece in by_pieces:
        place = y - by
        place = jnp.where(place < 0, place + N_Y, place)
        width = piece.shape[2]
        share, line = width // N_Y, piece.shape[1] - 8
        cross = piece[:, :line].reshape(-1, width) * (1.0 / math.sqrt(bins))
        moment = piece[:, line:].reshape(-1, width)
        lane = lax.broadcasted_iota(jnp.int32, (8, width), 1)
        free = share * jnp.where(place == N_Y - 1, 0, place + 1)
        error = jnp.zeros((8, width), F32)
        for z in range(N_Z):
            by = line * z - free
            by = jnp.where(by < 0, by + width, by)
            turned = roll_lanes(moment[8 * z : 8 * z + 8], by)
            error = jnp.where((lane >= line * z) & (lane < line * z + line), turned, error)
        yield 0, (tiled(place * cross.shape[0]), cross.shape[0]), cross
        yield 1, (tiled(place * share), share), moment
        yield 2, (tiled(place * 8), 8), error


def tiled(start):
    return pl.multiple_of(start, 8) if KERNELS else start


def first_blocks(bins, own, near):
    yield from blocks_of(bins, [(0, own[...]), (1, near[...])])


def last_blocks(bins, far, back, cross, moments, errors):
    moment, error = moments[...], errors[...]
    for i, (start, size), value in blocks_of(bins, [(3, back[...]), (2, far[...])]):
        if i == 0:
            yield 0, (start, size), value
            continue
        rows = moment if i == 1 else error
        mine = (row_index(rows) >= start) & (row_index(rows) < start + size)
        rows = jnp.where(mine, jnp.concatenate([value] * N_Y, axis=0), rows)
        if i == 1:
            moment = rows
        else:
            error = rows
    share = moment.shape[0] // N_Y
    row = lax.broadcasted_iota(jnp.int32, moment.shape, 0) // share
    column = lax.broadcasted_iota(jnp.int32, moment.shape, 1) // share
    free = column == jnp.where(row == N_Y - 1, 0, row + 1)
    yield 1, None, jnp.where(free, moment.T, moment) * (1.0 / bins)
    error = jnp.concatenate([error[8 * i : 8 * i + 1] for i in range(N_Y)], axis=1)
    yield 2, None, error * (1.0 / bins)


def shift(value, axis, count, by):
    return lax.ppermute(value, axis, [(i, (i + by) % count) for i in range(count)])


def shift_flat(value, axis, count, by):
    return shift(value.reshape(-1, value.shape[-1]), axis, count, by).reshape(value.shape)


def bit_reversed(count):
    bits = count.bit_length() - 1
    return [int(format(i, "0%db" % bits)[::-1], 2) for i in range(count)]


def row_order(bins):
    length = bins // SUB
    times = np.array([[j * length + t for j in range(SUB)] for t in bit_reversed(length)])
    return np.eye(bins, dtype=np.float32)[times.reshape(-1)]


def local(
    observations, emission, noise_precision, transition, info_gain, smoother_gain, smoother_input
):
    bins, channels = observations.shape
    width = transition.shape[0]
    order = jnp.asarray(row_order(bins), BF16)
    natural = jnp.asarray(row_order(bins).T, BF16)

    mine, other, seen = call(
        information_part,
        [((bins // 2, width), F32)] * 2 + [((bins, channels), BF16)],
        order,
        noise_precision.reshape(1, channels),
        emission,
        observations,
        large=(0, 1, 2, 3),
    )
    mine = mine + shift(other, "core", N_CORE, 1)
    moved = [shift(mine, "x", N_X, by) for by in (2, 1, 3)]

    square = (width, width)
    stack = lambda n: [((n,) + square, BF16)] * 2
    known = call(
        powers,
        stack(5) + stack(8) * 2 + stack(FIRST + 1) + stack(FIRST) + stack(5) * 2 + [(square, F32)],
        transition,
        info_gain,
        smoother_gain,
        smoother_input,
    )
    moved, known = lax.optimization_barrier((moved, known))
    lead, a_cut, b_cut, m_cut, n_cut, a_big, b_big = (known[i : i + 2] for i in range(0, 14, 2))
    late = call(
        last_effects,
        stack(7 - FIRST) + stack(8 - FIRST) + [(square, BF16)] * 2,
        *a_cut,
        *b_cut,
        known[14],
    )

    total = mine + moved[0] + moved[1] + moved[2]
    theirs = shift(total, "core", N_CORE, 1)
    ends, *tree = call(
        block_tree,
        [
            ((BLOCKS, 2, width), F32),
            ((bins, width), F32),
            ((SUB * 31, width), F32),
            ((SUB * 31, width), F32),
            ((SUB * 3, width), F32),
            ((SUB * 3, width), F32),
        ],
        total,
        theirs,
        *lead,
        *m_cut,
        *late[:2],
        *b_cut,
        *a_cut,
    )
    ends, late = lax.optimization_barrier((ends, late))
    gathered = lax.all_to_all(ends, ("y", "z"), 0, 0)
    rows = channels // (N_Y * N_Z) + 8
    chunk = ((N_Z, rows, width), F32)
    shown, tree_ends, follows, sub_ends, sub_follows = tree
    smoothed, *chunks = call(
        states_and_sums,
        [((bins, width), F32)] + [chunk] * N_Y,
        gathered,
        *a_big,
        *lead,
        *late[4:],
        *b_big,
        sub_ends,
        sub_follows,
        *a_cut,
        *n_cut,
        *late[2:4],
        *b_cut,
        tree_ends,
        follows,
        shown,
        emission,
        seen,
    )
    back, near, far = (shift_flat(chunks[by], "y", N_Y, by) for by in (3, 1, 2))
    (smoothed,) = call(in_time_order, [((bins, width), F32)], natural, smoothed)
    (payload,) = call(add_chunks, [chunk], chunks[0], near, back, far)
    payload = lax.all_to_all(payload, "z", 0, 0)
    (spread,) = call(add_pieces, [chunk], payload)
    whole = lax.all_to_all(spread, "z", 0, 0)
    far, near, back = (shift_flat(whole, "y", N_Y, by) for by in (2, 1, 3))
    named = lambda body: functools.wraps(body)(functools.partial(body, bins * BLOCKS))
    kinds = [((channels, width), F32), (square, F32)]
    cross, moment, error = call(
        named(first_blocks), kinds + [((8 * N_Y, width), F32)], whole, near, sent=(0,)
    )
    cross, moment, error = call(
        named(last_blocks),
        kinds + [((1, channels), F32)],
        far,
        back,
        cross,
        moment,
        error,
        large=(2,),
        sent=(0, 1, 2),
        aliases={2: 0},
    )
    return smoothed, cross, error.reshape(channels), moment


def solution(mesh):
    tm, chan = ("y", "z"), ("x", "core")
    split = Mesh(mesh.devices.reshape(N_Y, N_Z, N_X, N_CORE), tm + chan)
    placed = (P(tm, chan), P(chan, None), P(chan), P(), P(), P(), P())
    return jax.shard_map(
        local,
        mesh=split,
        in_specs=placed,
        out_specs=(P(tm, None), P(chan, None), P(chan), P()),
        check_vma=False,
    )
```

```python
import functools
import math

import jax
import jax.numpy as jnp
import numpy as np
from jax import lax
from jax.experimental import pallas as pl
from jax.experimental.pallas import tpu as pltpu
from jax.sharding import Mesh, PartitionSpec as P

N_Y, N_Z, N_X, N_CORE = 4, 8, 4, 2
BLOCKS = N_Y * N_Z
SUB = 8
F32, BF16 = jnp.float32, jnp.bfloat16
KERNELS = True


class Late:
    def __init__(self, buffer, copies):
        self.buffer, self.copies, self.shape = buffer, copies, buffer.shape

    def __getitem__(self, key):
        while self.copies:
            self.copies.pop().wait()
        return self.buffer[key]


def pieces_of(shape):
    count = 4 if shape[0] >= 256 else 1
    return [(i * (shape[0] // count), shape[0] // count) for i in range(count)]


def call(body, outs, *args, large=(), sent=(), aliases={}, limit=16):
    if not KERNELS:
        results = [jnp.zeros(shape, dtype) for shape, dtype in outs]
        for i in aliases:
            results[aliases[i]] = args[i]
        for i, place, value in body(*args):
            if place is None:
                results[i] = value
            elif isinstance(place, int):
                results[i] = results[i].at[place].set(value)
            else:
                results[i] = lax.dynamic_update_slice_in_dim(results[i], value, place[0], 0)
        return results

    n_in, n_out = len(args), len(outs)
    loaded = [i for i in large if i not in aliases]

    def kernel(*refs):
        values, out_refs, rest = list(refs[:n_in]), refs[n_in : n_in + n_out], refs[n_in + n_out :]
        targets = dict(zip(sent, rest[len(loaded) : -2]))
        in_sems, out_sems = rest[-2:]
        number = 0
        for i, buffer in zip(loaded, rest[: len(loaded)]):
            copies = []
            for start, size in pieces_of(buffer.shape):
                rows = pl.ds(start, size)
                copies.append(
                    pltpu.make_async_copy(refs[i].at[rows], buffer.at[rows], in_sems.at[number])
                )
                copies[-1].start()
                number += 1
            values[i] = Late(buffer, copies)
        leaving = []
        for i, place, value in body(*values):
            index = Ellipsis if place is None else place
            if isinstance(place, tuple):
                index = pl.ds(place[0], place[1])
            if i not in sent:
                out_refs[i][index] = value
                continue
            buffer = targets[i]
            buffer[index] = value
            first = 0 if place is None else place[0]
            for start, size in pieces_of(value.shape):
                rows = pl.ds(first + start, size)
                leaving.append(
                    pltpu.make_async_copy(
                        buffer.at[rows], out_refs[i].at[rows], out_sems.at[len(leaving)]
                    )
                )
                leaving[-1].start()
        for copy in leaving:
            copy.wait()

    args = [
        pltpu.with_memory_space_constraint(arg, pltpu.HBM if i in large else pltpu.VMEM)
        for i, arg in enumerate(args)
    ]
    vmem, far = pl.BlockSpec(memory_space=pltpu.VMEM), pl.BlockSpec(memory_space=pltpu.HBM)
    return pl.pallas_call(
        kernel,
        out_shape=[(pltpu.HBM if i in sent else pltpu.VMEM)(*kind) for i, kind in enumerate(outs)],
        in_specs=[far if i in large else vmem for i in range(n_in)],
        out_specs=[far if i in sent else vmem for i in range(n_out)],
        scratch_shapes=[pltpu.VMEM(args[i].shape, args[i].dtype) for i in loaded]
        + [pltpu.VMEM(*outs[i]) for i in sent]
        + [pltpu.SemaphoreType.DMA((32,)), pltpu.SemaphoreType.DMA((32,))],
        input_output_aliases=dict(aliases),
        compiler_params=pltpu.CompilerParams(vmem_limit_bytes=limit * 2**20),
        name=body.__name__,
    )(*args)


def roll(rows, by):
    if KERNELS:
        return pltpu.roll(rows, by % rows.shape[0], 0)
    return jnp.roll(rows, by, 0)


def roll_lanes(rows, by):
    if KERNELS:
        return pltpu.roll(rows, by, 1)
    return jnp.roll(rows, by, 1)


def row_index(rows):
    return lax.broadcasted_iota(jnp.int32, rows.shape, 0)


def dot(left, right, dims=((1,), (0,))):
    return lax.dot_general(left, right, (dims, ((), ())), preferred_element_type=F32)


def cut(value):
    count = value.shape[0]
    if count < 16:
        value = jnp.concatenate([value, value], axis=0)
    high = value.astype(BF16)
    return high, (value - high.astype(F32)).astype(BF16), count


def cut_full(value):
    high = value.astype(BF16)
    rest = value - high.astype(F32)
    middle = rest.astype(BF16)
    return high, middle, (rest - middle.astype(F32)).astype(BF16)


def dot_pairs(pairs):
    left = jnp.concatenate([pair[0] for pair in pairs], axis=1)
    right = jnp.concatenate([pair[1] for pair in pairs], axis=0)
    return dot(left, right)


def dot_full(left, right):
    a, b = left, right
    return dot_pairs(
        [(a[0], b[0]), (a[0], b[1]), (a[1], b[0]), (a[1], b[1]), (a[0], b[2]), (a[2], b[0])]
    )


def mul(rows, matrix):
    count = rows[0].shape[0]
    if count > 128:
        return dot_pairs([(rows[0], matrix[0]), (rows[1], matrix[0]), (rows[0], matrix[1])])
    found = dot(jnp.concatenate(rows[:2], axis=0), matrix[0])
    found = found[:count] + (found[count:] + dot(rows[0], matrix[1]))
    return found[: rows[2]]


def at(stacks, level):
    for high, low in stacks:
        if level < high.shape[0]:
            return high[level], low[level]
        level -= high.shape[0]


def put(first, place, value):
    yield first, place, value[0]
    yield first + 1, place, value[1]


def squares(a, b, level):
    if level < 3:
        a, b = cut_full(a), cut_full(b)
        return dot_full(a, a), dot_full(b, b)
    a, b = cut(a), cut(b)
    return mul(a, a), mul(b, b)


FIRST = 6


def powers(transition, info_gain, smoother_gain, smoother_input):
    a, g = transition[...].T, cut(smoother_input[...].T)
    b, k = smoother_gain[...].T, cut(info_gain[...].T)
    a_cut, b_cut = cut(a), cut(b)
    ag = cut(mul(a_cut, g))
    kg = cut(mul(k, g))
    m_cut = None
    for level in range(13):
        a_cut, b_cut = cut(a), cut(b)
        place = level if level < 8 else level - 8
        yield from put(2 if level < 8 else 10, place, a_cut)
        yield from put(4 if level < 8 else 12, place, b_cut)
        if level < 12:
            a, b = squares(a, b, level)
        if level == 0:
            m = mul(ag, b_cut)
            for i, value in enumerate([k, kg, cut(mul(kg, b_cut)), ag, g]):
                yield from put(0, i, value)
        if level <= FIRST:
            m_cut = cut(m)
            yield from put(6, level, m_cut)
        if level < FIRST:
            n_cut = cut(mul(a_cut, m_cut))
            m = m + mul(n_cut, b_cut)
            yield from put(8, level, n_cut)
    yield 14, None, m


def last_effects(a_h, a_l, b_h, b_l, m):
    m = m[...]
    a_cut = (a_h[FIRST], a_l[FIRST], m.shape[0])
    n_cut = cut(mul(a_cut, cut(m)))
    yield from put(2, 0, n_cut)
    m = m + mul(n_cut, (b_h[FIRST], b_l[FIRST]))
    yield from put(0, 0, cut(m))
    yield 4, None, m


def information_part(order, noise_precision, emission, observations):
    scale = jnp.broadcast_to(noise_precision[...], (128, noise_precision.shape[1])).T
    scale = jnp.concatenate([scale] * (emission.shape[1] // 128), axis=1)
    weighted = (emission[...].astype(F32) * scale).astype(BF16)
    rows = dot(order[...], observations[...]).astype(BF16)
    information = dot(rows, weighted)
    half = rows.shape[0] // 2
    first = lax.axis_index("core") == 0
    yield 1, None, jnp.where(first, information[half:], information[:half])
    yield 0, None, jnp.where(first, information[:half], information[half:])
    yield 2, None, rows


def chosen(number, values):
    out = values[0]
    for i in range(1, len(values)):
        out = jnp.where(number == i, values[i], out)
    return out


def up_sweep(lead, a_cut, b_cut, m_cut, information):
    information = cut(information)
    end, shown, start = (mul(information, at(lead, i)) for i in range(3))
    ends, follows = [], []
    for level in range(5):
        half = end.shape[0] // 2
        first, second = end[:half], end[half:]
        first_cut = cut(first)
        follow = start[half:] + mul(first_cut, at(m_cut, level))
        ends.append(first)
        follows.append(follow)
        start = start[:half] + mul(cut(follow), at(b_cut, level))
        end = second + mul(first_cut, at(a_cut, level))
    return shown, end, start, ends, follows


def sub_sweep(a_cut, b_cut, m_cut, end, start):
    ends, follows = [], []
    for level in range(5, 8):
        by = 2 ** (level - 5)
        end_cut = cut(end)
        follow = roll(start, -by) + mul(end_cut, at(m_cut, level))
        ends.append(end)
        follows.append(follow)
        start = start + mul(cut(follow), at(b_cut, level))
        end = mul(end_cut, at(a_cut, level)) + roll(end, -by)
    return end, start, ends, follows


def both_halves(total, theirs):
    first = lax.axis_index("core") == 0
    total, theirs = total[...], theirs[...]
    return jnp.concatenate(
        [jnp.where(first, total, theirs), jnp.where(first, theirs, total)], axis=0
    )


def block_tree(
    total, theirs, lead_h, lead_l, m_h, m_l, m_last_h, m_last_l, b_h, b_l, a_h, a_l
):
    information = both_halves(total, theirs)
    a_cut, b_cut = [(a_h, a_l)], [(b_h, b_l)]
    m_cut = [(m_h, m_l), (m_last_h, m_last_l)]
    shown, end, start, ends, follows = up_sweep(
        [(lead_h, lead_l)], a_cut, b_cut, m_cut, information
    )
    end, start, sub_ends, sub_follows = sub_sweep(a_cut, b_cut, m_cut, end, start)
    pair = jnp.concatenate([end[None, :1], start[None, :1]], axis=1)
    yield 0, None, jnp.broadcast_to(pair, (BLOCKS, 2, end.shape[1]))
    yield 1, None, shown
    place = 0
    for i in range(5):
        yield 2, (place, ends[i].shape[0]), ends[i]
        yield 3, (place, ends[i].shape[0]), follows[i]
        place += ends[i].shape[0]
    for i in range(3):
        yield 4, (i * SUB, SUB), spread_first(sub_ends[i], 2**i)
        yield 5, (i * SUB, SUB), spread_first(sub_follows[i], 2**i)


def spread_first(rows, by):
    rows = jnp.where(row_index(rows) % (2 * by) == 0, rows, 0.0)
    step = 1
    while step < 2 * by:
        rows = rows + roll(rows, step)
        step *= 2
    return rows


def states_and_sums(
    gathered,
    a_big_h,
    a_big_l,
    lead_h,
    lead_l,
    m,
    b_big_h,
    b_big_l,
    sub_ends,
    sub_follows,
    a_h,
    a_l,
    n_h,
    n_l,
    n_last_h,
    n_last_l,
    b_h,
    b_l,
    ends,
    follows,
    shown,
    emission,
    observed,
):
    block = lax.axis_index("y") * N_Z + lax.axis_index("z")
    width = shown.shape[1]
    m = m[...]
    n_cut = cut(mul((a_h[7], a_l[7], m.shape[0]), cut(m)))
    m_whole = cut(m + mul(n_cut, (b_h[7], b_l[7])))
    gathered = gathered[...]
    after = gathered[:, 0]
    index = row_index(after)
    for level in range(5):
        by = 2**level
        before = jnp.where(index >= by, roll(after, by), 0.0)
        after = after + mul(cut(before), at([(a_big_h, a_big_l)], level))
    enter = jnp.where(index >= 1, roll(after, 1), 0.0)
    follow = gathered[:, 1] + mul(cut(enter), m_whole[:2])
    final = after - mul(cut(after), at([(lead_h, lead_l)], 4))
    follow = jnp.where(index < BLOCKS - 1, roll(follow, -1), final)
    for level in range(5):
        by = 2**level
        later = jnp.where(index < BLOCKS - by, roll(follow, -by), 0.0)
        follow = follow + mul(cut(later), at([(b_big_h, b_big_l)], level))

    source = lax.broadcasted_iota(jnp.int32, (16, BLOCKS), 1)
    pick = (source == block).astype(BF16)

    def picked(rows):
        high, low, _ = cut(rows)
        return (dot(pick, high) + dot(pick, low))[:SUB]

    def children(enter, follow, level):
        enter = cut(enter)
        n_level = n_cut[:2] if level == 7 else at([(n_h, n_l), (n_last_h, n_last_l)], level)
        first = mul(enter, n_level) + mul(cut(follow), at([(b_h, b_l)], level))
        return mul(enter, at([(a_h, a_l)], level)), first

    enter, follow = picked(enter), picked(follow)
    count = SUB
    index = row_index(enter)
    for level in (7, 6, 5):
        by = 2 ** (level - 5)
        part = (level - 5) * count
        second, first = children(enter, follow, level)
        second = sub_ends[part : part + count] + second
        first = sub_follows[part : part + count] + first
        is_second = (index // by) % 2 == 1
        enter = jnp.where(is_second, second, enter)
        follow = jnp.where(is_second, follow, first)

    bottom = ends.shape[0]
    for level in (4, 3, 2, 1, 0):
        rows = enter.shape[0]
        top, bottom = bottom, bottom - rows
        second, first = children(enter, follow, level)
        second = ends[bottom:top] + second
        first = follows[bottom:top] + first
        enter = jnp.concatenate([enter, second], axis=0)
        follow = jnp.concatenate([first, follow], axis=0)
    smoothed = shown[...] + mul(cut(enter), at([(lead_h, lead_l)], 3)) + follow
    observed, emission = observed[...], emission[...]

    high, low, _ = cut(smoothed)
    cross = dot(observed, high, ((0,), (0,)))
    predicted = dot(high, emission, ((1,), (1,)))
    error = observed.astype(F32) - predicted
    error = jnp.broadcast_to(jnp.sum(error * error, axis=0, keepdims=True), (8, error.shape[1]))
    crossed = dot(high, jnp.concatenate([high, low], axis=1), ((0,), (0,)))
    moment = crossed[:, :width] + (crossed[:, width:] + crossed[:, width:].T)

    channels = cross.shape[0] // N_Y
    share, line = width // N_Y, channels // N_Z
    lane = lax.broadcasted_iota(jnp.int32, (8, width), 1)
    row = lax.broadcasted_iota(jnp.int32, (8, width), 0)
    parts = []
    for y in range(N_Y):
        free = share * ((y + 1) % N_Y)
        is_free = (lane >= free) & (lane < free + share)
        is_error = (lane >= free) & (lane < free + line) & (row == 0)
        tiles = []
        for z in range(N_Z):
            turned = roll_lanes(
                error[:, y * channels : (y + 1) * channels], (free - line * z) % width
            )
            top = y * share + 8 * z
            tile = jnp.where(is_free, 0.0, moment[top : top + 8])
            tiles.append(jnp.where(is_error, turned, tile))
        mine = cross[y * channels : (y + 1) * channels].reshape(N_Z, line, width)
        parts.append(jnp.concatenate([mine, jnp.stack(tiles)], axis=1))
    y = block // N_Z
    for by in (2, 1, 3, 0):
        yield 1 + by, None, chosen(y, [parts[(i + by) % N_Y] for i in range(N_Y)])

    yield 0, None, smoothed


def in_time_order(natural, smoothed):
    rest, out = smoothed[...], None
    for _ in range(3):
        high = rest.astype(BF16)
        rest = rest - high.astype(F32)
        moved = dot(natural[...], high)
        out = moved if out is None else out + moved
    yield 0, None, out


def add_chunks(c0, c1, c2, c3):
    yield 0, None, (c0[...] + c1[...]) + (c2[...] + c3[...])


def add_pieces(pieces):
    total = pieces[0]
    for i in range(1, N_Z):
        total = total + pieces[i]
    yield 0, None, jnp.broadcast_to(total[None], (N_Z,) + total.shape)


def blocks_of(bins, by_pieces):
    y = lax.axis_index("y")
    for by, piece in by_pieces:
        place = y - by
        place = jnp.where(place < 0, place + N_Y, place)
        width = piece.shape[2]
        share, line = width // N_Y, piece.shape[1] - 8
        cross = piece[:, :line].reshape(-1, width) * (1.0 / math.sqrt(bins))
        moment = piece[:, line:].reshape(-1, width)
        lane = lax.broadcasted_iota(jnp.int32, (8, width), 1)
        free = share * jnp.where(place == N_Y - 1, 0, place + 1)
        error = jnp.zeros((8, width), F32)
        for z in range(N_Z):
            by = line * z - free
            by = jnp.where(by < 0, by + width, by)
            turned = roll_lanes(moment[8 * z : 8 * z + 8], by)
            error = jnp.where((lane >= line * z) & (lane < line * z + line), turned, error)
        yield 0, (tiled(place * cross.shape[0]), cross.shape[0]), cross
        yield 1, (tiled(place * share), share), moment
        yield 2, (tiled(place * 8), 8), error


def tiled(start):
    return pl.multiple_of(start, 8) if KERNELS else start


def first_blocks(bins, own, near):
    yield from blocks_of(bins, [(0, own[...]), (1, near[...])])


def last_blocks(bins, far, back, cross, moments, errors):
    moment, error = moments[...], errors[...]
    for i, (start, size), value in blocks_of(bins, [(3, back[...]), (2, far[...])]):
        if i == 0:
            yield 0, (start, size), value
            continue
        rows = moment if i == 1 else error
        mine = (row_index(rows) >= start) & (row_index(rows) < start + size)
        rows = jnp.where(mine, jnp.concatenate([value] * N_Y, axis=0), rows)
        if i == 1:
            moment = rows
        else:
            error = rows
    share = moment.shape[0] // N_Y
    row = lax.broadcasted_iota(jnp.int32, moment.shape, 0) // share
    column = lax.broadcasted_iota(jnp.int32, moment.shape, 1) // share
    free = column == jnp.where(row == N_Y - 1, 0, row + 1)
    yield 1, None, jnp.where(free, moment.T, moment) * (1.0 / bins)
    error = jnp.concatenate([error[8 * i : 8 * i + 1] for i in range(N_Y)], axis=1)
    yield 2, None, error * (1.0 / bins)


def shift(value, axis, count, by):
    return lax.ppermute(value, axis, [(i, (i + by) % count) for i in range(count)])


def shift_flat(value, axis, count, by):
    return shift(value.reshape(-1, value.shape[-1]), axis, count, by).reshape(value.shape)


def bit_reversed(count):
    bits = count.bit_length() - 1
    return [int(format(i, "0%db" % bits)[::-1], 2) for i in range(count)]


def row_order(bins):
    length = bins // SUB
    times = np.array([[j * length + t for j in range(SUB)] for t in bit_reversed(length)])
    return np.eye(bins, dtype=np.float32)[times.reshape(-1)]


def local(
    observations, emission, noise_precision, transition, info_gain, smoother_gain, smoother_input
):
    bins, channels = observations.shape
    width = transition.shape[0]
    order = jnp.asarray(row_order(bins), BF16)
    natural = jnp.asarray(row_order(bins).T, BF16)

    mine, other, seen = call(
        information_part,
        [((bins // 2, width), F32)] * 2 + [((bins, channels), BF16)],
        order,
        noise_precision.reshape(1, channels),
        emission,
        observations,
        large=(0, 1, 2, 3),
    )
    mine = mine + shift(other, "core", N_CORE, 1)
    moved = [shift(mine, "x", N_X, by) for by in (2, 1, 3)]

    square = (width, width)
    stack = lambda n: [((n,) + square, BF16)] * 2
    known = call(
        powers,
        stack(5) + stack(8) * 2 + stack(FIRST + 1) + stack(FIRST) + stack(5) * 2 + [(square, F32)],
        transition,
        info_gain,
        smoother_gain,
        smoother_input,
    )
    moved, known = lax.optimization_barrier((moved, known))
    lead, a_cut, b_cut, m_cut, n_cut, a_big, b_big = (known[i : i + 2] for i in range(0, 14, 2))
    late = call(
        last_effects,
        stack(1) * 2 + [(square, F32)],
        *a_cut,
        *b_cut,
        known[14],
    )

    total = mine + moved[0] + moved[1] + moved[2]
    theirs = shift(total, "core", N_CORE, 1)
    ends, *tree = call(
        block_tree,
        [
            ((BLOCKS, 2, width), F32),
            ((bins, width), F32),
            ((SUB * 31, width), F32),
            ((SUB * 31, width), F32),
            ((SUB * 3, width), F32),
            ((SUB * 3, width), F32),
        ],
        total,
        theirs,
        *lead,
        *m_cut,
        *late[:2],
        *b_cut,
        *a_cut,
    )
    ends, late = lax.optimization_barrier((ends, late))
    gathered = lax.all_to_all(ends, ("y", "z"), 0, 0)
    rows = channels // (N_Y * N_Z) + 8
    chunk = ((N_Z, rows, width), F32)
    shown, tree_ends, follows, sub_ends, sub_follows = tree
    smoothed, *chunks = call(
        states_and_sums,
        [((bins, width), F32)] + [chunk] * N_Y,
        gathered,
        *a_big,
        *lead,
        *late[4:],
        *b_big,
        sub_ends,
        sub_follows,
        *a_cut,
        *n_cut,
        *late[2:4],
        *b_cut,
        tree_ends,
        follows,
        shown,
        emission,
        seen,
    )
    back, near, far = (shift_flat(chunks[by], "y", N_Y, by) for by in (3, 1, 2))
    (smoothed,) = call(in_time_order, [((bins, width), F32)], natural, smoothed)
    (payload,) = call(add_chunks, [chunk], chunks[0], near, back, far)
    payload = lax.all_to_all(payload, "z", 0, 0)
    (spread,) = call(add_pieces, [chunk], payload)
    whole = lax.all_to_all(spread, "z", 0, 0)
    far, near, back = (shift_flat(whole, "y", N_Y, by) for by in (2, 1, 3))
    named = lambda body: functools.wraps(body)(functools.partial(body, bins * BLOCKS))
    kinds = [((channels, width), F32), (square, F32)]
    cross, moment, error = call(
        named(first_blocks), kinds + [((8 * N_Y, width), F32)], whole, near, sent=(0,)
    )
    cross, moment, error = call(
        named(last_blocks),
        kinds + [((1, channels), F32)],
        far,
        back,
        cross,
        moment,
        error,
        large=(2,),
        sent=(0, 1, 2),
        aliases={2: 0},
    )
    return smoothed, cross, error.reshape(channels), moment


def solution(mesh):
    tm, chan = ("y", "z"), ("x", "core")
    split = Mesh(mesh.devices.reshape(N_Y, N_Z, N_X, N_CORE), tm + chan)
    placed = (P(tm, chan), P(chan, None), P(chan), P(), P(), P(), P())
    return jax.shard_map(
        local,
        mesh=split,
        in_specs=placed,
        out_specs=(P(tm, None), P(chan, None), P(chan), P()),
        check_vma=False,
    )
```
